32 devices in a mesh: groups: 2 (over x), owner: 16 (over z, y, core).
Axes of the slice: x: 2, y: 2, z: 4, core: 2. Of those that a mesh axis runs over, the one named last changes fastest.
Arguments:
- embeddings: bfloat16 [65536, 768], P(('groups', 'owner')), parts along dimension 0, as said below
- cluster_ids: int32 [65536], P(('groups', 'owner')), parts along dimension 0, may hold values from 0 to 63, as said below
Outputs:
- neighbour_max: float32 [65536], P(('groups', 'owner')), parts along dimension 0
- centroid_gap: float32 [65536], P(('groups', 'owner')), parts along dimension 0
The draws below stay inside these ranges and needn't reach their ends.
There are 2 independent parts, one for each index of `groups`. The reference program is written for one: setup_inputs(seed, part) draws one part's arguments, and reference() takes and returns one part's arrays. A program takes and returns all parts, laid end to end along the dimension named above; each array names one. Nothing has to cross between parts.
Inputs may be any that keep to these rules, and one draw needn't show every extreme that they name: `cluster_ids`: A fine cluster holds at most 64 of the 2048 rows of one device and at most 1024 rows in all; both bounds are reached in every draw. A fine cluster may hold no rows. `embeddings`: every row has a nonzero length.
All inputs are finite; a program needn't handle non-finite values.
Results may differ from the reference program's by a relative error of at most 0.00079.
Values may be sent and summed in bfloat16 or wider, within the bound.
No kernel may reach another device: no remote copies, remote signals or barrier semaphores. Data moves between devices by JAX's collectives and lax.ppermute only.
A program may use at most 64 MiB of HBM per device.

```python
import jax
import jax.numpy as jnp
from jax import lax

D = 768
ROWS_DEV = 2048
CL_DEV = 4
CLUSTERS = 64
ROWS = 32768
KMAX = 64
CAP = 1024
N_OWNER = 16


def cluster_table(key):
    cluster_total = CLUSTERS
    pick_key, perm_key, spread_key, shuffle_key = jax.random.split(key, 4)
    top_block = jax.random.randint(pick_key, (), 0, cluster_total // CL_DEV)
    labels = jnp.arange(cluster_total, dtype=jnp.int32)
    shuffled = jax.random.permutation(perm_key, cluster_total).astype(jnp.int32)
    shuffled_at = jnp.zeros((cluster_total,), jnp.int32).at[shuffled].set(labels)
    priority = jnp.where(labels // CL_DEV == top_block, labels % CL_DEV, jnp.where(labels == cluster_total - 1, CL_DEV, CL_DEV + 1 + shuffled_at))
    by_rank = jnp.argsort(priority, stable=True).astype(jnp.int32)
    rank_of = jnp.zeros((cluster_total,), jnp.int32).at[by_rank].set(labels)
    pair_count = cluster_total // 2
    pair_index = jnp.arange(pair_count, dtype=jnp.int32)
    light_share = jnp.where(pair_index < CL_DEV, 0, pair_index % (KMAX // 2 + 1))
    values = jnp.sort(jnp.concatenate([KMAX - light_share, light_share]))[::-1]
    rank_index = jnp.arange(cluster_total, dtype=jnp.int32)
    window = max(cluster_total // 8, 1)
    jitter = jax.random.randint(spread_key, (N_OWNER, cluster_total), 0, 4 * window)
    sort_keys = jnp.where(rank_index < CL_DEV, rank_index - 8 * cluster_total, jnp.where(rank_index >= cluster_total - CL_DEV, rank_index + 8 * cluster_total, 4 * rank_index + jitter))
    rank_order = jnp.argsort(sort_keys * cluster_total + rank_index, axis=1, stable=True)
    anchor_index = jnp.arange(N_OWNER, dtype=jnp.int32)[:, None]
    amount_by_rank = jnp.zeros((N_OWNER, cluster_total), jnp.int32).at[anchor_index, rank_order].set(values[None, :])
    amounts = amount_by_rank[:, rank_of]
    bounds_end = jnp.cumsum(amounts, axis=1)
    positions = jnp.arange(ROWS_DEV, dtype=jnp.int32)
    grouped_ids = jnp.sum((bounds_end[:, None, :] <= positions[None, :, None]).astype(jnp.int32), axis=2)
    anchor_keys = jax.random.split(shuffle_key, N_OWNER)

    def shuffle_rows(row_key):
        return jax.random.permutation(row_key, ROWS_DEV)
    shuffles = jax.vmap(shuffle_rows)(anchor_keys)
    return jnp.take_along_axis(grouped_ids, shuffles, axis=1).reshape(-1).astype(jnp.int32)


def draw_cluster_ids(key, part):
    return cluster_table(key)


def draw_embeddings(key, part):
    labels = cluster_table(key)
    key = jax.random.fold_in(key, 7)
    center_key, noise_key, row_key, col_key = jax.random.split(key, 4)
    centers = jnp.clip(jax.random.normal(center_key, (CLUSTERS, D), jnp.float32), -6.0, 6.0)
    col_scale = jnp.exp(jax.random.uniform(col_key, (1, D), jnp.float32, jnp.log(0.5), jnp.log(5.0)))
    noise = jnp.clip(jax.random.normal(noise_key, (ROWS, D), jnp.float32), -6.0, 6.0)
    row_scale = jnp.exp(jax.random.uniform(row_key, (ROWS, 1), jnp.float32, 0.0, jnp.log(10.0)))
    weight = 0.6
    return ((weight * centers[labels] + noise) * col_scale * row_scale).astype(jnp.bfloat16)


def setup_inputs(seed: int = 0, part: int = 0) -> dict:
    arg_keys = jax.random.split(jax.random.key(seed), 3)
    part_splits = jax.random.split(jax.random.fold_in(arg_keys[2], part), 3)
    return {
        "embeddings": draw_embeddings(jax.random.fold_in(jax.random.fold_in(arg_keys[2], part), 71), part),
        "cluster_ids": draw_cluster_ids(jax.random.fold_in(jax.random.fold_in(arg_keys[2], part), 71), part),
    }


epsilon = 1e-06

def reference(embeddings, cluster_ids):
    widened = embeddings.astype(jnp.float32)
    unit_rows = (widened * lax.rsqrt(lax.optimization_barrier(jnp.sum(widened * widened, axis=1, keepdims=True)) + epsilon)).astype(jnp.bfloat16)
    counts = jnp.zeros((CLUSTERS,), jnp.int32).at[cluster_ids].add(1)
    cluster_sums = jax.ops.segment_sum(unit_rows.astype(jnp.float32), cluster_ids, num_segments=CLUSTERS)
    centroids = (cluster_sums / jnp.maximum(counts, 1).astype(jnp.float32)[:, None]).astype(jnp.bfloat16)
    picked = centroids[cluster_ids].astype(jnp.float32)
    centroid_gap = 1.0 - lax.optimization_barrier(jnp.sum(unit_rows.astype(jnp.float32) * picked, axis=1))
    sorted_rows = jnp.argsort(cluster_ids, stable=True).astype(jnp.int32)
    starts = (jnp.cumsum(counts) - counts).astype(jnp.int32)
    padded_order = jnp.concatenate([sorted_rows, jnp.full((CAP,), ROWS, jnp.int32)])
    padded_unit = jnp.concatenate([unit_rows, jnp.zeros((1, D), jnp.bfloat16)])
    positions = jnp.arange(CAP, dtype=jnp.int32)

    def cluster_best(bounds):
        first_row, live_count = bounds
        row_index = lax.dynamic_slice_in_dim(padded_order, first_row, CAP)
        cluster_rows = padded_unit[row_index]
        scores = jnp.dot(cluster_rows, cluster_rows.T, preferred_element_type=jnp.float32)
        allowed = (positions[None, :] < live_count) & (positions[None, :] != positions[:, None])
        best_match = lax.optimization_barrier(jnp.max(jnp.where(allowed, scores, -1.0), axis=1))
        return (jnp.where(positions < live_count, row_index, ROWS).astype(jnp.int32), best_match)
    where_to, matches = lax.map(cluster_best, (starts, counts))
    neighbour = jnp.full((ROWS + 1,), -1.0, jnp.float32).at[where_to.reshape(-1)].set(matches.reshape(-1))
    return (neighbour[:ROWS], centroid_gap)
```

```python
import functools

import jax
import jax.numpy as jnp
from jax import lax
from jax.experimental import pallas as pl
from jax.experimental.pallas import tpu as pltpu
from jax.sharding import PartitionSpec as P

CL_DEV = 4
VARIANTS = 8
STEP = 16
TILE = 256
MIB = 1 << 20

epsilon = 1e-06
f32 = jnp.float32
bf16 = jnp.bfloat16
i32 = jnp.int32


def iota(shape, axis):
    return lax.broadcasted_iota(i32, shape, axis)


def round_up(value, unit):
    return -(-value // unit) * unit


def nt_dot(a, b):
    return lax.dot_general(a, b, (((1,), (1,)), ((), ())), preferred_element_type=f32)


def mm(a, b):
    return jnp.dot(a, b, preferred_element_type=f32)


def sort_kernel(clusters, ids_ref, rows_ref, sorted_ref, rank_ref, unit_ref, pos_ref):
    rows = rows_ref.shape[0]
    blocks = rows // TILE
    label = iota((clusters, TILE), 0)
    upto = (iota((TILE, TILE), 0) <= iota((TILE, TILE), 1)).astype(bf16)
    total = jnp.zeros((clusters, 1), f32)
    for b in range(blocks):
        at = slice(b * TILE, (b + 1) * TILE)
        hot = ids_ref[:, at] == label
        hot16 = hot.astype(f32).astype(bf16)
        prefix = mm(hot16, upto)
        rank_ref[:, at] = jnp.sum(jnp.where(hot, prefix + total - 1.0, 0.0), axis=0, keepdims=True)
        total = total + prefix[:, TILE - 1 :]
    square = (clusters, clusters)
    total_row = jnp.sum(
        jnp.where(iota(square, 0) == iota(square, 1), total, 0.0), axis=0, keepdims=True
    )
    start = jnp.sum(
        jnp.where(iota(square, 1) < iota(square, 0), total_row, 0.0), axis=1, keepdims=True
    )
    for b in range(blocks):
        at = slice(b * TILE, (b + 1) * TILE)
        hot = ids_ref[:, at] == label
        first = jnp.sum(jnp.where(hot, start, 0.0), axis=0, keepdims=True)
        pos_ref[:, at] = (first + rank_ref[:, at]).astype(i32)

    def normalise(b, carry):
        at = pl.ds(pl.multiple_of(b * TILE, TILE), TILE)
        x = rows_ref[at, :].astype(f32)
        scale = lax.rsqrt(jnp.sum(x * x, axis=1, keepdims=True) + epsilon)
        unit_ref[at, :] = (x * scale).astype(bf16)
        return carry

    lax.fori_loop(0, blocks, normalise, 0)

    def arrange(b, carry):
        first = pl.multiple_of(b * TILE, TILE)
        take = (iota((TILE, rows), 0) + first) == pos_ref[...]
        sorted_ref[pl.ds(first, TILE), :] = mm(
            take.astype(f32).astype(bf16), unit_ref[...]
        ).astype(bf16)
        return carry

    lax.fori_loop(0, blocks, arrange, 0)
    tail = sorted_ref.shape[0] - rows
    sorted_ref[rows:, :] = jnp.zeros((tail, sorted_ref.shape[1]), bf16)


def sort_rows(embeddings, ids_row, clusters, tail):
    rows, width = embeddings.shape
    vmem = pl.BlockSpec(memory_space=pltpu.VMEM)
    return pl.pallas_call(
        functools.partial(sort_kernel, clusters),
        out_shape=(
            jax.ShapeDtypeStruct((rows + tail, width), bf16),
            jax.ShapeDtypeStruct((1, rows), f32),
        ),
        in_specs=[vmem, vmem],
        out_specs=(vmem, vmem),
        scratch_shapes=[pltpu.VMEM((rows, width), bf16), pltpu.VMEM((1, rows), i32)],
        compiler_params=pltpu.CompilerParams(vmem_limit_bytes=40 * MIB),
        cost_estimate=pl.CostEstimate(
            flops=2 * rows * rows * width, bytes_accessed=4 * rows * width, transcendentals=rows
        ),
        name="sort_rows",
    )(ids_row, embeddings)


def assign_kernel(owners, me_ref, counts_ref, tab_ref, bound_ref, bound_t_ref, place_ref):
    clusters = counts_ref.shape[1]
    shift = owners.bit_length() - 1
    me = me_ref[0]
    count = counts_ref[...].astype(f32)
    count16 = count.astype(bf16)
    square = (clusters, clusters)
    sub, lane = iota(square, 0), iota(square, 1)
    eye = sub == lane

    def to_col(row):
        return jnp.sum(jnp.where(eye, row, 0.0), axis=1, keepdims=True)

    total_row = jnp.sum(count, axis=0, keepdims=True)
    total_col = to_col(total_row)
    tie = total_row == total_col
    outranks_col = (total_row > total_col) | (tie & (lane < sub))
    outranks_row = (total_col > total_row) | (tie & (sub < lane))
    rank_col = jnp.sum(outranks_col.astype(f32), axis=1, keepdims=True).astype(i32)
    rank_row = jnp.sum(outranks_row.astype(f32), axis=0, keepdims=True).astype(i32)

    def owner_of(rank, variant):
        layer = rank >> shift
        within = rank & (owners - 1)
        flip = jnp.zeros_like(variant)
        for p in range(1, CL_DEV):
            flip = flip + jnp.where(layer == p, (variant >> (p - 1)) & 1, 0)
        within = within ^ flip
        return jnp.where((layer & 1) == 1, owners - 1 - within, within)

    wide = (clusters, VARIANTS * owners)
    variant = iota(wide, 1) >> shift
    tried = owner_of(rank_col, variant) == (iota(wide, 1) & (owners - 1))
    load = jnp.max(mm(count16, tried.astype(f32).astype(bf16)), axis=0, keepdims=True)
    by_variant = (VARIANTS, VARIANTS * owners)
    worst = jnp.max(
        jnp.where((iota(by_variant, 1) >> shift) == iota(by_variant, 0), load, 0.0),
        axis=1,
        keepdims=True,
    )
    best = jnp.min(worst, axis=0, keepdims=True)
    chosen = jnp.min(
        jnp.where(worst == best, iota((VARIANTS, 1), 0), VARIANTS), axis=0, keepdims=True
    )
    owner_col = owner_of(rank_col, chosen + jnp.zeros_like(rank_col))
    owner_row = owner_of(rank_row, chosen + jnp.zeros_like(rank_row))
    layer_col, layer_row = rank_col >> shift, rank_row >> shift

    mine_row = jnp.sum(
        jnp.where(iota(count.shape, 0) == me, count, 0.0), axis=0, keepdims=True
    )
    mine_col = to_col(mine_row)
    start_col = jnp.sum(jnp.where(lane < sub, mine_row, 0.0), axis=1, keepdims=True)
    earlier = (owner_row == owner_col) & (layer_row < layer_col)
    offset_col = jnp.sum(jnp.where(earlier, mine_row, 0.0), axis=1, keepdims=True)
    perm = lane == layer_col * owners + owner_col

    def by_slot(col):
        return jnp.sum(jnp.where(perm, col, 0.0), axis=0, keepdims=True).astype(i32)

    tab_ref[...] = jnp.zeros_like(tab_ref)
    tab_ref[0:1, 0:clusters] = by_slot(start_col)
    tab_ref[1:2, 0:clusters] = by_slot(mine_col)
    tab_ref[2:3, 0:clusters] = by_slot(offset_col)
    tab_ref[5:6, :] = jnp.broadcast_to(best, (1, tab_ref.shape[1])).astype(i32)

    select = (owner_col == me) & (layer_col <= iota((clusters, 128), 1))
    bound = mm(count16, select.astype(f32).astype(bf16))
    bound_ref[...] = bound
    select_t = (owner_row == me) & (layer_row <= iota((8, clusters), 0))
    bound_t_ref[...] = nt_dot(select_t.astype(f32).astype(bf16), count16)
    first = (iota((owners, 128), 1) * STEP).astype(f32)
    low = jnp.zeros((owners, 128), f32)
    high = jnp.zeros((owners, 128), f32)
    for k in range(CL_DEV):
        edge = bound[:, k : k + 1]
        low = low + (first >= edge).astype(f32)
        high = high + (first + (STEP - 1.0) >= edge).astype(f32)
    tab_ref[3:4, 0:128] = jnp.min(low, axis=0, keepdims=True).astype(i32)
    tab_ref[4:5, 0:128] = jnp.max(high, axis=0, keepdims=True).astype(i32)
    place_ref[...] = jnp.where(
        iota((clusters, 128), 1) == 0, owner_col.astype(f32), offset_col
    )


def assign(counts, me):
    owners, clusters = counts.shape
    vmem = pl.BlockSpec(memory_space=pltpu.VMEM)
    return pl.pallas_call(
        functools.partial(assign_kernel, owners),
        out_shape=(
            jax.ShapeDtypeStruct((8, max(clusters, 128)), i32),
            jax.ShapeDtypeStruct((owners, 128), f32),
            jax.ShapeDtypeStruct((8, owners), f32),
            jax.ShapeDtypeStruct((clusters, 128), f32),
        ),
        in_specs=[pl.BlockSpec(memory_space=pltpu.SMEM), vmem],
        out_specs=(vmem,) * 4,
        compiler_params=pltpu.CompilerParams(vmem_limit_bytes=24 * MIB),
        name="assign",
    )(me, counts)


def pack_kernel(owners, window, group, tab_ref, sorted_ref, out_ref):
    slots = out_ref.shape[1]
    slot = iota((slots, 1), 0)
    for g in range(group):
        owner = pl.program_id(0) * group + g
        runs = []
        source = jnp.full((slots, 1), -1, i32)
        for k in range(CL_DEV):
            start = tab_ref[0, k * owners + owner]
            size = tab_ref[1, k * owners + owner]
            offset = tab_ref[2, k * owners + owner]
            first = pl.multiple_of((start // STEP) * STEP, STEP)
            runs.append(sorted_ref[pl.ds(first, window), :])
            inside = (slot >= offset) & (slot < offset + size)
            source = jnp.where(inside, slot + (k * window + start - first - offset), source)
        take = iota((slots, CL_DEV * window), 1) == source
        out_ref[g] = mm(take.astype(f32).astype(bf16), jnp.concatenate(runs, axis=0)).astype(bf16)


def pack(sorted_rows, tab, owners, slots, window):
    total, width = sorted_rows.shape
    group = 4
    return pl.pallas_call(
        functools.partial(pack_kernel, owners, window, group),
        out_shape=jax.ShapeDtypeStruct((owners, slots, width), bf16),
        grid=(owners // group,),
        in_specs=[
            pl.BlockSpec(memory_space=pltpu.SMEM),
            pl.BlockSpec((total, width), lambda i: (0, 0)),
        ],
        out_specs=pl.BlockSpec((group, slots, width), lambda i: (i, 0, 0)),
        compiler_params=pltpu.CompilerParams(vmem_limit_bytes=40 * MIB),
        name="pack_rows",
    )(tab, sorted_rows)


def score_kernel(
    tab_ref, bound_ref, bound_t_ref, x_ref, out_ref, cid_col, cid_row, row_acc, col_acc
):
    owners, slots, width = x_ref.shape
    chunk = owners * STEP
    chunks = slots // STEP
    half = out_ref.shape[1] // 2

    def load(q):
        return x_ref[:, pl.ds(pl.multiple_of(q * STEP, STEP), STEP), :].reshape(chunk, width)

    spread = (iota((chunk, owners), 0) // STEP) == iota((chunk, owners), 1)
    edges = mm(spread.astype(f32).astype(bf16), bound_ref[...].astype(bf16))
    spread_t = (iota((owners, chunk), 1) // STEP) == iota((owners, chunk), 0)
    edges_t = mm(bound_t_ref[...].astype(bf16), spread_t.astype(f32).astype(bf16))
    in_col = (iota((chunk, 1), 0) % STEP).astype(f32)
    in_row = (iota((1, chunk), 1) % STEP).astype(f32)
    for q in range(chunks):
        col = jnp.zeros((chunk, 1), f32)
        row = jnp.zeros((1, chunk), f32)
        for k in range(CL_DEV):
            col = col + (in_col + q * STEP >= edges[:, k : k + 1]).astype(f32)
            row = row + (in_row + q * STEP >= edges_t[k : k + 1, :]).astype(f32)
        cid_col[q] = col
        cid_row[q] = row

    sums = jnp.zeros((8, width), f32)
    members = jnp.zeros((8, 1), f32)
    for q in range(chunks):
        hot = (cid_row[q] == iota((8, chunk), 0).astype(f32)).astype(f32)
        sums = sums + mm(hot.astype(bf16), load(q))
        members = members + jnp.sum(hot, axis=1, keepdims=True)
    centroid = (sums / jnp.maximum(members, 1.0)).astype(bf16)

    row_acc[...] = jnp.full(row_acc.shape, -1.0, f32)
    col_acc[...] = jnp.full(col_acc.shape, -1.0, f32)

    def lane_fold(m):
        r = m[:, 0:128]
        for i in range(1, chunk // 128):
            r = jnp.maximum(r, m[:, i * 128 : (i + 1) * 128])
        return r

    def sub_fold(m):
        return jnp.max(m.reshape(chunk // 8, 8, chunk), axis=0)

    def own(q1, carry):
        x1 = load(q1)
        same = (cid_col[q1] == cid_row[q1]) & (iota((chunk, chunk), 0) != iota((chunk, chunk), 1))
        m = jnp.where(same, nt_dot(x1, x1), -1.0)
        row_acc[q1] = jnp.maximum(row_acc[q1], lane_fold(m))

        def other(q2, inner):
            @pl.when(tab_ref[3, q2] <= jnp.minimum(tab_ref[4, q1], CL_DEV - 1))
            def _():
                s = nt_dot(load(q1), load(q2))
                t = jnp.where(cid_col[q1] == cid_row[q2], s, -1.0)
                row_acc[q1] = jnp.maximum(row_acc[q1], lane_fold(t))
                col_acc[q2] = jnp.maximum(col_acc[q2], sub_fold(t))

            return inner

        return lax.fori_loop(q1 + 1, chunks, other, carry)

    lax.fori_loop(0, chunks, own, 0)

    eye = iota((chunk, chunk), 0) == iota((chunk, chunk), 1)
    lanes = iota((chunk, half), 1)
    best_z = jnp.zeros((chunk, half), f32)
    gap_z = jnp.zeros((chunk, half), f32)
    for q in range(chunks):
        col = jnp.max(col_acc[q], axis=0, keepdims=True)
        both = jnp.maximum(row_acc[q], lane_fold(jnp.where(eye, col, -1.0)))
        best = jnp.max(both, axis=1, keepdims=True)
        dots = nt_dot(load(q), centroid)
        hit = cid_col[q] == iota((chunk, 8), 1).astype(f32)
        gap = 1.0 - jnp.sum(jnp.where(hit, dots, 0.0), axis=1, keepdims=True)
        here = (lanes // STEP) == q
        best_z = jnp.where(here, best, best_z)
        gap_z = jnp.where(here, gap, gap_z)
    keep = (lanes % STEP) == (iota((chunk, half), 0) % STEP)
    for i, z in enumerate((best_z, gap_z)):
        z = jnp.where(keep, z, 0.0).reshape(owners, STEP, half)
        out_ref[:, i * half : (i + 1) * half] = jnp.sum(z, axis=1)


def score(incoming, tab, bound, bound_t):
    owners, slots, width = incoming.shape
    chunk, chunks = owners * STEP, slots // STEP
    vmem = pl.BlockSpec(memory_space=pltpu.VMEM)
    return pl.pallas_call(
        score_kernel,
        out_shape=jax.ShapeDtypeStruct((owners, 2 * round_up(slots, 128)), f32),
        in_specs=[pl.BlockSpec(memory_space=pltpu.SMEM), vmem, vmem, vmem],
        out_specs=vmem,
        scratch_shapes=[
            pltpu.VMEM((chunks, chunk, 1), f32),
            pltpu.VMEM((chunks, 1, chunk), f32),
            pltpu.VMEM((chunks, chunk, 128), f32),
            pltpu.VMEM((chunks, 8, chunk), f32),
        ],
        compiler_params=pltpu.CompilerParams(vmem_limit_bytes=48 * MIB),
        name="score_rows",
    )(tab, bound, bound_t, incoming)


def restore_kernel(slots, ids_ref, rank_ref, place_ref, back_ref, best_ref, gap_ref):
    rows = ids_ref.shape[1]
    clusters = place_ref.shape[0]
    owners = back_ref.shape[0]
    half = back_ref.shape[1] // 2
    hot = ids_ref[...] == iota((clusters, rows), 0)
    owner = jnp.sum(jnp.where(hot, place_ref[:, 0:1], 0.0), axis=0, keepdims=True)
    offset = jnp.sum(jnp.where(hot, place_ref[:, 1:2], 0.0), axis=0, keepdims=True)
    slot = (offset + rank_ref[...]).astype(i32)
    from_owner = (owner.astype(i32) == iota((owners, rows), 0)).astype(f32).astype(bf16)
    from_owner = jnp.concatenate([from_owner] * 3, axis=0)
    at_slot = slot == iota((slots, rows), 0)
    back = back_ref[...]
    part0 = back.astype(bf16)
    rest = back - part0.astype(f32)
    part1 = rest.astype(bf16)
    part2 = (rest - part1.astype(f32)).astype(bf16)
    parts = jnp.concatenate([part0, part1, part2], axis=0)
    for i, ref in enumerate((best_ref, gap_ref)):
        table = lax.dot_general(
            parts[:, i * half : i * half + slots],
            from_owner,
            (((0,), (0,)), ((), ())),
            preferred_element_type=f32,
        )
        ref[...] = jnp.sum(jnp.where(at_slot, table, 0.0), axis=0, keepdims=True)


def restore(ids_row, rank, place, back, slots):
    rows = ids_row.shape[1]
    vmem = pl.BlockSpec(memory_space=pltpu.VMEM)
    return pl.pallas_call(
        functools.partial(restore_kernel, slots),
        out_shape=(jax.ShapeDtypeStruct((1, rows), f32),) * 2,
        in_specs=[vmem] * 4,
        out_specs=(vmem, vmem),
        compiler_params=pltpu.CompilerParams(vmem_limit_bytes=40 * MIB),
        name="restore_rows",
    )(ids_row, rank, place, back)


def exchange(x):
    return lax.all_to_all(x, "owner", split_axis=0, concat_axis=0, tiled=True)


def local(embeddings, cluster_ids):
    rows = embeddings.shape[0]
    owners = lax.axis_size("owner")
    clusters = CL_DEV * owners
    row_limit = 2 * rows // clusters
    window = round_up(row_limit, STEP) + STEP
    most = round_up(CL_DEV * row_limit, STEP)
    usual = min(most, round_up(9 * rows // (8 * owners), STEP))
    me = lax.axis_index("owner").astype(i32).reshape(1)
    labels = jnp.arange(clusters, dtype=i32)
    local_counts = jnp.sum((cluster_ids[:, None] == labels[None, :]).astype(i32), axis=0)
    counts = exchange(jnp.broadcast_to(local_counts[None, :], (owners, clusters)))
    ids_row = cluster_ids.reshape(1, rows)
    sorted_rows, rank = sort_rows(embeddings, ids_row, clusters, window)
    tab, bound, bound_t, place = assign(counts, me)

    def compare(slots):
        incoming = exchange(pack(sorted_rows, tab, owners, slots, window))
        back = exchange(score(incoming, tab, bound, bound_t))
        return restore(ids_row, rank, place, back, slots)

    best, gap = compare(usual)
    if usual < most:
        best, gap = lax.cond(tab[5, 0] <= usual, lambda: (best, gap), lambda: compare(most))
    return best.reshape(rows), gap.reshape(rows)


def solution(mesh):
    return jax.shard_map(
        local,
        mesh=mesh,
        in_specs=(P(("groups", "owner"), None), P(("groups", "owner"))),
        out_specs=(P(("groups", "owner")), P(("groups", "owner"))),
        check_vma=False,
    )
```

```python
import functools

import jax
import jax.numpy as jnp
from jax import lax
from jax.experimental import pallas as pl
from jax.experimental.pallas import tpu as pltpu
from jax.sharding import PartitionSpec as P

CL_DEV = 4
VARIANTS = 8
STEP = 16
TILE = 256
GROUP = 4
MAX_PERMUTES = 16
MIB = 1 << 20

epsilon = 1e-06
f32 = jnp.float32
bf16 = jnp.bfloat16
i32 = jnp.int32


def iota(shape, axis):
    return lax.broadcasted_iota(i32, shape, axis)


def round_up(value, unit):
    return -(-value // unit) * unit


def nt_dot(a, b):
    return lax.dot_general(a, b, (((1,), (1,)), ((), ())), preferred_element_type=f32)


def mm(a, b):
    return jnp.dot(a, b, preferred_element_type=f32)


def sort_kernel(clusters, ids_ref, rows_ref, sorted_ref, rank_ref, unit_ref, pos_ref):
    rows = rows_ref.shape[0]
    blocks = rows // TILE
    label = iota((clusters, TILE), 0)
    upto = (iota((TILE, TILE), 0) <= iota((TILE, TILE), 1)).astype(bf16)
    total = jnp.zeros((clusters, 1), f32)
    for b in range(blocks):
        at = slice(b * TILE, (b + 1) * TILE)
        hot = ids_ref[:, at] == label
        hot16 = hot.astype(f32).astype(bf16)
        prefix = mm(hot16, upto)
        rank_ref[:, at] = jnp.sum(jnp.where(hot, prefix + total - 1.0, 0.0), axis=0, keepdims=True)
        total = total + prefix[:, TILE - 1 :]
    square = (clusters, clusters)
    total_row = jnp.sum(
        jnp.where(iota(square, 0) == iota(square, 1), total, 0.0), axis=0, keepdims=True
    )
    start = jnp.sum(
        jnp.where(iota(square, 1) < iota(square, 0), total_row, 0.0), axis=1, keepdims=True
    )
    for b in range(blocks):
        at = slice(b * TILE, (b + 1) * TILE)
        hot = ids_ref[:, at] == label
        first = jnp.sum(jnp.where(hot, start, 0.0), axis=0, keepdims=True)
        pos_ref[:, at] = (first + rank_ref[:, at]).astype(i32)

    def normalise(b, carry):
        at = pl.ds(pl.multiple_of(b * TILE, TILE), TILE)
        x = rows_ref[at, :].astype(f32)
        scale = lax.rsqrt(jnp.sum(x * x, axis=1, keepdims=True) + epsilon)
        unit_ref[at, :] = (x * scale).astype(bf16)
        return carry

    lax.fori_loop(0, blocks, normalise, 0)

    def arrange(b, carry):
        first = pl.multiple_of(b * TILE, TILE)
        take = (iota((TILE, rows), 0) + first) == pos_ref[...]
        sorted_ref[pl.ds(first, TILE), :] = mm(
            take.astype(f32).astype(bf16), unit_ref[...]
        ).astype(bf16)
        return carry

    lax.fori_loop(0, blocks, arrange, 0)
    tail = sorted_ref.shape[0] - rows
    sorted_ref[rows:, :] = jnp.zeros((tail, sorted_ref.shape[1]), bf16)


def sort_rows(embeddings, ids_row, clusters, tail):
    rows, width = embeddings.shape
    vmem = pl.BlockSpec(memory_space=pltpu.VMEM)
    return pl.pallas_call(
        functools.partial(sort_kernel, clusters),
        out_shape=(
            jax.ShapeDtypeStruct((rows + tail, width), bf16),
            jax.ShapeDtypeStruct((1, rows), f32),
        ),
        in_specs=[vmem, vmem],
        out_specs=(vmem, vmem),
        scratch_shapes=[pltpu.VMEM((rows, width), bf16), pltpu.VMEM((1, rows), i32)],
        compiler_params=pltpu.CompilerParams(vmem_limit_bytes=40 * MIB),
        cost_estimate=pl.CostEstimate(
            flops=2 * rows * rows * width, bytes_accessed=4 * rows * width, transcendentals=rows
        ),
        name="sort_rows",
    )(ids_row, embeddings)


def assign_kernel(owners, me_ref, *refs):
    counts_refs, (tab_ref, bound_ref, bound_t_ref, place_ref) = refs[:owners], refs[owners:]
    clusters = counts_refs[0].shape[1]
    shift = owners.bit_length() - 1
    me = me_ref[0]
    count = jnp.concatenate([ref[...] for ref in counts_refs], axis=0).astype(f32)
    count16 = count.astype(bf16)
    square = (clusters, clusters)
    sub, lane = iota(square, 0), iota(square, 1)
    eye = sub == lane

    def to_col(row):
        return jnp.sum(jnp.where(eye, row, 0.0), axis=1, keepdims=True)

    total_row = jnp.sum(count, axis=0, keepdims=True)
    total_col = to_col(total_row)
    tie = total_row == total_col
    outranks_col = (total_row > total_col) | (tie & (lane < sub))
    outranks_row = (total_col > total_row) | (tie & (sub < lane))
    rank_col = jnp.sum(outranks_col.astype(f32), axis=1, keepdims=True).astype(i32)
    rank_row = jnp.sum(outranks_row.astype(f32), axis=0, keepdims=True).astype(i32)

    def owner_of(rank, variant):
        layer = rank >> shift
        within = rank & (owners - 1)
        flip = jnp.zeros_like(variant)
        for p in range(1, CL_DEV):
            flip = flip + jnp.where(layer == p, (variant >> (p - 1)) & 1, 0)
        within = within ^ flip
        return jnp.where((layer & 1) == 1, owners - 1 - within, within)

    wide = (clusters, VARIANTS * owners)
    variant = iota(wide, 1) >> shift
    tried = owner_of(rank_col, variant) == (iota(wide, 1) & (owners - 1))
    load = jnp.max(mm(count16, tried.astype(f32).astype(bf16)), axis=0, keepdims=True)
    by_variant = (VARIANTS, VARIANTS * owners)
    worst = jnp.max(
        jnp.where((iota(by_variant, 1) >> shift) == iota(by_variant, 0), load, 0.0),
        axis=1,
        keepdims=True,
    )
    best = jnp.min(worst, axis=0, keepdims=True)
    chosen = jnp.min(
        jnp.where(worst == best, iota((VARIANTS, 1), 0), VARIANTS), axis=0, keepdims=True
    )
    owner_col = owner_of(rank_col, chosen + jnp.zeros_like(rank_col))
    owner_row = owner_of(rank_row, chosen + jnp.zeros_like(rank_row))
    layer_col, layer_row = rank_col >> shift, rank_row >> shift

    mine_row = count[0:1, :]
    mine_col = to_col(mine_row)
    start_col = jnp.sum(jnp.where(lane < sub, mine_row, 0.0), axis=1, keepdims=True)
    earlier = (owner_row == owner_col) & (layer_row < layer_col)
    offset_col = jnp.sum(jnp.where(earlier, mine_row, 0.0), axis=1, keepdims=True)
    perm = lane == layer_col * owners + (owner_col ^ me)

    def by_slot(col):
        return jnp.sum(jnp.where(perm, col, 0.0), axis=0, keepdims=True).astype(i32)

    tab_ref[...] = jnp.zeros_like(tab_ref)
    tab_ref[0:1, 0:clusters] = by_slot(start_col)
    tab_ref[1:2, 0:clusters] = by_slot(mine_col)
    tab_ref[2:3, 0:clusters] = by_slot(offset_col)
    tab_ref[5:6, :] = jnp.broadcast_to(best, (1, tab_ref.shape[1])).astype(i32)

    select = (owner_col == me) & (layer_col <= iota((clusters, 128), 1))
    bound = mm(count16, select.astype(f32).astype(bf16))
    bound_ref[...] = bound
    select_t = (owner_row == me) & (layer_row <= iota((8, clusters), 0))
    bound_t_ref[...] = nt_dot(select_t.astype(f32).astype(bf16), count16)
    first = (iota((owners, 128), 1) * STEP).astype(f32)
    low = jnp.zeros((owners, 128), f32)
    high = jnp.zeros((owners, 128), f32)
    for k in range(CL_DEV):
        edge = bound[:, k : k + 1]
        low = low + (first >= edge).astype(f32)
        high = high + (first + (STEP - 1.0) >= edge).astype(f32)
    tab_ref[3:4, 0:128] = jnp.min(low, axis=0, keepdims=True).astype(i32)
    tab_ref[4:5, 0:128] = jnp.max(high, axis=0, keepdims=True).astype(i32)
    place_ref[...] = jnp.where(
        iota((clusters, 128), 1) == 0, (owner_col ^ me).astype(f32), offset_col
    )


def assign(counts, me):
    owners, clusters = len(counts), counts[0].shape[1]
    vmem = pl.BlockSpec(memory_space=pltpu.VMEM)
    return pl.pallas_call(
        functools.partial(assign_kernel, owners),
        out_shape=(
            jax.ShapeDtypeStruct((8, max(clusters, 128)), i32),
            jax.ShapeDtypeStruct((owners, 128), f32),
            jax.ShapeDtypeStruct((8, owners), f32),
            jax.ShapeDtypeStruct((clusters, 128), f32),
        ),
        in_specs=[pl.BlockSpec(memory_space=pltpu.SMEM)] + [vmem] * owners,
        out_specs=(vmem,) * 4,
        compiler_params=pltpu.CompilerParams(vmem_limit_bytes=24 * MIB),
        name="assign",
    )(me, *counts)


def pack_kernel(owners, window, partners, tab_ref, sorted_ref, *out_refs):
    slots = out_refs[0].shape[0]
    slot = iota((slots, 1), 0)
    for partner, out_ref in zip(partners, out_refs):
        runs = []
        source = jnp.full((slots, 1), -1, i32)
        for k in range(CL_DEV):
            start = tab_ref[0, k * owners + partner]
            size = tab_ref[1, k * owners + partner]
            offset = tab_ref[2, k * owners + partner]
            first = pl.multiple_of((start // STEP) * STEP, STEP)
            runs.append(sorted_ref[pl.ds(first, window), :])
            inside = (slot >= offset) & (slot < offset + size)
            source = jnp.where(inside, slot + (k * window + start - first - offset), source)
        take = iota((slots, CL_DEV * window), 1) == source
        out_ref[...] = mm(take.astype(f32).astype(bf16), jnp.concatenate(runs, axis=0)).astype(bf16)


def pack(sorted_rows, tab, owners, partners, slots, window):
    width = sorted_rows.shape[1]
    vmem = pl.BlockSpec(memory_space=pltpu.VMEM)
    return pl.pallas_call(
        functools.partial(pack_kernel, owners, window, partners),
        out_shape=(jax.ShapeDtypeStruct((slots, width), bf16),) * len(partners),
        in_specs=[pl.BlockSpec(memory_space=pltpu.SMEM), vmem],
        out_specs=(vmem,) * len(partners),
        compiler_params=pltpu.CompilerParams(vmem_limit_bytes=24 * MIB),
        name="pack_rows",
    )(tab, sorted_rows)


def score_kernel(
    owners, tab_ref, bound_ref, bound_t_ref, *refs
):
    x_refs, out_refs = refs[:owners], refs[owners : 2 * owners]
    cid_col, cid_row, row_acc, col_acc = refs[2 * owners :]
    slots, width = x_refs[0].shape
    chunk = owners * STEP
    chunks = slots // STEP
    half = out_refs[0].shape[1] // 2

    def load(q):
        at = pl.ds(pl.multiple_of(q * STEP, STEP), STEP)
        return jnp.concatenate([ref[at, :] for ref in x_refs], axis=0)

    spread = (iota((chunk, owners), 0) // STEP) == iota((chunk, owners), 1)
    edges = mm(spread.astype(f32).astype(bf16), bound_ref[...].astype(bf16))
    spread_t = (iota((owners, chunk), 1) // STEP) == iota((owners, chunk), 0)
    edges_t = mm(bound_t_ref[...].astype(bf16), spread_t.astype(f32).astype(bf16))
    in_col = (iota((chunk, 1), 0) % STEP).astype(f32)
    in_row = (iota((1, chunk), 1) % STEP).astype(f32)
    for q in range(chunks):
        col = jnp.zeros((chunk, 1), f32)
        row = jnp.zeros((1, chunk), f32)
        for k in range(CL_DEV):
            col = col + (in_col + q * STEP >= edges[:, k : k + 1]).astype(f32)
            row = row + (in_row + q * STEP >= edges_t[k : k + 1, :]).astype(f32)
        cid_col[q] = col
        cid_row[q] = row

    sums = jnp.zeros((8, width), f32)
    members = jnp.zeros((8, 1), f32)
    for q in range(chunks):
        hot = (cid_row[q] == iota((8, chunk), 0).astype(f32)).astype(f32)
        sums = sums + mm(hot.astype(bf16), load(q))
        members = members + jnp.sum(hot, axis=1, keepdims=True)
    centroid = (sums / jnp.maximum(members, 1.0)).astype(bf16)

    row_acc[...] = jnp.full(row_acc.shape, -1.0, f32)
    col_acc[...] = jnp.full(col_acc.shape, -1.0, f32)

    def lane_fold(m):
        r = m[:, 0:128]
        for i in range(1, chunk // 128):
            r = jnp.maximum(r, m[:, i * 128 : (i + 1) * 128])
        return r

    def sub_fold(m):
        return jnp.max(m.reshape(chunk // 8, 8, chunk), axis=0)

    def own(q1, carry):
        x1 = load(q1)
        same = (cid_col[q1] == cid_row[q1]) & (iota((chunk, chunk), 0) != iota((chunk, chunk), 1))
        m = jnp.where(same, nt_dot(x1, x1), -1.0)
        row_acc[q1] = jnp.maximum(row_acc[q1], lane_fold(m))

        def other(q2, inner):
            @pl.when(tab_ref[3, q2] <= jnp.minimum(tab_ref[4, q1], CL_DEV - 1))
            def _():
                s = nt_dot(load(q1), load(q2))
                t = jnp.where(cid_col[q1] == cid_row[q2], s, -1.0)
                row_acc[q1] = jnp.maximum(row_acc[q1], lane_fold(t))
                col_acc[q2] = jnp.maximum(col_acc[q2], sub_fold(t))

            return inner

        return lax.fori_loop(q1 + 1, chunks, other, carry)

    lax.fori_loop(0, chunks, own, 0)

    eye = iota((chunk, chunk), 0) == iota((chunk, chunk), 1)
    lanes = iota((chunk, half), 1)
    best_z = jnp.zeros((chunk, half), f32)
    gap_z = jnp.zeros((chunk, half), f32)
    for q in range(chunks):
        col = jnp.max(col_acc[q], axis=0, keepdims=True)
        both = jnp.maximum(row_acc[q], lane_fold(jnp.where(eye, col, -1.0)))
        best = jnp.max(both, axis=1, keepdims=True)
        dots = nt_dot(load(q), centroid)
        hit = cid_col[q] == iota((chunk, 8), 1).astype(f32)
        gap = 1.0 - jnp.sum(jnp.where(hit, dots, 0.0), axis=1, keepdims=True)
        here = (lanes // STEP) == q
        best_z = jnp.where(here, best, best_z)
        gap_z = jnp.where(here, gap, gap_z)
    keep = (lanes % STEP) == (iota((chunk, half), 0) % STEP)
    for i, z in enumerate((best_z, gap_z)):
        z = jnp.where(keep, z, 0.0).reshape(owners, STEP, half)
        z = jnp.sum(z, axis=1)
        for r, ref in enumerate(out_refs):
            ref[:, i * half : (i + 1) * half] = z[r : r + 1, :]


def score(incoming, tab, bound, bound_t):
    owners = len(incoming)
    slots, width = incoming[0].shape
    chunk, chunks = owners * STEP, slots // STEP
    vmem = pl.BlockSpec(memory_space=pltpu.VMEM)
    return pl.pallas_call(
        functools.partial(score_kernel, owners),
        out_shape=(jax.ShapeDtypeStruct((1, 2 * round_up(slots, 128)), f32),) * owners,
        in_specs=[pl.BlockSpec(memory_space=pltpu.SMEM)] + [vmem] * (2 + owners),
        out_specs=(vmem,) * owners,
        scratch_shapes=[
            pltpu.VMEM((chunks, chunk, 1), f32),
            pltpu.VMEM((chunks, 1, chunk), f32),
            pltpu.VMEM((chunks, chunk, 128), f32),
            pltpu.VMEM((chunks, 8, chunk), f32),
        ],
        compiler_params=pltpu.CompilerParams(vmem_limit_bytes=48 * MIB),
        name="score_rows",
    )(tab, bound, bound_t, *incoming)


def restore_kernel(slots, ids_ref, rank_ref, place_ref, *refs):
    back_refs, (best_ref, gap_ref) = refs[:-2], refs[-2:]
    rows = ids_ref.shape[1]
    clusters = place_ref.shape[0]
    owners = len(back_refs)
    half = back_refs[0].shape[1] // 2
    hot = ids_ref[...] == iota((clusters, rows), 0)
    owner = jnp.sum(jnp.where(hot, place_ref[:, 0:1], 0.0), axis=0, keepdims=True)
    offset = jnp.sum(jnp.where(hot, place_ref[:, 1:2], 0.0), axis=0, keepdims=True)
    slot = (offset + rank_ref[...]).astype(i32)
    from_owner = (owner.astype(i32) == iota((owners, rows), 0)).astype(f32).astype(bf16)
    from_owner = jnp.concatenate([from_owner] * 3, axis=0)
    at_slot = slot == iota((slots, rows), 0)
    back = jnp.concatenate([ref[...] for ref in back_refs], axis=0)
    part0 = back.astype(bf16)
    rest = back - part0.astype(f32)
    part1 = rest.astype(bf16)
    part2 = (rest - part1.astype(f32)).astype(bf16)
    parts = jnp.concatenate([part0, part1, part2], axis=0)
    for i, ref in enumerate((best_ref, gap_ref)):
        table = lax.dot_general(
            parts[:, i * half : i * half + slots],
            from_owner,
            (((0,), (0,)), ((), ())),
            preferred_element_type=f32,
        )
        ref[...] = jnp.sum(jnp.where(at_slot, table, 0.0), axis=0, keepdims=True)


def restore(ids_row, rank, place, back, slots):
    rows = ids_row.shape[1]
    vmem = pl.BlockSpec(memory_space=pltpu.VMEM)
    return pl.pallas_call(
        functools.partial(restore_kernel, slots),
        out_shape=(jax.ShapeDtypeStruct((1, rows), f32),) * 2,
        in_specs=[vmem] * (3 + len(back)),
        out_specs=(vmem, vmem),
        compiler_params=pltpu.CompilerParams(vmem_limit_bytes=40 * MIB),
        name="restore_rows",
    )(ids_row, rank, place, *back)


def swap(x, partner):
    if partner == 0:
        return x
    owners = lax.axis_size("owner")
    return lax.ppermute(x, "owner", [(i, i ^ partner) for i in range(owners)])


def swap_together(blocks):
    owners = len(blocks)
    order = jnp.arange(owners, dtype=i32) ^ lax.axis_index("owner").astype(i32)
    stacked = jnp.stack(blocks)[order]
    arrived = lax.all_to_all(stacked, "owner", split_axis=0, concat_axis=0, tiled=True)[order]
    return [arrived[r] for r in range(owners)]


def swap_all(blocks, apart):
    if not apart:
        return swap_together(blocks)
    return [swap(block, r) for r, block in enumerate(blocks)]


def local(embeddings, cluster_ids):
    rows = embeddings.shape[0]
    owners = lax.axis_size("owner")
    clusters = CL_DEV * owners
    row_limit = 2 * rows // clusters
    window = round_up(row_limit, STEP) + STEP
    most = round_up(CL_DEV * row_limit, STEP)
    usual = min(most, round_up(9 * rows // (8 * owners), STEP))
    me = lax.axis_index("owner").astype(i32).reshape(1)
    labels = jnp.arange(clusters, dtype=i32)
    local_counts = jnp.sum((cluster_ids[:, None] == labels[None, :]).astype(i32), axis=0)
    local_counts = local_counts.reshape(1, clusters)
    few = owners <= MAX_PERMUTES
    counts = swap_all([local_counts] * owners, few)
    ids_row = cluster_ids.reshape(1, rows)
    sorted_rows, rank = sort_rows(embeddings, ids_row, clusters, window)
    tab, bound, bound_t, place = assign(counts, me)

    half = owners // 2
    order = [r for i in reversed(range(half)) for r in (half + i, i)]

    def compare(slots, apart):
        blocks = [None] * owners
        for first in range(0, owners, GROUP):
            partners = tuple(order[first : first + GROUP])
            packed = pack(sorted_rows, tab, owners, partners, slots, window)
            for r, block in zip(partners, packed):
                blocks[r] = swap(block, r) if apart else block
        incoming = blocks if apart else swap_together(blocks)
        back = swap_all(score(incoming, tab, bound, bound_t), apart)
        return restore(ids_row, rank, place, back, slots)

    best, gap = compare(usual, few)
    if usual < most:
        best, gap = lax.cond(
            tab[5, 0] <= usual, lambda: (best, gap), lambda: compare(most, False)
        )
    return best.reshape(rows), gap.reshape(rows)


def solution(mesh):
    return jax.shard_map(
        local,
        mesh=mesh,
        in_specs=(P(("groups", "owner"), None), P(("groups", "owner"))),
        out_specs=(P(("groups", "owner")), P(("groups", "owner"))),
        check_vma=False,
    )
```

```python
import functools

import jax
import jax.numpy as jnp
from jax import lax
from jax.experimental import pallas as pl
from jax.experimental.pallas import tpu as pltpu
from jax.sharding import PartitionSpec as P

CL_DEV = 4
VARIANTS = 8
STEP = 16
TILE = 256
LANES = 128
GROUP = 4
FLIGHT = 5
MAX_PERMUTES = 16
MIB = 1 << 20

epsilon = 1e-06
f32 = jnp.float32
bf16 = jnp.bfloat16
i32 = jnp.int32
VMEM = pl.BlockSpec(memory_space=pltpu.VMEM)
SMEM = pl.BlockSpec(memory_space=pltpu.SMEM)


def iota(shape, axis):
    return lax.broadcasted_iota(i32, shape, axis)


def round_up(value, unit):
    return -(-value // unit) * unit


def nt_dot(a, b):
    return lax.dot_general(a, b, (((1,), (1,)), ((), ())), preferred_element_type=f32)


def mm(a, b):
    return jnp.dot(a, b, preferred_element_type=f32)


def to_bf16(mask):
    return mask.astype(f32).astype(bf16)


def count_kernel(ids_ref, counts_ref, rank_ref):
    rows = ids_ref.shape[1]
    owners, _, clusters = counts_ref.shape
    label = iota((clusters, TILE), 0)
    upto = to_bf16(iota((TILE, TILE), 0) <= iota((TILE, TILE), 1))
    total = jnp.zeros((clusters, 1), f32)
    for b in range(rows // TILE):
        at = slice(b * TILE, (b + 1) * TILE)
        hot = ids_ref[:, at] == label
        prefix = mm(to_bf16(hot), upto)
        rank_ref[:, at] = jnp.sum(jnp.where(hot, prefix + total - 1.0, 0.0), axis=0, keepdims=True)
        total = total + prefix[:, TILE - 1 :]
    square = (clusters, clusters)
    eye = iota(square, 0) == iota(square, 1)
    total_row = jnp.sum(jnp.where(eye, total, 0.0), axis=0, keepdims=True).astype(i32)
    for owner in range(owners):
        counts_ref[owner] = total_row


def count_rows(ids_row, owners, clusters):
    return pl.pallas_call(
        count_kernel,
        out_shape=(
            jax.ShapeDtypeStruct((owners, 1, clusters), i32),
            jax.ShapeDtypeStruct(ids_row.shape, f32),
        ),
        in_specs=[VMEM],
        out_specs=(VMEM, VMEM),
        compiler_params=pltpu.CompilerParams(vmem_limit_bytes=16 * MIB),
        name="count_rows",
    )(ids_row)


def assign_kernel(
    me_ref, counts_ref, ids_ref, rank_ref, owner_ref, slot_ref, bound_ref, total_ref, load_ref
):
    owners, _, clusters = counts_ref.shape
    rows = ids_ref.shape[1]
    shift = owners.bit_length() - 1
    me = me_ref[0]
    count = jnp.concatenate([counts_ref[s] for s in range(owners)], axis=0).astype(f32)
    count16 = count.astype(bf16)
    square = (clusters, clusters)
    sub, lane = iota(square, 0), iota(square, 1)
    total_row = jnp.sum(count, axis=0, keepdims=True)
    total_col = jnp.sum(jnp.where(sub == lane, total_row, 0.0), axis=1, keepdims=True)
    tie = total_row == total_col
    outranks_col = (total_row > total_col) | (tie & (lane < sub))
    outranks_row = (total_col > total_row) | (tie & (sub < lane))
    rank_col = jnp.sum(outranks_col.astype(f32), axis=1, keepdims=True).astype(i32)
    rank_row = jnp.sum(outranks_row.astype(f32), axis=0, keepdims=True).astype(i32)

    def owner_of(rank, variant):
        layer = rank >> shift
        within = rank & (owners - 1)
        flip = jnp.zeros_like(variant)
        for p in range(1, CL_DEV):
            flip = flip + jnp.where(layer == p, (variant >> (p - 1)) & 1, 0)
        within = within ^ flip
        return jnp.where((layer & 1) == 1, owners - 1 - within, within)

    wide = (clusters, VARIANTS * owners)
    variant = iota(wide, 1) >> shift
    tried = owner_of(rank_col, variant) == (iota(wide, 1) & (owners - 1))
    load = jnp.max(mm(count16, to_bf16(tried)), axis=0, keepdims=True)
    by_variant = (VARIANTS, VARIANTS * owners)
    worst = jnp.max(
        jnp.where((iota(by_variant, 1) >> shift) == iota(by_variant, 0), load, 0.0),
        axis=1,
        keepdims=True,
    )
    best = jnp.min(worst, axis=0, keepdims=True)
    chosen = jnp.min(
        jnp.where(worst == best, iota((VARIANTS, 1), 0), VARIANTS), axis=0, keepdims=True
    )
    owner_col = owner_of(rank_col, chosen + jnp.zeros_like(rank_col))
    owner_row = owner_of(rank_row, chosen + jnp.zeros_like(rank_row))
    layer_col, layer_row = rank_col >> shift, rank_row >> shift
    load_ref[...] = jnp.broadcast_to(best, load_ref.shape).astype(i32)

    mine = jnp.sum(jnp.where(iota(count.shape, 0) == me, count, 0.0), axis=0, keepdims=True)
    earlier = (owner_row == owner_col) & (layer_row < layer_col)
    offset_col = jnp.sum(jnp.where(earlier, mine, 0.0), axis=1, keepdims=True)
    hot = ids_ref[...] == iota((clusters, rows), 0)
    owner_ref[...] = jnp.sum(
        jnp.where(hot, owner_col.astype(f32), 0.0), axis=0, keepdims=True
    ).astype(i32)
    slot_ref[...] = (
        jnp.sum(jnp.where(hot, offset_col, 0.0), axis=0, keepdims=True) + rank_ref[...]
    ).astype(i32)

    select = (owner_col == me) & (layer_col <= iota((clusters, LANES), 1))
    turn = iota((owners, owners), 1) == (iota((owners, owners), 0) ^ me)
    turned = mm(to_bf16(turn), count16).astype(bf16)
    bound_ref[...] = mm(turned, to_bf16(select))
    own = (owner_row == me) & (layer_row == iota((8, clusters), 0))
    total_ref[...] = jnp.broadcast_to(
        jnp.sum(jnp.where(own, total_row, 0.0), axis=1, keepdims=True), total_ref.shape
    )


def assign(me, counts, ids_row, rank):
    owners, _, clusters = counts.shape
    rows = ids_row.shape[1]
    return pl.pallas_call(
        assign_kernel,
        out_shape=(
            jax.ShapeDtypeStruct((1, rows), i32),
            jax.ShapeDtypeStruct((1, rows), i32),
            jax.ShapeDtypeStruct((owners, LANES), f32),
            jax.ShapeDtypeStruct((8, LANES), f32),
            jax.ShapeDtypeStruct((1, LANES), i32),
        ),
        in_specs=[SMEM, VMEM, VMEM, VMEM],
        out_specs=(VMEM,) * 5,
        compiler_params=pltpu.CompilerParams(vmem_limit_bytes=16 * MIB),
        name="assign",
    )(me, counts, ids_row, rank)


def pack_kernel(slots, partners, me_ref, owner_ref, slot_ref, rows_ref, *out_refs):
    rows = rows_ref.shape[0]
    me = me_ref[0]
    slot = iota((slots, rows), 0)
    takes = []
    for partner in partners:
        key = jnp.where(owner_ref[...] == (me ^ partner), slot_ref[...], -1)
        takes.append(to_bf16(slot == key))
    picked = mm(jnp.concatenate(takes, axis=0), rows_ref[...]).astype(bf16)
    for i, ref in enumerate(out_refs):
        ref[...] = picked[i * slots : (i + 1) * slots]


def pack(me, owner_row, slot_row, embeddings, partners, slots):
    rows, width = embeddings.shape
    flops = 2 * len(partners) * slots * rows * width
    return pl.pallas_call(
        functools.partial(pack_kernel, slots, partners),
        out_shape=(jax.ShapeDtypeStruct((slots, width), bf16),) * len(partners),
        in_specs=[SMEM, VMEM, VMEM, VMEM],
        out_specs=(VMEM,) * len(partners),
        compiler_params=pltpu.CompilerParams(vmem_limit_bytes=28 * MIB),
        cost_estimate=pl.CostEstimate(
            flops=flops, bytes_accessed=2 * rows * width, transcendentals=0
        ),
        name="pack_rows",
    )(me, owner_row, slot_row, embeddings)


def unit_rows(ref):
    x = ref[...].astype(f32)
    scale = lax.rsqrt(jnp.sum(x * x, axis=1, keepdims=True) + epsilon)
    return (x * scale).astype(bf16)


def cluster_lanes(bound_ref, partners, slots, width):
    lane = iota((1, width), 1).astype(f32)
    result = jnp.where(lane < len(partners) * slots, 0.0, -1.0)
    for i, r in enumerate(partners):
        for k in range(CL_DEV):
            first = bound_ref[r : r + 1, k : k + 1] + float(i * slots)
            result = result + ((lane >= first) & (lane < float((i + 1) * slots))).astype(f32)
    return result


def cluster_rows(bound_ref, r, slots):
    slot = iota((slots, LANES), 0).astype(f32)
    result = jnp.zeros((slots, LANES), f32)
    for k in range(CL_DEV):
        result = result + (slot >= bound_ref[r : r + 1, k : k + 1]).astype(f32)
    return result


def score_group(new_ref, new_cids, olds, cid_row, slots_new):
    padded = new_ref.shape[0]
    groups = padded // LANES
    new = new_ref[...]

    def folded(scores, cids, skip_same):
        rows = scores.shape[0]
        row = iota((rows, LANES), 0)
        lane = iota((rows, LANES), 1)
        best, cols = None, []
        for g in range(groups):
            at = slice(g * LANES, (g + 1) * LANES)
            allowed = cids == cid_row[:, at]
            if skip_same:
                allowed = allowed & (row != lane + g * LANES)
            part = jnp.where(allowed, scores[:, at], -1.0)
            best = part if best is None else jnp.maximum(best, part)
            cols.append(jnp.max(part, axis=0, keepdims=True))
        return best, cols

    columns = None
    results = []
    for unit_ref, acc_ref, cid_ref in olds:
        scores = nt_dot(unit_ref[...], new)
        best, cols = folded(scores, cid_ref[...], False)
        columns = cols if columns is None else [jnp.maximum(a, b) for a, b in zip(columns, cols)]
        results.append((scores, jnp.maximum(acc_ref[...], best)))
    scores = nt_dot(new[0:slots_new], new)
    best, _ = folded(scores, new_cids, True)
    if columns is not None:
        row = iota((slots_new, LANES), 0)
        lane = iota((slots_new, LANES), 1)
        for g, col in enumerate(columns):
            best = jnp.maximum(best, jnp.where(row == lane + g * LANES, col, -1.0))
    results.append((scores, best))
    return results


def member_sums(cid_row, new):
    hot = to_bf16(cid_row == iota((8, cid_row.shape[1]), 0).astype(f32))
    return mm(hot, new)


def score_kernel(slots, partners, olds, bound_ref, *refs):
    fresh = len(partners)
    raw_refs, refs = refs[:fresh], refs[fresh:]
    old_refs = [refs[3 * i : 3 * i + 3] for i in range(olds)]
    refs = refs[3 * olds :]
    if olds:
        sums_ref, refs = refs[0], refs[1:]
    unit_ref, acc_ref, cid_ref, sums_out = refs[:4]
    old_accs = refs[4 : 4 + olds]
    new_ref = refs[4 + olds]
    rows = fresh * slots
    for i, r in enumerate(partners):
        at = slice(i * slots, (i + 1) * slots)
        new_ref[at, :] = unit_rows(raw_refs[i])
        cid_ref[at, :] = cluster_rows(bound_ref, r, slots)
    padded = new_ref.shape[0]
    if padded > rows:
        new_ref[rows:, :] = jnp.zeros((padded - rows, new_ref.shape[1]), bf16)
    unit_ref[...] = new_ref[0:rows, :]
    cid_row = cluster_lanes(bound_ref, partners, slots, padded)
    results = score_group(new_ref, cid_ref[...], old_refs, cid_row, rows)
    for (_, best), ref in zip(results, list(old_accs) + [acc_ref]):
        ref[...] = best
    sums = member_sums(cid_row, new_ref[...])
    sums_out[...] = sums + sums_ref[...] if olds else sums


def score(bound, blocks, partners, state):
    slots, width = blocks[0].shape
    units, accs, cids, sums = state
    rows = len(blocks) * slots
    padded = round_up(rows, LANES)
    old = [x for group in zip(units, accs, cids) for x in group]
    old_rows = sum(u.shape[0] for u in units)
    acc_shapes = [jax.ShapeDtypeStruct(a.shape, f32) for a in accs]
    out_shape = (
        jax.ShapeDtypeStruct((rows, width), bf16),
        jax.ShapeDtypeStruct((rows, LANES), f32),
        jax.ShapeDtypeStruct((rows, LANES), f32),
        jax.ShapeDtypeStruct((8, width), f32),
        *acc_shapes,
    )
    args = [bound, *blocks, *old] + ([sums] if units else [])
    out = pl.pallas_call(
        functools.partial(score_kernel, slots, partners, len(units)),
        out_shape=out_shape,
        in_specs=[VMEM] * len(args),
        out_specs=(VMEM,) * len(out_shape),
        scratch_shapes=[pltpu.VMEM((padded, width), bf16)],
        compiler_params=pltpu.CompilerParams(vmem_limit_bytes=36 * MIB),
        cost_estimate=pl.CostEstimate(
            flops=2 * (old_rows + rows) * padded * width,
            bytes_accessed=2 * (old_rows + rows) * width,
            transcendentals=rows,
        ),
        name="score_rows",
    )(*args)
    return units + [out[0]], list(out[4:]) + [out[1]], cids + [out[2]], out[3]


def finish_kernel(slots, partners, earlier, olds, me_ref, bound_ref, total_ref, *refs):
    fresh = len(partners)
    raw_refs, refs = refs[:fresh], refs[fresh:]
    old_refs = [refs[3 * i : 3 * i + 3] for i in range(olds)]
    sums_ref, out_ref, new_ref = refs[3 * olds :]
    me = me_ref[0]
    rows = fresh * slots
    padded, width = new_ref.shape
    new_ref[rows:, :] = jnp.zeros((padded - rows, width), bf16)
    pieces = []
    for i, r in enumerate(partners):
        new_ref[i * slots : (i + 1) * slots, :] = unit_rows(raw_refs[i])
        pieces.append(cluster_rows(bound_ref, r, slots))
    new_cids = jnp.concatenate(pieces, axis=0)
    cid_row = cluster_lanes(bound_ref, partners, slots, padded)
    sums = sums_ref[...] + member_sums(cid_row, new_ref[...])
    centroid = (sums / jnp.maximum(total_ref[:, 0:1], 1.0)).astype(bf16)
    centroid = jnp.concatenate([centroid, jnp.zeros_like(centroid)], axis=0)
    new_ref[rows : rows + STEP, :] = centroid
    results = score_group(new_ref, new_cids, old_refs, cid_row, rows)
    half = out_ref.shape[2] // 2
    group, within = rows // LANES, rows % LANES
    eye = iota((slots, half), 0) == iota((slots, half), 1)
    all_cids = [old[2][...] for old in old_refs] + [new_cids]
    for (scores, acc), cids, names in zip(results, all_cids, earlier + [partners]):
        best = jnp.max(acc, axis=1, keepdims=True)
        lane = iota(cids.shape, 1).astype(f32)
        dots = scores[:, group * LANES : (group + 1) * LANES]
        gap = 1.0 - jnp.sum(
            jnp.where(lane == cids + float(within), dots, 0.0), axis=1, keepdims=True
        )
        for i, r in enumerate(names):
            at = slice(i * slots, (i + 1) * slots)
            for j, col in enumerate((best, gap)):
                line = jnp.sum(jnp.where(eye, col[at], 0.0), axis=0, keepdims=True)
                out_ref[r ^ me, :, j * half : (j + 1) * half] = line


def finish(me, bound, total, blocks, partners, earlier, state):
    slots, width = blocks[0].shape
    owners = bound.shape[0]
    units, accs, cids, sums = state
    rows = len(blocks) * slots
    padded = round_up(rows + STEP, LANES)
    old = [x for group in zip(units, accs, cids) for x in group]
    args = [me, bound, total, *blocks, *old, sums]
    return pl.pallas_call(
        functools.partial(finish_kernel, slots, partners, earlier, len(units)),
        out_shape=jax.ShapeDtypeStruct((owners, 1, 2 * round_up(slots, LANES)), f32),
        in_specs=[SMEM] + [VMEM] * (len(args) - 1),
        out_specs=VMEM,
        scratch_shapes=[pltpu.VMEM((padded, width), bf16)],
        compiler_params=pltpu.CompilerParams(vmem_limit_bytes=36 * MIB),
        cost_estimate=pl.CostEstimate(
            flops=2 * owners * slots * padded * width,
            bytes_accessed=2 * owners * slots * width,
            transcendentals=rows,
        ),
        name="finish_rows",
    )(*args)


def restore_kernel(slots, owner_ref, slot_ref, back_ref, best_ref, gap_ref):
    rows = owner_ref.shape[1]
    owners, _, width = back_ref.shape
    half = width // 2
    from_owner = to_bf16(owner_ref[...] == iota((owners, rows), 0))
    from_owner = jnp.concatenate([from_owner] * 3, axis=0)
    at_slot = slot_ref[...] == iota((slots, rows), 0)
    back = jnp.concatenate([back_ref[s] for s in range(owners)], axis=0)
    part0 = back.astype(bf16)
    rest = back - part0.astype(f32)
    part1 = rest.astype(bf16)
    part2 = (rest - part1.astype(f32)).astype(bf16)
    parts = jnp.concatenate([part0, part1, part2], axis=0)
    for i, ref in enumerate((best_ref, gap_ref)):
        table = lax.dot_general(
            parts[:, i * half : i * half + slots],
            from_owner,
            (((0,), (0,)), ((), ())),
            preferred_element_type=f32,
        )
        ref[...] = jnp.sum(jnp.where(at_slot, table, 0.0), axis=0, keepdims=True)


def restore(owner_row, slot_row, back, slots):
    return pl.pallas_call(
        functools.partial(restore_kernel, slots),
        out_shape=(jax.ShapeDtypeStruct(owner_row.shape, f32),) * 2,
        in_specs=[VMEM] * 3,
        out_specs=(VMEM, VMEM),
        compiler_params=pltpu.CompilerParams(vmem_limit_bytes=28 * MIB),
        name="restore_rows",
    )(owner_row, slot_row, back)


def exchange(x):
    return lax.all_to_all(x, "owner", split_axis=0, concat_axis=0, tiled=True)


def swap_together(blocks):
    owners = len(blocks)
    order = jnp.arange(owners, dtype=i32) ^ lax.axis_index("owner").astype(i32)
    arrived = exchange(jnp.stack(blocks)[order])[order]
    return [arrived[r] for r in range(owners)]


def swap_apart(blocks, order):
    owners = len(blocks)
    arrived = list(blocks)
    for i, r in enumerate(order):
        block = blocks[r]
        if i >= FLIGHT:
            before = order[i - FLIGHT]
            block, arrived[before] = lax.optimization_barrier((block, arrived[before]))
        arrived[r] = lax.ppermute(block, "owner", [(s, s ^ r) for s in range(owners)])
    return arrived


def local(embeddings, cluster_ids):
    rows = embeddings.shape[0]
    owners = lax.axis_size("owner")
    clusters = CL_DEV * owners
    row_limit = 2 * rows // clusters
    most = round_up(CL_DEV * row_limit, STEP)
    usual = min(most, round_up(9 * rows // (8 * owners), STEP))
    few = owners <= MAX_PERMUTES
    me = lax.axis_index("owner").astype(i32).reshape(1)
    ids_row = cluster_ids.reshape(1, rows)
    counts, rank = count_rows(ids_row, owners, clusters)
    owner_row, slot_row, bound, total, load = assign(me, exchange(counts), ids_row, rank)

    half = owners // 2
    order = [r for i in reversed(range(half)) for r in (half + i, i)][:-1]
    sent = order + [0]
    seen = [0] + order
    share = owners // 16 if owners >= 16 else 1
    groups, at = [], 0
    for size in (5, 4, 4, 2):
        groups.append(seen[at : at + size * share])
        at += size * share
    groups.append(seen[at:])

    def compare(slots, apart):
        blocks = [None] * owners
        for first in range(0, owners, GROUP):
            partners = tuple(sent[first : first + GROUP])
            packed = pack(me, owner_row, slot_row, embeddings, partners, slots)
            for r, block in zip(partners, packed):
                blocks[r] = block
        arrived = swap_apart(blocks, order) if apart else swap_together(blocks)
        state = ([], [], [], None)
        for group in groups[:-1]:
            state = score(bound, [arrived[r] for r in group], group, state)
        last = groups[-1]
        answers = finish(
            me, bound, total, [arrived[r] for r in last], last, groups[:-1], state
        )
        return restore(owner_row, slot_row, exchange(answers), slots)

    best, gap = compare(usual, few)
    if usual < most:
        best, gap = lax.cond(
            load[0, 0] <= usual, lambda: (best, gap), lambda: compare(most, False)
        )
    return best.reshape(rows), gap.reshape(rows)


def solution(mesh):
    return jax.shard_map(
        local,
        mesh=mesh,
        in_specs=(P(("groups", "owner"), None), P(("groups", "owner"))),
        out_specs=(P(("groups", "owner")), P(("groups", "owner"))),
        check_vma=False,
    )
```

```python
import functools

import jax
import jax.numpy as jnp
from jax import lax
from jax.experimental import pallas as pl
from jax.experimental.pallas import tpu as pltpu
from jax.sharding import PartitionSpec as P

CL_DEV = 4
VARIANTS = 8
STEP = 16
TILE = 256
LANES = 128
GROUP = 4
MAX_PERMUTES = 16
RANKS = 4096
MIB = 1 << 20

epsilon = 1e-06
f32 = jnp.float32
bf16 = jnp.bfloat16
i32 = jnp.int32
VMEM = pl.BlockSpec(memory_space=pltpu.VMEM)
SMEM = pl.BlockSpec(memory_space=pltpu.SMEM)


def iota(shape, axis):
    return lax.broadcasted_iota(i32, shape, axis)


def round_up(value, unit):
    return -(-value // unit) * unit


def nt_dot(a, b):
    return lax.dot_general(a, b, (((1,), (1,)), ((), ())), preferred_element_type=f32)


def mm(a, b):
    return jnp.dot(a, b, preferred_element_type=f32)


def to_bf16(mask):
    return mask.astype(f32).astype(bf16)


def count_kernel(ids_ref, counts_ref, rank_ref):
    rows = ids_ref.shape[1]
    peers, _, clusters = counts_ref.shape
    label = iota((clusters, TILE), 0)
    upto = to_bf16(iota((TILE, TILE), 0) <= iota((TILE, TILE), 1))
    total = jnp.zeros((clusters, 1), f32)
    for b in range(rows // TILE):
        at = slice(b * TILE, (b + 1) * TILE)
        hot = ids_ref[:, at] == label
        prefix = mm(to_bf16(hot), upto)
        rank = jnp.sum(jnp.where(hot, prefix + total - 1.0, 0.0), axis=0, keepdims=True)
        rank_ref[:, at] = ids_ref[:, at] * RANKS + rank.astype(i32)
        total = total + prefix[:, TILE - 1 :]
    square = (clusters, clusters)
    eye = iota(square, 0) == iota(square, 1)
    total_row = jnp.sum(jnp.where(eye, total, 0.0), axis=0, keepdims=True).astype(i32)
    for peer in range(peers):
        counts_ref[peer] = total_row


def count_rows(ids_row, peers, clusters):
    return pl.pallas_call(
        count_kernel,
        out_shape=(
            jax.ShapeDtypeStruct((peers, 1, clusters), i32),
            jax.ShapeDtypeStruct(ids_row.shape, i32),
        ),
        in_specs=[VMEM],
        out_specs=(VMEM, VMEM),
        compiler_params=pltpu.CompilerParams(vmem_limit_bytes=16 * MIB),
        name="count_rows",
    )(ids_row)


def assign_kernel(
    me_ref, counts_ref, rank_ref, owner_ref, slot_ref, bound_ref, total_ref, load_ref
):
    far, near, clusters = counts_ref.shape
    owners = far * near
    rows = rank_ref.shape[1]
    shift = owners.bit_length() - 1
    me = me_ref[0]
    count = jnp.concatenate([counts_ref[s].astype(f32) for s in range(far)], axis=0)
    count16 = count.astype(bf16)
    square = (clusters, clusters)
    sub, lane = iota(square, 0), iota(square, 1)
    total_row = jnp.sum(count, axis=0, keepdims=True)
    total_col = jnp.sum(jnp.where(sub == lane, total_row, 0.0), axis=1, keepdims=True)
    tie = total_row == total_col
    outranks_col = (total_row > total_col) | (tie & (lane < sub))
    outranks_row = (total_col > total_row) | (tie & (sub < lane))
    rank_col = jnp.sum(outranks_col.astype(f32), axis=1, keepdims=True).astype(i32)
    rank_row = jnp.sum(outranks_row.astype(f32), axis=0, keepdims=True).astype(i32)

    def owner_of(rank, variant):
        layer = rank >> shift
        within = rank & (owners - 1)
        flip = jnp.zeros_like(variant)
        for p in range(1, CL_DEV):
            flip = flip + jnp.where(layer == p, (variant >> (p - 1)) & 1, 0)
        within = within ^ flip
        return jnp.where((layer & 1) == 1, owners - 1 - within, within)

    wide = (clusters, VARIANTS * owners)
    variant = iota(wide, 1) >> shift
    tried = owner_of(rank_col, variant) == (iota(wide, 1) & (owners - 1))
    load = jnp.max(mm(count16, to_bf16(tried)), axis=0, keepdims=True)
    by_variant = (VARIANTS, VARIANTS * owners)
    worst = jnp.max(
        jnp.where((iota(by_variant, 1) >> shift) == iota(by_variant, 0), load, 0.0),
        axis=1,
        keepdims=True,
    )
    best = jnp.min(worst, axis=0, keepdims=True)
    chosen = jnp.min(
        jnp.where(worst == best, iota((VARIANTS, 1), 0), VARIANTS), axis=0, keepdims=True
    )
    owner_col = owner_of(rank_col, chosen + jnp.zeros_like(rank_col))
    owner_row = owner_of(rank_row, chosen + jnp.zeros_like(rank_row))
    layer_col, layer_row = rank_col >> shift, rank_row >> shift
    load_ref[...] = jnp.broadcast_to(best, load_ref.shape).astype(i32)

    mine = jnp.sum(jnp.where(iota(count.shape, 0) == me, count, 0.0), axis=0, keepdims=True)
    earlier = (owner_row == owner_col) & (layer_row < layer_col)
    offset_col = jnp.sum(jnp.where(earlier, mine, 0.0), axis=1, keepdims=True)
    ids = rank_ref[...] // RANKS
    hot = ids == iota((clusters, rows), 0)
    owner_ref[...] = jnp.sum(
        jnp.where(hot, owner_col.astype(f32), 0.0), axis=0, keepdims=True
    ).astype(i32)
    slot_ref[...] = (
        jnp.sum(jnp.where(hot, offset_col, 0.0), axis=0, keepdims=True)
    ).astype(i32) + (rank_ref[...] & (RANKS - 1))

    select = (owner_col == me) & (layer_col <= iota((clusters, LANES), 1))
    turn = iota((owners, owners), 1) == (iota((owners, owners), 0) ^ me)
    turned = mm(to_bf16(turn), count16).astype(bf16)
    bound_ref[...] = mm(turned, to_bf16(select))
    own = (owner_row == me) & (layer_row == iota((8, clusters), 0))
    total_ref[...] = jnp.broadcast_to(
        jnp.sum(jnp.where(own, total_row, 0.0), axis=1, keepdims=True), total_ref.shape
    )


def assign(me, counts, rank):
    far, near, clusters = counts.shape
    owners, rows = far * near, rank.shape[1]
    return pl.pallas_call(
        assign_kernel,
        out_shape=(
            jax.ShapeDtypeStruct((1, rows), i32),
            jax.ShapeDtypeStruct((1, rows), i32),
            jax.ShapeDtypeStruct((owners, LANES), f32),
            jax.ShapeDtypeStruct((8, LANES), f32),
            jax.ShapeDtypeStruct((1, LANES), i32),
        ),
        in_specs=[SMEM, VMEM, VMEM],
        out_specs=(VMEM,) * 5,
        compiler_params=pltpu.CompilerParams(vmem_limit_bytes=16 * MIB),
        name="assign",
    )(me, counts, rank)


def pack_kernel(slots, partners, me_ref, owner_ref, slot_ref, rows_ref, *out_refs):
    rows = rows_ref.shape[0]
    me = me_ref[0]
    slot = iota((slots, rows), 0)
    takes = []
    for partner in partners:
        key = jnp.where(owner_ref[...] == (me ^ partner), slot_ref[...], -1)
        takes.append(to_bf16(slot == key))
    picked = mm(jnp.concatenate(takes, axis=0), rows_ref[...]).astype(bf16)
    for i, ref in enumerate(out_refs):
        ref[...] = picked[i * slots : (i + 1) * slots]


def pack(me, owner_row, slot_row, unit, partners, slots):
    rows, width = unit.shape
    flops = 2 * len(partners) * slots * rows * width
    return pl.pallas_call(
        functools.partial(pack_kernel, slots, partners),
        out_shape=(jax.ShapeDtypeStruct((slots, width), bf16),) * len(partners),
        in_specs=[SMEM, VMEM, VMEM, VMEM],
        out_specs=(VMEM,) * len(partners),
        compiler_params=pltpu.CompilerParams(vmem_limit_bytes=28 * MIB),
        cost_estimate=pl.CostEstimate(
            flops=flops, bytes_accessed=2 * rows * width, transcendentals=0
        ),
        name="pack_rows",
    )(me, owner_row, slot_row, unit)


def unit_kernel(rows_ref, unit_ref):
    def body(b, carry):
        at = pl.ds(pl.multiple_of(b * TILE, TILE), TILE)
        x = rows_ref[at, :].astype(f32)
        scale = lax.rsqrt(jnp.sum(x * x, axis=1, keepdims=True) + epsilon)
        unit_ref[at, :] = (x * scale).astype(bf16)
        return carry

    lax.fori_loop(0, rows_ref.shape[0] // TILE, body, 0)


def unit_rows(embeddings):
    rows, width = embeddings.shape
    return pl.pallas_call(
        unit_kernel,
        out_shape=jax.ShapeDtypeStruct((rows, width), bf16),
        in_specs=[VMEM],
        out_specs=VMEM,
        compiler_params=pltpu.CompilerParams(vmem_limit_bytes=16 * MIB),
        cost_estimate=pl.CostEstimate(
            flops=8 * rows * width, bytes_accessed=4 * rows * width, transcendentals=rows
        ),
        name="unit_rows",
    )(embeddings)


def cluster_lanes(bound_ref, partners, slots, width):
    lane = iota((1, width), 1).astype(f32)
    result = jnp.where(lane < len(partners) * slots, 0.0, -1.0)
    for i, r in enumerate(partners):
        for k in range(CL_DEV):
            first = bound_ref[r : r + 1, k : k + 1] + float(i * slots)
            result = result + ((lane >= first) & (lane < float((i + 1) * slots))).astype(f32)
    return result


def cluster_rows(bound_ref, r, slots):
    slot = iota((slots, LANES), 0).astype(f32)
    result = jnp.zeros((slots, LANES), f32)
    for k in range(CL_DEV):
        result = result + (slot >= bound_ref[r : r + 1, k : k + 1]).astype(f32)
    return result


def score_group(new_ref, new_cids, olds, cid_row, slots_new):
    padded = new_ref.shape[0]
    groups = padded // LANES
    new = new_ref[...]

    def folded(scores, cids, skip_same):
        rows = scores.shape[0]
        row = iota((rows, LANES), 0)
        lane = iota((rows, LANES), 1)
        best, cols = None, []
        for g in range(groups):
            at = slice(g * LANES, (g + 1) * LANES)
            allowed = cids == cid_row[:, at]
            if skip_same:
                allowed = allowed & (row != lane + g * LANES)
            part = jnp.where(allowed, scores[:, at], -1.0)
            best = part if best is None else jnp.maximum(best, part)
            cols.append(jnp.max(part, axis=0, keepdims=True))
        return best, cols

    columns = None
    results = []
    for unit_ref, acc_ref, cid_ref in olds:
        scores = nt_dot(unit_ref[...], new)
        best, cols = folded(scores, cid_ref[...], False)
        columns = cols if columns is None else [jnp.maximum(a, b) for a, b in zip(columns, cols)]
        results.append((scores, jnp.maximum(acc_ref[...], best)))
    scores = nt_dot(new[0:slots_new], new)
    best, _ = folded(scores, new_cids, True)
    if columns is not None:
        row = iota((slots_new, LANES), 0)
        lane = iota((slots_new, LANES), 1)
        for g, col in enumerate(columns):
            best = jnp.maximum(best, jnp.where(row == lane + g * LANES, col, -1.0))
    results.append((scores, best))
    return results


def member_sums(cid_row, new):
    hot = to_bf16(cid_row == iota((8, cid_row.shape[1]), 0).astype(f32))
    return mm(hot, new)


def score_kernel(slots, partners, olds, bound_ref, *refs):
    fresh = len(partners)
    raw_refs, refs = refs[:fresh], refs[fresh:]
    old_refs = [refs[3 * i : 3 * i + 3] for i in range(olds)]
    refs = refs[3 * olds :]
    if olds:
        sums_ref, refs = refs[0], refs[1:]
    unit_ref, acc_ref, cid_ref, sums_out = refs[:4]
    old_accs = refs[4 : 4 + olds]
    new_ref = refs[4 + olds]
    rows = fresh * slots
    for i, r in enumerate(partners):
        at = slice(i * slots, (i + 1) * slots)
        new_ref[at, :] = raw_refs[i][...]
        cid_ref[at, :] = cluster_rows(bound_ref, r, slots)
    padded = new_ref.shape[0]
    if padded > rows:
        new_ref[rows:, :] = jnp.zeros((padded - rows, new_ref.shape[1]), bf16)
    unit_ref[...] = new_ref[0:rows, :]
    cid_row = cluster_lanes(bound_ref, partners, slots, padded)
    results = score_group(new_ref, cid_ref[...], old_refs, cid_row, rows)
    for (_, best), ref in zip(results, list(old_accs) + [acc_ref]):
        ref[...] = best
    sums = member_sums(cid_row, new_ref[...])
    sums_out[...] = sums + sums_ref[...] if olds else sums


def score(bound, blocks, partners, state):
    slots, width = blocks[0].shape
    units, accs, cids, sums = state
    rows = len(blocks) * slots
    padded = round_up(rows, LANES)
    old = [x for group in zip(units, accs, cids) for x in group]
    old_rows = sum(u.shape[0] for u in units)
    acc_shapes = [jax.ShapeDtypeStruct(a.shape, f32) for a in accs]
    out_shape = (
        jax.ShapeDtypeStruct((rows, width), bf16),
        jax.ShapeDtypeStruct((rows, LANES), f32),
        jax.ShapeDtypeStruct((rows, LANES), f32),
        jax.ShapeDtypeStruct((8, width), f32),
        *acc_shapes,
    )
    args = [bound, *blocks, *old] + ([sums] if units else [])
    out = pl.pallas_call(
        functools.partial(score_kernel, slots, partners, len(units)),
        out_shape=out_shape,
        in_specs=[VMEM] * len(args),
        out_specs=(VMEM,) * len(out_shape),
        scratch_shapes=[pltpu.VMEM((padded, width), bf16)],
        compiler_params=pltpu.CompilerParams(vmem_limit_bytes=36 * MIB),
        cost_estimate=pl.CostEstimate(
            flops=2 * (old_rows + rows) * padded * width,
            bytes_accessed=2 * (old_rows + rows) * width,
            transcendentals=rows,
        ),
        name="score_rows",
    )(*args)
    return units + [out[0]], list(out[4:]) + [out[1]], cids + [out[2]], out[3]


def finish_kernel(slots, partners, earlier, olds, me_ref, bound_ref, total_ref, *refs):
    fresh = len(partners)
    raw_refs, refs = refs[:fresh], refs[fresh:]
    old_refs = [refs[3 * i : 3 * i + 3] for i in range(olds)]
    sums_ref, out_ref, new_ref = refs[3 * olds :]
    me = me_ref[0]
    rows = fresh * slots
    padded, width = new_ref.shape
    new_ref[rows:, :] = jnp.zeros((padded - rows, width), bf16)
    pieces = []
    for i, r in enumerate(partners):
        new_ref[i * slots : (i + 1) * slots, :] = raw_refs[i][...]
        pieces.append(cluster_rows(bound_ref, r, slots))
    new_cids = jnp.concatenate(pieces, axis=0)
    cid_row = cluster_lanes(bound_ref, partners, slots, padded)
    sums = sums_ref[...] + member_sums(cid_row, new_ref[...])
    centroid = (sums / jnp.maximum(total_ref[:, 0:1], 1.0)).astype(bf16)
    centroid = jnp.concatenate([centroid, jnp.zeros_like(centroid)], axis=0)
    new_ref[rows : rows + STEP, :] = centroid
    results = score_group(new_ref, new_cids, old_refs, cid_row, rows)
    half = out_ref.shape[2] // 2
    group, within = rows // LANES, rows % LANES
    eye = iota((slots, half), 0) == iota((slots, half), 1)
    all_cids = [old[2][...] for old in old_refs] + [new_cids]
    for (scores, acc), cids, names in zip(results, all_cids, earlier + [partners]):
        best = jnp.max(acc, axis=1, keepdims=True)
        lane = iota(cids.shape, 1).astype(f32)
        dots = scores[:, group * LANES : (group + 1) * LANES]
        gap = 1.0 - jnp.sum(
            jnp.where(lane == cids + float(within), dots, 0.0), axis=1, keepdims=True
        )
        for i, r in enumerate(names):
            at = slice(i * slots, (i + 1) * slots)
            for j, col in enumerate((best, gap)):
                line = jnp.sum(jnp.where(eye, col[at], 0.0), axis=0, keepdims=True)
                out_ref[r ^ me, :, j * half : (j + 1) * half] = line


def finish(me, bound, total, blocks, partners, earlier, state):
    slots, width = blocks[0].shape
    owners = bound.shape[0]
    units, accs, cids, sums = state
    rows = len(blocks) * slots
    padded = round_up(rows + STEP, LANES)
    old = [x for group in zip(units, accs, cids) for x in group]
    args = [me, bound, total, *blocks, *old, sums]
    return pl.pallas_call(
        functools.partial(finish_kernel, slots, partners, earlier, len(units)),
        out_shape=jax.ShapeDtypeStruct((owners, 1, 2 * round_up(slots, LANES)), f32),
        in_specs=[SMEM] + [VMEM] * (len(args) - 1),
        out_specs=VMEM,
        scratch_shapes=[pltpu.VMEM((padded, width), bf16)],
        compiler_params=pltpu.CompilerParams(vmem_limit_bytes=36 * MIB),
        cost_estimate=pl.CostEstimate(
            flops=2 * owners * slots * padded * width,
            bytes_accessed=2 * owners * slots * width,
            transcendentals=rows,
        ),
        name="finish_rows",
    )(*args)


def restore_kernel(slots, owner_ref, slot_ref, back_ref, best_ref, gap_ref):
    rows = owner_ref.shape[1]
    owners, _, width = back_ref.shape
    half = width // 2
    from_owner = to_bf16(owner_ref[...] == iota((owners, rows), 0))
    from_owner = jnp.concatenate([from_owner] * 3, axis=0)
    at_slot = slot_ref[...] == iota((slots, rows), 0)
    back = jnp.concatenate([back_ref[s] for s in range(owners)], axis=0)
    part0 = back.astype(bf16)
    rest = back - part0.astype(f32)
    part1 = rest.astype(bf16)
    part2 = (rest - part1.astype(f32)).astype(bf16)
    parts = jnp.concatenate([part0, part1, part2], axis=0)
    for i, ref in enumerate((best_ref, gap_ref)):
        table = lax.dot_general(
            parts[:, i * half : i * half + slots],
            from_owner,
            (((0,), (0,)), ((), ())),
            preferred_element_type=f32,
        )
        ref[...] = jnp.sum(jnp.where(at_slot, table, 0.0), axis=0, keepdims=True)


def restore(owner_row, slot_row, back, slots):
    return pl.pallas_call(
        functools.partial(restore_kernel, slots),
        out_shape=(jax.ShapeDtypeStruct(owner_row.shape, f32),) * 2,
        in_specs=[VMEM] * 3,
        out_specs=(VMEM, VMEM),
        compiler_params=pltpu.CompilerParams(vmem_limit_bytes=28 * MIB),
        name="restore_rows",
    )(owner_row, slot_row, back)


def exchange(x):
    return lax.all_to_all(x, "owner", split_axis=0, concat_axis=0, tiled=True)


def swap_together(blocks):
    owners = len(blocks)
    order = jnp.arange(owners, dtype=i32) ^ lax.axis_index("owner").astype(i32)
    arrived = exchange(jnp.stack(blocks)[order])[order]
    return [arrived[r] for r in range(owners)]


def swap_apart(blocks):
    pairs = [[(s, s ^ r) for s in range(len(blocks))] for r in range(len(blocks))]
    return blocks[:1] + [
        lax.ppermute(block, "owner", pair) for block, pair in zip(blocks[1:], pairs[1:])
    ]


def gather_counts(counts, owners):
    near, _, clusters = counts.shape
    far = owners // near
    close = [[f * near + n for n in range(near)] for f in range(far)]
    apart = [[f * near + n for f in range(far)] for n in range(near)]
    seen = lax.all_to_all(counts, "owner", 0, 0, axis_index_groups=close, tiled=True)
    seen = jnp.broadcast_to(seen.reshape(1, near, clusters), (far, near, clusters))
    return lax.all_to_all(seen, "owner", 0, 0, axis_index_groups=apart, tiled=True)


def local(embeddings, cluster_ids):
    rows = embeddings.shape[0]
    owners = lax.axis_size("owner")
    clusters = CL_DEV * owners
    row_limit = 2 * rows // clusters
    most = round_up(CL_DEV * row_limit, STEP)
    usual = min(most, round_up(9 * rows // (8 * owners), STEP))
    few = owners <= MAX_PERMUTES
    me = lax.axis_index("owner").astype(i32).reshape(1)
    ids_row = cluster_ids.reshape(1, rows)
    peers = 1 << ((owners.bit_length() - 1) // 2)
    counts, rank = count_rows(ids_row, peers, clusters)
    unit = unit_rows(embeddings)
    counts = gather_counts(counts, owners)
    owner_row, slot_row, bound, total, load = assign(me, counts, rank)

    half = owners // 2
    far = list(range(owners - 1, half - 1, -1))
    near = list(range(half - 1, 0, -1))
    sent = far[:2] + [r for pair in zip(far[2:-1], near) for r in pair]
    sent = sent + near[len(far) - 3 :] + far[-1:]
    seen = [0] + sent
    sent = sent + [0]
    packs = [tuple(sent[:2]), tuple(sent[2:4])]
    packs += [tuple(sent[i : i + GROUP]) for i in range(4, owners, GROUP)]
    share = owners // 16 if owners >= 16 else 1
    groups, at = [], 0
    for size in (5, 4, 4, 2):
        groups.append(seen[at : at + size * share])
        at += size * share
    groups.append(seen[at:])

    def compare(slots, apart):
        blocks = [None] * owners
        slot_in = slot_row
        for partners in packs:
            packed = pack(me, owner_row, slot_in, unit, partners, slots)
            slot_in, *packed = lax.optimization_barrier((slot_in, *packed))
            for r, block in zip(partners, packed):
                blocks[r] = block
        arrived = swap_apart(blocks) if apart else swap_together(blocks)
        state = ([], [], [], None)
        for group in groups[:-1]:
            state = score(bound, [arrived[r] for r in group], group, state)
        last = groups[-1]
        answers = finish(
            me, bound, total, [arrived[r] for r in last], last, groups[:-1], state
        )
        return restore(owner_row, slot_row, exchange(answers), slots)

    best, gap = compare(usual, few)
    if usual < most:
        best, gap = lax.cond(
            load[0, 0] <= usual, lambda: (best, gap), lambda: compare(most, False)
        )
    return best.reshape(rows), gap.reshape(rows)


def solution(mesh):
    return jax.shard_map(
        local,
        mesh=mesh,
        in_specs=(P(("groups", "owner"), None), P(("groups", "owner"))),
        out_specs=(P(("groups", "owner")), P(("groups", "owner"))),
        check_vma=False,
    )
```

```python
import functools

import jax
import jax.numpy as jnp
from jax import lax
from jax.experimental import pallas as pl
from jax.experimental.pallas import tpu as pltpu
from jax.sharding import PartitionSpec as P

CL_DEV = 4
VARIANTS = 8
STEP = 16
TILE = 256
LANES = 128
MAX_PERMUTES = 16
RANKS = 4096
MIB = 1 << 20

epsilon = 1e-06
f32 = jnp.float32
bf16 = jnp.bfloat16
i32 = jnp.int32
VMEM = pl.BlockSpec(memory_space=pltpu.VMEM)
SMEM = pl.BlockSpec(memory_space=pltpu.SMEM)


def iota(shape, axis):
    return lax.broadcasted_iota(i32, shape, axis)


def round_up(value, unit):
    return -(-value // unit) * unit


def nt_dot(a, b):
    return lax.dot_general(a, b, (((1,), (1,)), ((), ())), preferred_element_type=f32)


def mm(a, b):
    return jnp.dot(a, b, preferred_element_type=f32)


def to_bf16(mask):
    return mask.astype(f32).astype(bf16)


def count_kernel(ids_ref, counts_ref, rank_ref):
    rows = ids_ref.shape[1]
    peers, _, clusters = counts_ref.shape
    label = iota((clusters, TILE), 0)
    upto = to_bf16(iota((TILE, TILE), 0) <= iota((TILE, TILE), 1))
    total = jnp.zeros((clusters, 1), f32)
    for b in range(rows // TILE):
        at = slice(b * TILE, (b + 1) * TILE)
        hot = ids_ref[:, at] == label
        prefix = mm(to_bf16(hot), upto)
        rank = jnp.sum(jnp.where(hot, prefix + total - 1.0, 0.0), axis=0, keepdims=True)
        rank_ref[:, at] = ids_ref[:, at] * RANKS + rank.astype(i32)
        total = total + prefix[:, TILE - 1 :]
    square = (clusters, clusters)
    eye = iota(square, 0) == iota(square, 1)
    total_row = jnp.sum(jnp.where(eye, total, 0.0), axis=0, keepdims=True).astype(i32)
    for peer in range(peers):
        counts_ref[peer] = total_row


def count_rows(ids_row, peers, clusters):
    return pl.pallas_call(
        count_kernel,
        out_shape=(
            jax.ShapeDtypeStruct((peers, 1, clusters), i32),
            jax.ShapeDtypeStruct(ids_row.shape, i32),
        ),
        in_specs=[VMEM],
        out_specs=(VMEM, VMEM),
        compiler_params=pltpu.CompilerParams(vmem_limit_bytes=16 * MIB),
        name="count_rows",
    )(ids_row)


def assign_kernel(
    me_ref, counts_ref, rank_ref, owner_ref, slot_ref, bound_ref, total_ref, load_ref
):
    owners, _, clusters = counts_ref.shape
    rows = rank_ref.shape[1]
    shift = owners.bit_length() - 1
    me = me_ref[0]
    count = jnp.concatenate([counts_ref[s].astype(f32) for s in range(owners)], axis=0)
    count16 = count.astype(bf16)
    square = (clusters, clusters)
    sub, lane = iota(square, 0), iota(square, 1)
    total_row = jnp.sum(count, axis=0, keepdims=True)
    total_col = jnp.sum(jnp.where(sub == lane, total_row, 0.0), axis=1, keepdims=True)
    tie = total_row == total_col
    outranks_col = (total_row > total_col) | (tie & (lane < sub))
    outranks_row = (total_col > total_row) | (tie & (sub < lane))
    rank_col = jnp.sum(outranks_col.astype(f32), axis=1, keepdims=True).astype(i32)
    rank_row = jnp.sum(outranks_row.astype(f32), axis=0, keepdims=True).astype(i32)

    def owner_of(rank, variant):
        layer = rank >> shift
        within = rank & (owners - 1)
        flip = jnp.zeros_like(variant)
        for p in range(1, CL_DEV):
            flip = flip + jnp.where(layer == p, (variant >> (p - 1)) & 1, 0)
        within = within ^ flip
        return jnp.where((layer & 1) == 1, owners - 1 - within, within)

    wide = (clusters, VARIANTS * owners)
    variant = iota(wide, 1) >> shift
    tried = owner_of(rank_col, variant) == (iota(wide, 1) & (owners - 1))
    load = jnp.max(mm(count16, to_bf16(tried)), axis=0, keepdims=True)
    by_variant = (VARIANTS, VARIANTS * owners)
    worst = jnp.max(
        jnp.where((iota(by_variant, 1) >> shift) == iota(by_variant, 0), load, 0.0),
        axis=1,
        keepdims=True,
    )
    best = jnp.min(worst, axis=0, keepdims=True)
    chosen = jnp.min(
        jnp.where(worst == best, iota((VARIANTS, 1), 0), VARIANTS), axis=0, keepdims=True
    )
    owner_col = owner_of(rank_col, chosen + jnp.zeros_like(rank_col))
    owner_row = owner_of(rank_row, chosen + jnp.zeros_like(rank_row))
    layer_col, layer_row = rank_col >> shift, rank_row >> shift
    load_ref[...] = jnp.broadcast_to(best, load_ref.shape).astype(i32)

    mine = jnp.sum(jnp.where(iota(count.shape, 0) == me, count, 0.0), axis=0, keepdims=True)
    earlier = (owner_row == owner_col) & (layer_row < layer_col)
    offset_col = jnp.sum(jnp.where(earlier, mine, 0.0), axis=1, keepdims=True)
    ids = rank_ref[...] // RANKS
    hot = ids == iota((clusters, rows), 0)
    owner_ref[...] = jnp.sum(
        jnp.where(hot, owner_col.astype(f32), 0.0), axis=0, keepdims=True
    ).astype(i32)
    slot_ref[...] = (
        jnp.sum(jnp.where(hot, offset_col, 0.0), axis=0, keepdims=True)
    ).astype(i32) + (rank_ref[...] & (RANKS - 1))

    select = (owner_col == me) & (layer_col <= iota((clusters, LANES), 1))
    turn = iota((owners, owners), 1) == (iota((owners, owners), 0) ^ me)
    turned = mm(to_bf16(turn), count16).astype(bf16)
    bound_ref[...] = mm(turned, to_bf16(select))
    own = (owner_row == me) & (layer_row == iota((8, clusters), 0))
    total_ref[...] = jnp.broadcast_to(
        jnp.sum(jnp.where(own, total_row, 0.0), axis=1, keepdims=True), total_ref.shape
    )


def assign(me, counts, rank):
    owners, _, clusters = counts.shape
    rows = rank.shape[1]
    return pl.pallas_call(
        assign_kernel,
        out_shape=(
            jax.ShapeDtypeStruct((1, rows), i32),
            jax.ShapeDtypeStruct((1, rows), i32),
            jax.ShapeDtypeStruct((owners, LANES), f32),
            jax.ShapeDtypeStruct((8, LANES), f32),
            jax.ShapeDtypeStruct((1, LANES), i32),
        ),
        in_specs=[SMEM, VMEM, VMEM],
        out_specs=(VMEM,) * 5,
        compiler_params=pltpu.CompilerParams(vmem_limit_bytes=16 * MIB),
        name="assign",
    )(me, counts, rank)


def pack_kernel(slots, partners, me_ref, owner_ref, slot_ref, rows_ref, *out_refs):
    rows = rows_ref.shape[0]
    me = me_ref[0]
    slot = iota((slots, rows), 0)
    takes = []
    for partner in partners:
        key = jnp.where(owner_ref[...] == (me ^ partner), slot_ref[...], -1)
        takes.append(to_bf16(slot == key))
    picked = mm(jnp.concatenate(takes, axis=0), rows_ref[...]).astype(bf16)
    for i, r in enumerate(partners):
        block = picked[i * slots : (i + 1) * slots]
        if len(out_refs) == 1:
            out_refs[0][(r ^ me) & (len(partners) - 1)] = block
        else:
            out_refs[i][...] = block


def pack(me, owner_row, slot_row, unit, partners, slots, stacked):
    rows, width = unit.shape
    flops = 2 * len(partners) * slots * rows * width
    if stacked:
        out_shape = (jax.ShapeDtypeStruct((len(partners), slots, width), bf16),)
    else:
        out_shape = (jax.ShapeDtypeStruct((slots, width), bf16),) * len(partners)
    return pl.pallas_call(
        functools.partial(pack_kernel, slots, partners),
        out_shape=out_shape,
        in_specs=[SMEM, VMEM, VMEM, VMEM],
        out_specs=(VMEM,) * len(out_shape),
        compiler_params=pltpu.CompilerParams(vmem_limit_bytes=40 * MIB),
        cost_estimate=pl.CostEstimate(
            flops=flops, bytes_accessed=2 * rows * width, transcendentals=0
        ),
        name="pack_rows",
    )(me, owner_row, slot_row, unit)


def unit_kernel(rows_ref, unit_ref):
    def body(b, carry):
        at = pl.ds(pl.multiple_of(b * TILE, TILE), TILE)
        x = rows_ref[at, :].astype(f32)
        scale = lax.rsqrt(jnp.sum(x * x, axis=1, keepdims=True) + epsilon)
        unit_ref[at, :] = (x * scale).astype(bf16)
        return carry

    lax.fori_loop(0, rows_ref.shape[0] // TILE, body, 0)


def unit_rows(embeddings):
    rows, width = embeddings.shape
    return pl.pallas_call(
        unit_kernel,
        out_shape=jax.ShapeDtypeStruct((rows, width), bf16),
        in_specs=[VMEM],
        out_specs=VMEM,
        compiler_params=pltpu.CompilerParams(vmem_limit_bytes=16 * MIB),
        cost_estimate=pl.CostEstimate(
            flops=8 * rows * width, bytes_accessed=4 * rows * width, transcendentals=rows
        ),
        name="unit_rows",
    )(embeddings)


def cluster_lanes(bound_ref, partners, slots, width):
    lane = iota((1, width), 1).astype(f32)
    result = jnp.where(lane < len(partners) * slots, 0.0, -1.0)
    for i, r in enumerate(partners):
        for k in range(CL_DEV):
            first = bound_ref[r : r + 1, k : k + 1] + float(i * slots)
            result = result + ((lane >= first) & (lane < float((i + 1) * slots))).astype(f32)
    return result


def cluster_rows(bound_ref, r, slots):
    slot = iota((slots, LANES), 0).astype(f32)
    result = jnp.zeros((slots, LANES), f32)
    for k in range(CL_DEV):
        result = result + (slot >= bound_ref[r : r + 1, k : k + 1]).astype(f32)
    return result


def score_group(new_ref, new_cids, olds, cid_row, slots_new):
    padded = new_ref.shape[0]
    groups = padded // LANES
    new = new_ref[...]

    def folded(scores, cids, skip_same):
        rows = scores.shape[0]
        row = iota((rows, LANES), 0)
        lane = iota((rows, LANES), 1)
        best, cols = None, []
        for g in range(groups):
            at = slice(g * LANES, (g + 1) * LANES)
            allowed = cids == cid_row[:, at]
            if skip_same:
                allowed = allowed & (row != lane + g * LANES)
            part = jnp.where(allowed, scores[:, at], -1.0)
            best = part if best is None else jnp.maximum(best, part)
            cols.append(jnp.max(part, axis=0, keepdims=True))
        return best, cols

    columns = None
    results = []
    for unit_ref, acc_ref, cid_ref in olds:
        scores = nt_dot(unit_ref[...], new)
        best, cols = folded(scores, cid_ref[...], False)
        columns = cols if columns is None else [jnp.maximum(a, b) for a, b in zip(columns, cols)]
        results.append((scores, jnp.maximum(acc_ref[...], best)))
    scores = nt_dot(new[0:slots_new], new)
    best, _ = folded(scores, new_cids, True)
    if columns is not None:
        row = iota((slots_new, LANES), 0)
        lane = iota((slots_new, LANES), 1)
        for g, col in enumerate(columns):
            best = jnp.maximum(best, jnp.where(row == lane + g * LANES, col, -1.0))
    results.append((scores, best))
    return results


def member_sums(cid_row, new):
    hot = to_bf16(cid_row == iota((8, cid_row.shape[1]), 0).astype(f32))
    return mm(hot, new)


def score_kernel(slots, partners, olds, me_ref, bound_ref, *refs):
    fresh = len(partners)
    if olds:
        raw_refs, refs = refs[:fresh], refs[fresh:]
    else:
        stack_ref, refs = refs[0], refs[1:]
        raw_refs = [stack_ref.at[(r ^ me_ref[0]) & (fresh - 1)] for r in partners]
    old_refs = [refs[3 * i : 3 * i + 3] for i in range(olds)]
    refs = refs[3 * olds :]
    if olds:
        sums_ref, refs = refs[0], refs[1:]
    unit_ref, acc_ref, cid_ref, sums_out = refs[:4]
    old_accs = refs[4 : 4 + olds]
    new_ref = refs[4 + olds]
    rows = fresh * slots
    for i, r in enumerate(partners):
        at = slice(i * slots, (i + 1) * slots)
        new_ref[at, :] = raw_refs[i][...]
        cid_ref[at, :] = cluster_rows(bound_ref, r, slots)
    padded = new_ref.shape[0]
    if padded > rows:
        new_ref[rows:, :] = jnp.zeros((padded - rows, new_ref.shape[1]), bf16)
    unit_ref[...] = new_ref[0:rows, :]
    cid_row = cluster_lanes(bound_ref, partners, slots, padded)
    results = score_group(new_ref, cid_ref[...], old_refs, cid_row, rows)
    for (_, best), ref in zip(results, list(old_accs) + [acc_ref]):
        ref[...] = best
    sums = member_sums(cid_row, new_ref[...])
    sums_out[...] = sums + sums_ref[...] if olds else sums


def score(me, bound, blocks, partners, state):
    slots, width = blocks[0].shape[-2:]
    units, accs, cids, sums = state
    rows = len(partners) * slots
    padded = round_up(rows, LANES)
    old = [x for group in zip(units, accs, cids) for x in group]
    old_rows = sum(u.shape[0] for u in units)
    acc_shapes = [jax.ShapeDtypeStruct(a.shape, f32) for a in accs]
    out_shape = (
        jax.ShapeDtypeStruct((rows, width), bf16),
        jax.ShapeDtypeStruct((rows, LANES), f32),
        jax.ShapeDtypeStruct((rows, LANES), f32),
        jax.ShapeDtypeStruct((8, width), f32),
        *acc_shapes,
    )
    args = [me, bound, *blocks, *old] + ([sums] if units else [])
    out = pl.pallas_call(
        functools.partial(score_kernel, slots, partners, len(units)),
        out_shape=out_shape,
        in_specs=[SMEM] + [VMEM] * (len(args) - 1),
        out_specs=(VMEM,) * len(out_shape),
        scratch_shapes=[pltpu.VMEM((padded, width), bf16)],
        compiler_params=pltpu.CompilerParams(vmem_limit_bytes=36 * MIB),
        cost_estimate=pl.CostEstimate(
            flops=2 * (old_rows + rows) * padded * width,
            bytes_accessed=2 * (old_rows + rows) * width,
            transcendentals=rows,
        ),
        name="score_rows",
    )(*args)
    return units + [out[0]], list(out[4:]) + [out[1]], cids + [out[2]], out[3]


def finish_kernel(slots, partners, earlier, olds, me_ref, bound_ref, total_ref, *refs):
    fresh = len(partners)
    raw_refs, refs = refs[:fresh], refs[fresh:]
    old_refs = [refs[3 * i : 3 * i + 3] for i in range(olds)]
    sums_ref, out_ref, new_ref = refs[3 * olds :]
    me = me_ref[0]
    rows = fresh * slots
    padded, width = new_ref.shape
    new_ref[rows:, :] = jnp.zeros((padded - rows, width), bf16)
    pieces = []
    for i, r in enumerate(partners):
        new_ref[i * slots : (i + 1) * slots, :] = raw_refs[i][...]
        pieces.append(cluster_rows(bound_ref, r, slots))
    new_cids = jnp.concatenate(pieces, axis=0)
    cid_row = cluster_lanes(bound_ref, partners, slots, padded)
    sums = sums_ref[...] + member_sums(cid_row, new_ref[...])
    centroid = (sums / jnp.maximum(total_ref[:, 0:1], 1.0)).astype(bf16)
    centroid = jnp.concatenate([centroid, jnp.zeros_like(centroid)], axis=0)
    new_ref[rows : rows + STEP, :] = centroid
    results = score_group(new_ref, new_cids, old_refs, cid_row, rows)
    half = out_ref.shape[2] // 2
    group, within = rows // LANES, rows % LANES
    eye = iota((slots, half), 0) == iota((slots, half), 1)
    all_cids = [old[2][...] for old in old_refs] + [new_cids]
    for (scores, acc), cids, names in zip(results, all_cids, earlier + [partners]):
        best = jnp.max(acc, axis=1, keepdims=True)
        lane = iota(cids.shape, 1).astype(f32)
        dots = scores[:, group * LANES : (group + 1) * LANES]
        gap = 1.0 - jnp.sum(
            jnp.where(lane == cids + float(within), dots, 0.0), axis=1, keepdims=True
        )
        for i, r in enumerate(names):
            at = slice(i * slots, (i + 1) * slots)
            for j, col in enumerate((best, gap)):
                line = jnp.sum(jnp.where(eye, col[at], 0.0), axis=0, keepdims=True)
                out_ref[r ^ me, :, j * half : (j + 1) * half] = line


def finish(me, bound, total, blocks, partners, earlier, state):
    slots, width = blocks[0].shape
    owners = bound.shape[0]
    units, accs, cids, sums = state
    rows = len(blocks) * slots
    padded = round_up(rows + STEP, LANES)
    old = [x for group in zip(units, accs, cids) for x in group]
    args = [me, bound, total, *blocks, *old, sums]
    return pl.pallas_call(
        functools.partial(finish_kernel, slots, partners, earlier, len(units)),
        out_shape=jax.ShapeDtypeStruct((owners, 1, 2 * round_up(slots, LANES)), f32),
        in_specs=[SMEM] + [VMEM] * (len(args) - 1),
        out_specs=VMEM,
        scratch_shapes=[pltpu.VMEM((padded, width), bf16)],
        compiler_params=pltpu.CompilerParams(vmem_limit_bytes=36 * MIB),
        cost_estimate=pl.CostEstimate(
            flops=2 * owners * slots * padded * width,
            bytes_accessed=2 * owners * slots * width,
            transcendentals=rows,
        ),
        name="finish_rows",
    )(*args)


def restore_kernel(slots, owner_ref, slot_ref, back_ref, best_ref, gap_ref):
    rows = owner_ref.shape[1]
    owners, _, width = back_ref.shape
    half = width // 2
    from_owner = to_bf16(owner_ref[...] == iota((owners, rows), 0))
    from_owner = jnp.concatenate([from_owner] * 3, axis=0)
    at_slot = slot_ref[...] == iota((slots, rows), 0)
    back = jnp.concatenate([back_ref[s] for s in range(owners)], axis=0)
    part0 = back.astype(bf16)
    rest = back - part0.astype(f32)
    part1 = rest.astype(bf16)
    part2 = (rest - part1.astype(f32)).astype(bf16)
    parts = jnp.concatenate([part0, part1, part2], axis=0)
    for i, ref in enumerate((best_ref, gap_ref)):
        table = lax.dot_general(
            parts[:, i * half : i * half + slots],
            from_owner,
            (((0,), (0,)), ((), ())),
            preferred_element_type=f32,
        )
        ref[...] = jnp.sum(jnp.where(at_slot, table, 0.0), axis=0, keepdims=True)


def restore(owner_row, slot_row, back, slots):
    return pl.pallas_call(
        functools.partial(restore_kernel, slots),
        out_shape=(jax.ShapeDtypeStruct(owner_row.shape, f32),) * 2,
        in_specs=[VMEM] * 3,
        out_specs=(VMEM, VMEM),
        compiler_params=pltpu.CompilerParams(vmem_limit_bytes=28 * MIB),
        name="restore_rows",
    )(owner_row, slot_row, back)


def exchange(x):
    return lax.all_to_all(x, "owner", split_axis=0, concat_axis=0, tiled=True)


def exchange_near(x):
    owners = lax.axis_size("owner")
    half = owners // 2
    halves = [list(range(half)), list(range(half, owners))]
    return lax.all_to_all(
        x, "owner", split_axis=0, concat_axis=0, axis_index_groups=halves, tiled=True
    )


def swap_far(blocks, partners):
    owners = lax.axis_size("owner")
    return [
        lax.ppermute(block, "owner", [(s, s ^ r) for s in range(owners)])
        for block, r in zip(blocks, partners)
    ]


def swap_far_together(blocks, partners):
    owners = lax.axis_size("owner")
    half = owners // 2
    turn = (lax.axis_index("owner").astype(i32) ^ jnp.array(partners, i32)) & (half - 1)
    by_owner = jnp.stack(blocks)[jnp.argsort(turn)]
    across = lax.ppermute(by_owner, "owner", [(s, s ^ half) for s in range(owners)])
    arrived = exchange_near(across)[turn]
    return [arrived[i] for i in range(half)]


def local(embeddings, cluster_ids):
    rows = embeddings.shape[0]
    owners = lax.axis_size("owner")
    clusters = CL_DEV * owners
    row_limit = 2 * rows // clusters
    most = round_up(CL_DEV * row_limit, STEP)
    usual = min(most, round_up(9 * rows // (8 * owners), STEP))
    few = owners <= MAX_PERMUTES
    me = lax.axis_index("owner").astype(i32).reshape(1)
    ids_row = cluster_ids.reshape(1, rows)
    counts, rank = count_rows(ids_row, owners, clusters)
    unit = unit_rows(embeddings)
    owner_row, slot_row, bound, total, load = assign(me, exchange(counts), rank)

    half = owners // 2
    near = tuple(range(half))
    far = tuple(range(owners - 1, half - 1, -1))
    share = half // 8
    cuts = [0, 3 * share, 6 * share, 7 * share, 8 * share]
    groups = [far[a:b] for a, b in zip(cuts, cuts[1:])]

    def compare(slots, apart):
        def packed(slot_in, partners, stacked):
            out = pack(me, owner_row, slot_in, unit, partners, slots, stacked)
            slot_in, *out = lax.optimization_barrier((slot_in, *out))
            return slot_in, out

        slot_in, blocks = slot_row, []
        for first in range(0, half, 2):
            slot_in, pair = packed(slot_in, far[first : first + 2], False)
            blocks += pair
            if first == 2:
                slot_in, stack = packed(slot_in, near, True)
        close = exchange_near(stack[0])
        swap = swap_far if apart else swap_far_together
        arrived = dict(zip(far, swap(blocks, far)))
        state = score(me, bound, [close], near, ([], [], [], None))
        for group in groups[:-1]:
            state = score(me, bound, [arrived[r] for r in group], group, state)
        last = groups[-1]
        answers = finish(
            me, bound, total, [arrived[r] for r in last], last, [near] + groups[:-1], state
        )
        return restore(owner_row, slot_row, exchange(answers), slots)

    best, gap = compare(usual, few)
    if usual < most:
        best, gap = lax.cond(
            load[0, 0] <= usual, lambda: (best, gap), lambda: compare(most, False)
        )
    return best.reshape(rows), gap.reshape(rows)


def solution(mesh):
    return jax.shard_map(
        local,
        mesh=mesh,
        in_specs=(P(("groups", "owner"), None), P(("groups", "owner"))),
        out_specs=(P(("groups", "owner")), P(("groups", "owner"))),
        check_vma=False,
    )
```

```python
import functools

import jax
import jax.numpy as jnp
from jax import lax
from jax.experimental import pallas as pl
from jax.experimental.pallas import tpu as pltpu
from jax.sharding import PartitionSpec as P

CL_DEV = 4
VARIANTS = 8
STEP = 16
TILE = 256
LANES = 128
GROUP = 4
MAX_PERMUTES = 16
RANKS = 4096
MIB = 1 << 20

epsilon = 1e-06
f32 = jnp.float32
bf16 = jnp.bfloat16
i32 = jnp.int32
VMEM = pl.BlockSpec(memory_space=pltpu.VMEM)
SMEM = pl.BlockSpec(memory_space=pltpu.SMEM)


def iota(shape, axis):
    return lax.broadcasted_iota(i32, shape, axis)


def round_up(value, unit):
    return -(-value // unit) * unit


def nt_dot(a, b):
    return lax.dot_general(a, b, (((1,), (1,)), ((), ())), preferred_element_type=f32)


def mm(a, b):
    return jnp.dot(a, b, preferred_element_type=f32)


def to_bf16(mask):
    return mask.astype(f32).astype(bf16)


def count_kernel(ids_ref, counts_ref, rank_ref):
    rows = ids_ref.shape[1]
    peers, _, clusters = counts_ref.shape
    label = iota((clusters, TILE), 0)
    upto = to_bf16(iota((TILE, TILE), 0) <= iota((TILE, TILE), 1))
    total = jnp.zeros((clusters, 1), f32)
    for b in range(rows // TILE):
        at = slice(b * TILE, (b + 1) * TILE)
        hot = ids_ref[:, at] == label
        prefix = mm(to_bf16(hot), upto)
        rank = jnp.sum(jnp.where(hot, prefix + total - 1.0, 0.0), axis=0, keepdims=True)
        rank_ref[:, at] = ids_ref[:, at] * RANKS + rank.astype(i32)
        total = total + prefix[:, TILE - 1 :]
    square = (clusters, clusters)
    eye = iota(square, 0) == iota(square, 1)
    total_row = jnp.sum(jnp.where(eye, total, 0.0), axis=0, keepdims=True).astype(i32)
    for peer in range(peers):
        counts_ref[peer] = total_row


def count_rows(ids_row, peers, clusters):
    return pl.pallas_call(
        count_kernel,
        out_shape=(
            jax.ShapeDtypeStruct((peers, 1, clusters), i32),
            jax.ShapeDtypeStruct(ids_row.shape, i32),
        ),
        in_specs=[VMEM],
        out_specs=(VMEM, VMEM),
        compiler_params=pltpu.CompilerParams(vmem_limit_bytes=16 * MIB),
        name="count_rows",
    )(ids_row)


def assign_kernel(
    me_ref, counts_ref, rank_ref, owner_ref, slot_ref, bound_ref, total_ref, load_ref
):
    owners, _, clusters = counts_ref.shape
    rows = rank_ref.shape[1]
    shift = owners.bit_length() - 1
    me = me_ref[0]
    count = jnp.concatenate([counts_ref[s].astype(f32) for s in range(owners)], axis=0)
    count16 = count.astype(bf16)
    square = (clusters, clusters)
    sub, lane = iota(square, 0), iota(square, 1)
    total_row = jnp.sum(count, axis=0, keepdims=True)
    total_col = jnp.sum(jnp.where(sub == lane, total_row, 0.0), axis=1, keepdims=True)
    tie = total_row == total_col
    outranks_col = (total_row > total_col) | (tie & (lane < sub))
    outranks_row = (total_col > total_row) | (tie & (sub < lane))
    rank_col = jnp.sum(outranks_col.astype(f32), axis=1, keepdims=True).astype(i32)
    rank_row = jnp.sum(outranks_row.astype(f32), axis=0, keepdims=True).astype(i32)

    def owner_of(rank, variant):
        layer = rank >> shift
        within = rank & (owners - 1)
        flip = jnp.zeros_like(variant)
        for p in range(1, CL_DEV):
            flip = flip + jnp.where(layer == p, (variant >> (p - 1)) & 1, 0)
        within = within ^ flip
        return jnp.where((layer & 1) == 1, owners - 1 - within, within)

    wide = (clusters, VARIANTS * owners)
    variant = iota(wide, 1) >> shift
    tried = owner_of(rank_col, variant) == (iota(wide, 1) & (owners - 1))
    load = jnp.max(mm(count16, to_bf16(tried)), axis=0, keepdims=True)
    by_variant = (VARIANTS, VARIANTS * owners)
    worst = jnp.max(
        jnp.where((iota(by_variant, 1) >> shift) == iota(by_variant, 0), load, 0.0),
        axis=1,
        keepdims=True,
    )
    best = jnp.min(worst, axis=0, keepdims=True)
    chosen = jnp.min(
        jnp.where(worst == best, iota((VARIANTS, 1), 0), VARIANTS), axis=0, keepdims=True
    )
    owner_col = owner_of(rank_col, chosen + jnp.zeros_like(rank_col))
    owner_row = owner_of(rank_row, chosen + jnp.zeros_like(rank_row))
    layer_col, layer_row = rank_col >> shift, rank_row >> shift
    load_ref[...] = jnp.broadcast_to(best, load_ref.shape).astype(i32)

    mine = jnp.sum(jnp.where(iota(count.shape, 0) == me, count, 0.0), axis=0, keepdims=True)
    earlier = (owner_row == owner_col) & (layer_row < layer_col)
    offset_col = jnp.sum(jnp.where(earlier, mine, 0.0), axis=1, keepdims=True)
    ids = rank_ref[...] // RANKS
    hot = ids == iota((clusters, rows), 0)
    owner_ref[...] = jnp.sum(
        jnp.where(hot, owner_col.astype(f32), 0.0), axis=0, keepdims=True
    ).astype(i32)
    slot_ref[...] = (
        jnp.sum(jnp.where(hot, offset_col, 0.0), axis=0, keepdims=True)
    ).astype(i32) + (rank_ref[...] & (RANKS - 1))

    select = (owner_col == me) & (layer_col <= iota((clusters, LANES), 1))
    turn = iota((owners, owners), 1) == (iota((owners, owners), 0) ^ me)
    turned = mm(to_bf16(turn), count16).astype(bf16)
    bound_ref[...] = mm(turned, to_bf16(select))
    own = (owner_row == me) & (layer_row == iota((8, clusters), 0))
    total_ref[...] = jnp.broadcast_to(
        jnp.sum(jnp.where(own, total_row, 0.0), axis=1, keepdims=True), total_ref.shape
    )


def assign(me, counts, rank):
    owners, _, clusters = counts.shape
    rows = rank.shape[1]
    return pl.pallas_call(
        assign_kernel,
        out_shape=(
            jax.ShapeDtypeStruct((1, rows), i32),
            jax.ShapeDtypeStruct((1, rows), i32),
            jax.ShapeDtypeStruct((owners, LANES), f32),
            jax.ShapeDtypeStruct((8, LANES), f32),
            jax.ShapeDtypeStruct((1, LANES), i32),
        ),
        in_specs=[SMEM, VMEM, VMEM],
        out_specs=(VMEM,) * 5,
        compiler_params=pltpu.CompilerParams(vmem_limit_bytes=16 * MIB),
        name="assign",
    )(me, counts, rank)


def pack_kernel(slots, partners, me_ref, owner_ref, slot_ref, rows_ref, *out_refs):
    rows = rows_ref.shape[0]
    me = me_ref[0]
    slot = iota((slots, rows), 0)
    takes = []
    for partner in partners:
        key = jnp.where(owner_ref[...] == (me ^ partner), slot_ref[...], -1)
        takes.append(to_bf16(slot == key))
    picked = mm(jnp.concatenate(takes, axis=0), rows_ref[...]).astype(bf16)
    for i, ref in enumerate(out_refs):
        ref[...] = picked[i * slots : (i + 1) * slots]


def pack(me, owner_row, slot_row, unit, partners, slots):
    rows, width = unit.shape
    flops = 2 * len(partners) * slots * rows * width
    return pl.pallas_call(
        functools.partial(pack_kernel, slots, partners),
        out_shape=(jax.ShapeDtypeStruct((slots, width), bf16),) * len(partners),
        in_specs=[SMEM, VMEM, VMEM, VMEM],
        out_specs=(VMEM,) * len(partners),
        compiler_params=pltpu.CompilerParams(vmem_limit_bytes=28 * MIB),
        cost_estimate=pl.CostEstimate(
            flops=flops, bytes_accessed=2 * rows * width, transcendentals=0
        ),
        name="pack_rows",
    )(me, owner_row, slot_row, unit)


def unit_kernel(rows_ref, unit_ref):
    def body(b, carry):
        at = pl.ds(pl.multiple_of(b * TILE, TILE), TILE)
        x = rows_ref[at, :].astype(f32)
        scale = lax.rsqrt(jnp.sum(x * x, axis=1, keepdims=True) + epsilon)
        unit_ref[at, :] = (x * scale).astype(bf16)
        return carry

    lax.fori_loop(0, rows_ref.shape[0] // TILE, body, 0)


def unit_rows(embeddings):
    rows, width = embeddings.shape
    return pl.pallas_call(
        unit_kernel,
        out_shape=jax.ShapeDtypeStruct((rows, width), bf16),
        in_specs=[VMEM],
        out_specs=VMEM,
        compiler_params=pltpu.CompilerParams(vmem_limit_bytes=16 * MIB),
        cost_estimate=pl.CostEstimate(
            flops=8 * rows * width, bytes_accessed=4 * rows * width, transcendentals=rows
        ),
        name="unit_rows",
    )(embeddings)


def cluster_lanes(bound_ref, partners, slots, width):
    lane = iota((1, width), 1).astype(f32)
    result = jnp.where(lane < len(partners) * slots, 0.0, -1.0)
    for i, r in enumerate(partners):
        for k in range(CL_DEV):
            first = bound_ref[r : r + 1, k : k + 1] + float(i * slots)
            result = result + ((lane >= first) & (lane < float((i + 1) * slots))).astype(f32)
    return result


def cluster_rows(bound_ref, r, slots):
    slot = iota((slots, LANES), 0).astype(f32)
    result = jnp.zeros((slots, LANES), f32)
    for k in range(CL_DEV):
        result = result + (slot >= bound_ref[r : r + 1, k : k + 1]).astype(f32)
    return result


def score_group(new_ref, new_cids, olds, cid_row, slots_new):
    padded = new_ref.shape[0]
    groups = padded // LANES
    new = new_ref[...]

    def folded(scores, cids, skip_same):
        rows = scores.shape[0]
        row = iota((rows, LANES), 0)
        lane = iota((rows, LANES), 1)
        best, cols = None, []
        for g in range(groups):
            at = slice(g * LANES, (g + 1) * LANES)
            allowed = cids == cid_row[:, at]
            if skip_same:
                allowed = allowed & (row != lane + g * LANES)
            part = jnp.where(allowed, scores[:, at], -1.0)
            best = part if best is None else jnp.maximum(best, part)
            cols.append(jnp.max(part, axis=0, keepdims=True))
        return best, cols

    columns = None
    results = []
    for unit_ref, acc_ref, cid_ref in olds:
        scores = nt_dot(unit_ref[...], new)
        best, cols = folded(scores, cid_ref[...], False)
        columns = cols if columns is None else [jnp.maximum(a, b) for a, b in zip(columns, cols)]
        results.append((scores, jnp.maximum(acc_ref[...], best)))
    scores = nt_dot(new[0:slots_new], new)
    best, _ = folded(scores, new_cids, True)
    if columns is not None:
        row = iota((slots_new, LANES), 0)
        lane = iota((slots_new, LANES), 1)
        for g, col in enumerate(columns):
            best = jnp.maximum(best, jnp.where(row == lane + g * LANES, col, -1.0))
    results.append((scores, best))
    return results


def member_sums(cid_row, new):
    hot = to_bf16(cid_row == iota((8, cid_row.shape[1]), 0).astype(f32))
    return mm(hot, new)


def score_kernel(slots, partners, olds, bound_ref, *refs):
    fresh = len(partners)
    raw_refs, refs = refs[:fresh], refs[fresh:]
    old_refs = [refs[3 * i : 3 * i + 3] for i in range(olds)]
    refs = refs[3 * olds :]
    if olds:
        sums_ref, refs = refs[0], refs[1:]
    unit_ref, acc_ref, cid_ref, sums_out = refs[:4]
    old_accs = refs[4 : 4 + olds]
    new_ref = refs[4 + olds]
    rows = fresh * slots
    for i, r in enumerate(partners):
        at = slice(i * slots, (i + 1) * slots)
        new_ref[at, :] = raw_refs[i][...]
        cid_ref[at, :] = cluster_rows(bound_ref, r, slots)
    padded = new_ref.shape[0]
    if padded > rows:
        new_ref[rows:, :] = jnp.zeros((padded - rows, new_ref.shape[1]), bf16)
    unit_ref[...] = new_ref[0:rows, :]
    cid_row = cluster_lanes(bound_ref, partners, slots, padded)
    results = score_group(new_ref, cid_ref[...], old_refs, cid_row, rows)
    for (_, best), ref in zip(results, list(old_accs) + [acc_ref]):
        ref[...] = best
    sums = member_sums(cid_row, new_ref[...])
    sums_out[...] = sums + sums_ref[...] if olds else sums


def score(bound, blocks, partners, state):
    slots, width = blocks[0].shape
    units, accs, cids, sums = state
    rows = len(blocks) * slots
    padded = round_up(rows, LANES)
    old = [x for group in zip(units, accs, cids) for x in group]
    old_rows = sum(u.shape[0] for u in units)
    acc_shapes = [jax.ShapeDtypeStruct(a.shape, f32) for a in accs]
    out_shape = (
        jax.ShapeDtypeStruct((rows, width), bf16),
        jax.ShapeDtypeStruct((rows, LANES), f32),
        jax.ShapeDtypeStruct((rows, LANES), f32),
        jax.ShapeDtypeStruct((8, width), f32),
        *acc_shapes,
    )
    args = [bound, *blocks, *old] + ([sums] if units else [])
    out = pl.pallas_call(
        functools.partial(score_kernel, slots, partners, len(units)),
        out_shape=out_shape,
        in_specs=[VMEM] * len(args),
        out_specs=(VMEM,) * len(out_shape),
        scratch_shapes=[pltpu.VMEM((padded, width), bf16)],
        compiler_params=pltpu.CompilerParams(vmem_limit_bytes=36 * MIB),
        cost_estimate=pl.CostEstimate(
            flops=2 * (old_rows + rows) * padded * width,
            bytes_accessed=2 * (old_rows + rows) * width,
            transcendentals=rows,
        ),
        name="score_rows",
    )(*args)
    return units + [out[0]], list(out[4:]) + [out[1]], cids + [out[2]], out[3]


def finish_kernel(slots, partners, earlier, olds, me_ref, bound_ref, total_ref, *refs):
    fresh = len(partners)
    raw_refs, refs = refs[:fresh], refs[fresh:]
    old_refs = [refs[3 * i : 3 * i + 3] for i in range(olds)]
    sums_ref, out_ref, new_ref = refs[3 * olds :]
    me = me_ref[0]
    rows = fresh * slots
    padded, width = new_ref.shape
    new_ref[rows:, :] = jnp.zeros((padded - rows, width), bf16)
    pieces = []
    for i, r in enumerate(partners):
        new_ref[i * slots : (i + 1) * slots, :] = raw_refs[i][...]
        pieces.append(cluster_rows(bound_ref, r, slots))
    new_cids = jnp.concatenate(pieces, axis=0)
    cid_row = cluster_lanes(bound_ref, partners, slots, padded)
    sums = sums_ref[...] + member_sums(cid_row, new_ref[...])
    centroid = (sums / jnp.maximum(total_ref[:, 0:1], 1.0)).astype(bf16)
    centroid = jnp.concatenate([centroid, jnp.zeros_like(centroid)], axis=0)
    new_ref[rows : rows + STEP, :] = centroid
    results = score_group(new_ref, new_cids, old_refs, cid_row, rows)
    half = out_ref.shape[2] // 2
    group, within = rows // LANES, rows % LANES
    eye = iota((slots, half), 0) == iota((slots, half), 1)
    all_cids = [old[2][...] for old in old_refs] + [new_cids]
    for (scores, acc), cids, names in zip(results, all_cids, earlier + [partners]):
        best = jnp.max(acc, axis=1, keepdims=True)
        lane = iota(cids.shape, 1).astype(f32)
        dots = scores[:, group * LANES : (group + 1) * LANES]
        gap = 1.0 - jnp.sum(
            jnp.where(lane == cids + float(within), dots, 0.0), axis=1, keepdims=True
        )
        for i, r in enumerate(names):
            at = slice(i * slots, (i + 1) * slots)
            for j, col in enumerate((best, gap)):
                line = jnp.sum(jnp.where(eye, col[at], 0.0), axis=0, keepdims=True)
                out_ref[r ^ me, :, j * half : (j + 1) * half] = line


def finish(me, bound, total, blocks, partners, earlier, state):
    slots, width = blocks[0].shape
    owners = bound.shape[0]
    units, accs, cids, sums = state
    rows = len(blocks) * slots
    padded = round_up(rows + STEP, LANES)
    old = [x for group in zip(units, accs, cids) for x in group]
    args = [me, bound, total, *blocks, *old, sums]
    return pl.pallas_call(
        functools.partial(finish_kernel, slots, partners, earlier, len(units)),
        out_shape=jax.ShapeDtypeStruct((owners, 1, 2 * round_up(slots, LANES)), f32),
        in_specs=[SMEM] + [VMEM] * (len(args) - 1),
        out_specs=VMEM,
        scratch_shapes=[pltpu.VMEM((padded, width), bf16)],
        compiler_params=pltpu.CompilerParams(vmem_limit_bytes=36 * MIB),
        cost_estimate=pl.CostEstimate(
            flops=2 * owners * slots * padded * width,
            bytes_accessed=2 * owners * slots * width,
            transcendentals=rows,
        ),
        name="finish_rows",
    )(*args)


def restore_kernel(slots, owner_ref, slot_ref, back_ref, best_ref, gap_ref):
    rows = owner_ref.shape[1]
    owners, _, width = back_ref.shape
    half = width // 2
    from_owner = to_bf16(owner_ref[...] == iota((owners, rows), 0))
    from_owner = jnp.concatenate([from_owner] * 3, axis=0)
    at_slot = slot_ref[...] == iota((slots, rows), 0)
    back = jnp.concatenate([back_ref[s] for s in range(owners)], axis=0)
    part0 = back.astype(bf16)
    rest = back - part0.astype(f32)
    part1 = rest.astype(bf16)
    part2 = (rest - part1.astype(f32)).astype(bf16)
    parts = jnp.concatenate([part0, part1, part2], axis=0)
    for i, ref in enumerate((best_ref, gap_ref)):
        table = lax.dot_general(
            parts[:, i * half : i * half + slots],
            from_owner,
            (((0,), (0,)), ((), ())),
            preferred_element_type=f32,
        )
        ref[...] = jnp.sum(jnp.where(at_slot, table, 0.0), axis=0, keepdims=True)


def restore(owner_row, slot_row, back, slots):
    return pl.pallas_call(
        functools.partial(restore_kernel, slots),
        out_shape=(jax.ShapeDtypeStruct(owner_row.shape, f32),) * 2,
        in_specs=[VMEM] * 3,
        out_specs=(VMEM, VMEM),
        compiler_params=pltpu.CompilerParams(vmem_limit_bytes=28 * MIB),
        name="restore_rows",
    )(owner_row, slot_row, back)


def exchange(x):
    return lax.all_to_all(x, "owner", split_axis=0, concat_axis=0, tiled=True)


def swap_together(blocks):
    owners = len(blocks)
    order = jnp.arange(owners, dtype=i32) ^ lax.axis_index("owner").astype(i32)
    arrived = exchange(jnp.stack(blocks)[order])[order]
    return [arrived[r] for r in range(owners)]


def swap_apart(blocks):
    pairs = [[(s, s ^ r) for s in range(len(blocks))] for r in range(len(blocks))]
    return blocks[:1] + [
        lax.ppermute(block, "owner", pair) for block, pair in zip(blocks[1:], pairs[1:])
    ]


def local(embeddings, cluster_ids):
    rows = embeddings.shape[0]
    owners = lax.axis_size("owner")
    clusters = CL_DEV * owners
    row_limit = 2 * rows // clusters
    most = round_up(CL_DEV * row_limit, STEP)
    usual = min(most, round_up(9 * rows // (8 * owners), STEP))
    few = owners <= MAX_PERMUTES
    me = lax.axis_index("owner").astype(i32).reshape(1)
    ids_row = cluster_ids.reshape(1, rows)
    counts, rank = count_rows(ids_row, owners, clusters)
    unit = unit_rows(embeddings)
    owner_row, slot_row, bound, total, load = assign(me, exchange(counts), rank)

    sent = list(range(owners - 1, 0, -1))
    seen = [0] + sent
    sent = sent + [0]
    packs = [tuple(sent[:2]), tuple(sent[2:4])]
    packs += [tuple(sent[i : i + GROUP]) for i in range(4, owners, GROUP)]
    share = owners // 16 if owners >= 16 else 1
    groups, at = [], 0
    for size in (5, 4, 4):
        groups.append(seen[at : at + size * share])
        at += size * share
    groups.append(seen[at:])

    def compare(slots, apart):
        blocks = [None] * owners
        slot_in = slot_row
        for partners in packs:
            packed = pack(me, owner_row, slot_in, unit, partners, slots)
            slot_in, *packed = lax.optimization_barrier((slot_in, *packed))
            for r, block in zip(partners, packed):
                blocks[r] = block
        arrived = swap_apart(blocks) if apart else swap_together(blocks)
        state = ([], [], [], None)
        for group in groups[:-1]:
            state = score(bound, [arrived[r] for r in group], group, state)
        last = groups[-1]
        answers = finish(
            me, bound, total, [arrived[r] for r in last], last, groups[:-1], state
        )
        return restore(owner_row, slot_row, exchange(answers), slots)

    best, gap = compare(usual, few)
    if usual < most:
        best, gap = lax.cond(
            load[0, 0] <= usual, lambda: (best, gap), lambda: compare(most, False)
        )
    return best.reshape(rows), gap.reshape(rows)


def solution(mesh):
    return jax.shard_map(
        local,
        mesh=mesh,
        in_specs=(P(("groups", "owner"), None), P(("groups", "owner"))),
        out_specs=(P(("groups", "owner")), P(("groups", "owner"))),
        check_vma=False,
    )
```

```python
import functools

import jax
import jax.numpy as jnp
from jax import lax
from jax.experimental import pallas as pl
from jax.experimental.pallas import tpu as pltpu
from jax.sharding import PartitionSpec as P

CL_DEV = 4
VARIANTS = 8
STEP = 16
TILE = 256
LANES = 128
GROUP = 4
MAX_PERMUTES = 16
RANKS = 4096
MIB = 1 << 20

epsilon = 1e-06
f32 = jnp.float32
bf16 = jnp.bfloat16
i32 = jnp.int32
VMEM = pl.BlockSpec(memory_space=pltpu.VMEM)
SMEM = pl.BlockSpec(memory_space=pltpu.SMEM)


def iota(shape, axis):
    return lax.broadcasted_iota(i32, shape, axis)


def round_up(value, unit):
    return -(-value // unit) * unit


def nt_dot(a, b):
    return lax.dot_general(a, b, (((1,), (1,)), ((), ())), preferred_element_type=f32)


def mm(a, b):
    return jnp.dot(a, b, preferred_element_type=f32)


def to_bf16(mask):
    return mask.astype(f32).astype(bf16)


def count_kernel(ids_ref, counts_ref, rank_ref):
    rows = ids_ref.shape[1]
    peers, _, clusters = counts_ref.shape
    label = iota((clusters, TILE), 0)
    upto = to_bf16(iota((TILE, TILE), 0) <= iota((TILE, TILE), 1))
    total = jnp.zeros((clusters, 1), f32)
    for b in range(rows // TILE):
        at = slice(b * TILE, (b + 1) * TILE)
        hot = ids_ref[:, at] == label
        prefix = mm(to_bf16(hot), upto)
        rank = jnp.sum(jnp.where(hot, prefix + total - 1.0, 0.0), axis=0, keepdims=True)
        rank_ref[:, at] = ids_ref[:, at] * RANKS + rank.astype(i32)
        total = total + prefix[:, TILE - 1 :]
    square = (clusters, clusters)
    eye = iota(square, 0) == iota(square, 1)
    total_row = jnp.sum(jnp.where(eye, total, 0.0), axis=0, keepdims=True).astype(i32)
    for peer in range(peers):
        counts_ref[peer] = total_row


def count_rows(ids_row, peers, clusters):
    return pl.pallas_call(
        count_kernel,
        out_shape=(
            jax.ShapeDtypeStruct((peers, 1, clusters), i32),
            jax.ShapeDtypeStruct(ids_row.shape, i32),
        ),
        in_specs=[VMEM],
        out_specs=(VMEM, VMEM),
        compiler_params=pltpu.CompilerParams(vmem_limit_bytes=16 * MIB),
        name="count_rows",
    )(ids_row)


def assign_kernel(
    me_ref, counts_ref, rank_ref, owner_ref, slot_ref, bound_ref, total_ref, load_ref
):
    owners, _, clusters = counts_ref.shape
    rows = rank_ref.shape[1]
    shift = owners.bit_length() - 1
    me = me_ref[0]
    count = jnp.concatenate([counts_ref[s].astype(f32) for s in range(owners)], axis=0)
    count16 = count.astype(bf16)
    square = (clusters, clusters)
    sub, lane = iota(square, 0), iota(square, 1)
    total_row = jnp.sum(count, axis=0, keepdims=True)
    total_col = jnp.sum(jnp.where(sub == lane, total_row, 0.0), axis=1, keepdims=True)
    tie = total_row == total_col
    outranks_col = (total_row > total_col) | (tie & (lane < sub))
    outranks_row = (total_col > total_row) | (tie & (sub < lane))
    rank_col = jnp.sum(outranks_col.astype(f32), axis=1, keepdims=True).astype(i32)
    rank_row = jnp.sum(outranks_row.astype(f32), axis=0, keepdims=True).astype(i32)

    def owner_of(rank, variant):
        layer = rank >> shift
        within = rank & (owners - 1)
        flip = jnp.zeros_like(variant)
        for p in range(1, CL_DEV):
            flip = flip + jnp.where(layer == p, (variant >> (p - 1)) & 1, 0)
        within = within ^ flip
        return jnp.where((layer & 1) == 1, owners - 1 - within, within)

    wide = (clusters, VARIANTS * owners)
    variant = iota(wide, 1) >> shift
    tried = owner_of(rank_col, variant) == (iota(wide, 1) & (owners - 1))
    load = jnp.max(mm(count16, to_bf16(tried)), axis=0, keepdims=True)
    by_variant = (VARIANTS, VARIANTS * owners)
    worst = jnp.max(
        jnp.where((iota(by_variant, 1) >> shift) == iota(by_variant, 0), load, 0.0),
        axis=1,
        keepdims=True,
    )
    best = jnp.min(worst, axis=0, keepdims=True)
    chosen = jnp.min(
        jnp.where(worst == best, iota((VARIANTS, 1), 0), VARIANTS), axis=0, keepdims=True
    )
    owner_col = owner_of(rank_col, chosen + jnp.zeros_like(rank_col))
    owner_row = owner_of(rank_row, chosen + jnp.zeros_like(rank_row))
    layer_col, layer_row = rank_col >> shift, rank_row >> shift
    load_ref[...] = jnp.broadcast_to(best, load_ref.shape).astype(i32)

    mine = jnp.sum(jnp.where(iota(count.shape, 0) == me, count, 0.0), axis=0, keepdims=True)
    earlier = (owner_row == owner_col) & (layer_row < layer_col)
    offset_col = jnp.sum(jnp.where(earlier, mine, 0.0), axis=1, keepdims=True)
    ids = rank_ref[...] // RANKS
    hot = ids == iota((clusters, rows), 0)
    owner_ref[...] = jnp.sum(
        jnp.where(hot, owner_col.astype(f32), 0.0), axis=0, keepdims=True
    ).astype(i32)
    slot_ref[...] = (
        jnp.sum(jnp.where(hot, offset_col, 0.0), axis=0, keepdims=True)
    ).astype(i32) + (rank_ref[...] & (RANKS - 1))

    select = (owner_col == me) & (layer_col <= iota((clusters, LANES), 1))
    turn = iota((owners, owners), 1) == (iota((owners, owners), 0) ^ me)
    turned = mm(to_bf16(turn), count16).astype(bf16)
    bound_ref[...] = mm(turned, to_bf16(select))
    own = (owner_row == me) & (layer_row == iota((8, clusters), 0))
    total_ref[...] = jnp.broadcast_to(
        jnp.sum(jnp.where(own, total_row, 0.0), axis=1, keepdims=True), total_ref.shape
    )


def assign(me, counts, rank):
    owners, _, clusters = counts.shape
    rows = rank.shape[1]
    return pl.pallas_call(
        assign_kernel,
        out_shape=(
            jax.ShapeDtypeStruct((1, rows), i32),
            jax.ShapeDtypeStruct((1, rows), i32),
            jax.ShapeDtypeStruct((owners, LANES), f32),
            jax.ShapeDtypeStruct((8, LANES), f32),
            jax.ShapeDtypeStruct((1, LANES), i32),
        ),
        in_specs=[SMEM, VMEM, VMEM],
        out_specs=(VMEM,) * 5,
        compiler_params=pltpu.CompilerParams(vmem_limit_bytes=16 * MIB),
        name="assign",
    )(me, counts, rank)


def pack_kernel(slots, partners, me_ref, owner_ref, slot_ref, rows_ref, *out_refs):
    rows = rows_ref.shape[0]
    me = me_ref[0]
    slot = iota((slots, rows), 0)
    takes = []
    for partner in partners:
        key = jnp.where(owner_ref[...] == (me ^ partner), slot_ref[...], -1)
        takes.append(to_bf16(slot == key))
    picked = mm(jnp.concatenate(takes, axis=0), rows_ref[...]).astype(bf16)
    for i, ref in enumerate(out_refs):
        ref[...] = picked[i * slots : (i + 1) * slots]


def pack(me, owner_row, slot_row, unit, partners, slots):
    rows, width = unit.shape
    flops = 2 * len(partners) * slots * rows * width
    return pl.pallas_call(
        functools.partial(pack_kernel, slots, partners),
        out_shape=(jax.ShapeDtypeStruct((slots, width), bf16),) * len(partners),
        in_specs=[SMEM, VMEM, VMEM, VMEM],
        out_specs=(VMEM,) * len(partners),
        compiler_params=pltpu.CompilerParams(vmem_limit_bytes=28 * MIB),
        cost_estimate=pl.CostEstimate(
            flops=flops, bytes_accessed=2 * rows * width, transcendentals=0
        ),
        name="pack_rows",
    )(me, owner_row, slot_row, unit)


def unit_kernel(rows_ref, unit_ref):
    def body(b, carry):
        at = pl.ds(pl.multiple_of(b * TILE, TILE), TILE)
        x = rows_ref[at, :].astype(f32)
        scale = lax.rsqrt(jnp.sum(x * x, axis=1, keepdims=True) + epsilon)
        unit_ref[at, :] = (x * scale).astype(bf16)
        return carry

    lax.fori_loop(0, rows_ref.shape[0] // TILE, body, 0)


def unit_rows(embeddings):
    rows, width = embeddings.shape
    return pl.pallas_call(
        unit_kernel,
        out_shape=jax.ShapeDtypeStruct((rows, width), bf16),
        in_specs=[VMEM],
        out_specs=VMEM,
        compiler_params=pltpu.CompilerParams(vmem_limit_bytes=16 * MIB),
        cost_estimate=pl.CostEstimate(
            flops=8 * rows * width, bytes_accessed=4 * rows * width, transcendentals=rows
        ),
        name="unit_rows",
    )(embeddings)


def cluster_lanes(bound_ref, partners, slots, width):
    lane = iota((1, width), 1).astype(f32)
    result = jnp.where(lane < len(partners) * slots, 0.0, -1.0)
    for i, r in enumerate(partners):
        for k in range(CL_DEV):
            first = bound_ref[r : r + 1, k : k + 1] + float(i * slots)
            result = result + ((lane >= first) & (lane < float((i + 1) * slots))).astype(f32)
    return result


def cluster_rows(bound_ref, r, slots):
    slot = iota((slots, LANES), 0).astype(f32)
    result = jnp.zeros((slots, LANES), f32)
    for k in range(CL_DEV):
        result = result + (slot >= bound_ref[r : r + 1, k : k + 1]).astype(f32)
    return result


def score_group(new_ref, new_cids, olds, cid_row, slots_new):
    padded = new_ref.shape[0]
    groups = padded // LANES
    new = new_ref[...]

    def folded(scores, cids, skip_same):
        rows = scores.shape[0]
        row = iota((rows, LANES), 0)
        lane = iota((rows, LANES), 1)
        best, cols = None, []
        for g in range(groups):
            at = slice(g * LANES, (g + 1) * LANES)
            allowed = cids == cid_row[:, at]
            if skip_same:
                allowed = allowed & (row != lane + g * LANES)
            part = jnp.where(allowed, scores[:, at], -1.0)
            best = part if best is None else jnp.maximum(best, part)
            cols.append(jnp.max(part, axis=0, keepdims=True))
        return best, cols

    columns = None
    results = []
    for unit_ref, acc_ref, cid_ref in olds:
        scores = nt_dot(unit_ref[...], new)
        best, cols = folded(scores, cid_ref[...], False)
        columns = cols if columns is None else [jnp.maximum(a, b) for a, b in zip(columns, cols)]
        results.append((scores, jnp.maximum(acc_ref[...], best)))
    scores = nt_dot(new[0:slots_new], new)
    best, _ = folded(scores, new_cids, True)
    if columns is not None:
        row = iota((slots_new, LANES), 0)
        lane = iota((slots_new, LANES), 1)
        for g, col in enumerate(columns):
            best = jnp.maximum(best, jnp.where(row == lane + g * LANES, col, -1.0))
    results.append((scores, best))
    return results


def member_sums(cid_row, new):
    hot = to_bf16(cid_row == iota((8, cid_row.shape[1]), 0).astype(f32))
    return mm(hot, new)


def score_kernel(slots, partners, olds, bound_ref, *refs):
    fresh = len(partners)
    raw_refs, refs = refs[:fresh], refs[fresh:]
    old_refs = [refs[3 * i : 3 * i + 3] for i in range(olds)]
    refs = refs[3 * olds :]
    if olds:
        sums_ref, refs = refs[0], refs[1:]
    unit_ref, acc_ref, cid_ref, sums_out = refs[:4]
    old_accs = refs[4 : 4 + olds]
    new_ref = refs[4 + olds]
    rows = fresh * slots
    for i, r in enumerate(partners):
        at = slice(i * slots, (i + 1) * slots)
        new_ref[at, :] = raw_refs[i][...]
        cid_ref[at, :] = cluster_rows(bound_ref, r, slots)
    padded = new_ref.shape[0]
    if padded > rows:
        new_ref[rows:, :] = jnp.zeros((padded - rows, new_ref.shape[1]), bf16)
    unit_ref[...] = new_ref[0:rows, :]
    cid_row = cluster_lanes(bound_ref, partners, slots, padded)
    results = score_group(new_ref, cid_ref[...], old_refs, cid_row, rows)
    for (_, best), ref in zip(results, list(old_accs) + [acc_ref]):
        ref[...] = best
    sums = member_sums(cid_row, new_ref[...])
    sums_out[...] = sums + sums_ref[...] if olds else sums


def score(bound, blocks, partners, state):
    slots, width = blocks[0].shape
    units, accs, cids, sums = state
    rows = len(blocks) * slots
    padded = round_up(rows, LANES)
    old = [x for group in zip(units, accs, cids) for x in group]
    old_rows = sum(u.shape[0] for u in units)
    acc_shapes = [jax.ShapeDtypeStruct(a.shape, f32) for a in accs]
    out_shape = (
        jax.ShapeDtypeStruct((rows, width), bf16),
        jax.ShapeDtypeStruct((rows, LANES), f32),
        jax.ShapeDtypeStruct((rows, LANES), f32),
        jax.ShapeDtypeStruct((8, width), f32),
        *acc_shapes,
    )
    args = [bound, *blocks, *old] + ([sums] if units else [])
    out = pl.pallas_call(
        functools.partial(score_kernel, slots, partners, len(units)),
        out_shape=out_shape,
        in_specs=[VMEM] * len(args),
        out_specs=(VMEM,) * len(out_shape),
        scratch_shapes=[pltpu.VMEM((padded, width), bf16)],
        compiler_params=pltpu.CompilerParams(vmem_limit_bytes=36 * MIB),
        cost_estimate=pl.CostEstimate(
            flops=2 * (old_rows + rows) * padded * width,
            bytes_accessed=2 * (old_rows + rows) * width,
            transcendentals=rows,
        ),
        name="score_rows",
    )(*args)
    return units + [out[0]], list(out[4:]) + [out[1]], cids + [out[2]], out[3]


def finish_kernel(slots, partners, earlier, olds, me_ref, bound_ref, total_ref, *refs):
    fresh = len(partners)
    raw_refs, refs = refs[:fresh], refs[fresh:]
    old_refs = [refs[3 * i : 3 * i + 3] for i in range(olds)]
    sums_ref, out_ref, new_ref = refs[3 * olds :]
    me = me_ref[0]
    rows = fresh * slots
    padded, width = new_ref.shape
    new_ref[rows:, :] = jnp.zeros((padded - rows, width), bf16)
    pieces = []
    for i, r in enumerate(partners):
        new_ref[i * slots : (i + 1) * slots, :] = raw_refs[i][...]
        pieces.append(cluster_rows(bound_ref, r, slots))
    new_cids = jnp.concatenate(pieces, axis=0)
    cid_row = cluster_lanes(bound_ref, partners, slots, padded)
    sums = sums_ref[...] + member_sums(cid_row, new_ref[...])
    centroid = (sums / jnp.maximum(total_ref[:, 0:1], 1.0)).astype(bf16)
    centroid = jnp.concatenate([centroid, jnp.zeros_like(centroid)], axis=0)
    new_ref[rows : rows + STEP, :] = centroid
    results = score_group(new_ref, new_cids, old_refs, cid_row, rows)
    half = out_ref.shape[2] // 2
    group, within = rows // LANES, rows % LANES
    eye = iota((slots, half), 0) == iota((slots, half), 1)
    all_cids = [old[2][...] for old in old_refs] + [new_cids]
    for (scores, acc), cids, names in zip(results, all_cids, earlier + [partners]):
        best = jnp.max(acc, axis=1, keepdims=True)
        lane = iota(cids.shape, 1).astype(f32)
        dots = scores[:, group * LANES : (group + 1) * LANES]
        gap = 1.0 - jnp.sum(
            jnp.where(lane == cids + float(within), dots, 0.0), axis=1, keepdims=True
        )
        for i, r in enumerate(names):
            at = slice(i * slots, (i + 1) * slots)
            for j, col in enumerate((best, gap)):
                line = jnp.sum(jnp.where(eye, col[at], 0.0), axis=0, keepdims=True)
                out_ref[r ^ me, :, j * half : (j + 1) * half] = line


def finish(me, bound, total, blocks, partners, earlier, state):
    slots, width = blocks[0].shape
    owners = bound.shape[0]
    units, accs, cids, sums = state
    rows = len(blocks) * slots
    padded = round_up(rows + STEP, LANES)
    old = [x for group in zip(units, accs, cids) for x in group]
    args = [me, bound, total, *blocks, *old, sums]
    return pl.pallas_call(
        functools.partial(finish_kernel, slots, partners, earlier, len(units)),
        out_shape=jax.ShapeDtypeStruct((owners, 1, 2 * round_up(slots, LANES)), f32),
        in_specs=[SMEM] + [VMEM] * (len(args) - 1),
        out_specs=VMEM,
        scratch_shapes=[pltpu.VMEM((padded, width), bf16)],
        compiler_params=pltpu.CompilerParams(vmem_limit_bytes=36 * MIB),
        cost_estimate=pl.CostEstimate(
            flops=2 * owners * slots * padded * width,
            bytes_accessed=2 * owners * slots * width,
            transcendentals=rows,
        ),
        name="finish_rows",
    )(*args)


def restore_kernel(slots, owner_ref, slot_ref, back_ref, best_ref, gap_ref):
    rows = owner_ref.shape[1]
    owners, _, width = back_ref.shape
    half = width // 2
    from_owner = to_bf16(owner_ref[...] == iota((owners, rows), 0))
    from_owner = jnp.concatenate([from_owner] * 3, axis=0)
    at_slot = slot_ref[...] == iota((slots, rows), 0)
    back = jnp.concatenate([back_ref[s] for s in range(owners)], axis=0)
    part0 = back.astype(bf16)
    rest = back - part0.astype(f32)
    part1 = rest.astype(bf16)
    part2 = (rest - part1.astype(f32)).astype(bf16)
    parts = jnp.concatenate([part0, part1, part2], axis=0)
    for i, ref in enumerate((best_ref, gap_ref)):
        table = lax.dot_general(
            parts[:, i * half : i * half + slots],
            from_owner,
            (((0,), (0,)), ((), ())),
            preferred_element_type=f32,
        )
        ref[...] = jnp.sum(jnp.where(at_slot, table, 0.0), axis=0, keepdims=True)


def restore(owner_row, slot_row, back, slots):
    return pl.pallas_call(
        functools.partial(restore_kernel, slots),
        out_shape=(jax.ShapeDtypeStruct(owner_row.shape, f32),) * 2,
        in_specs=[VMEM] * 3,
        out_specs=(VMEM, VMEM),
        compiler_params=pltpu.CompilerParams(vmem_limit_bytes=28 * MIB),
        name="restore_rows",
    )(owner_row, slot_row, back)


def exchange(x):
    return lax.all_to_all(x, "owner", split_axis=0, concat_axis=0, tiled=True)


def swap_together(blocks):
    owners = len(blocks)
    order = jnp.arange(owners, dtype=i32) ^ lax.axis_index("owner").astype(i32)
    arrived = exchange(jnp.stack(blocks)[order])[order]
    return [arrived[r] for r in range(owners)]


def swap_apart(blocks):
    pairs = [[(s, s ^ r) for s in range(len(blocks))] for r in range(len(blocks))]
    return blocks[:1] + [
        lax.ppermute(block, "owner", pair) for block, pair in zip(blocks[1:], pairs[1:])
    ]


def local(embeddings, cluster_ids):
    rows = embeddings.shape[0]
    owners = lax.axis_size("owner")
    clusters = CL_DEV * owners
    row_limit = 2 * rows // clusters
    most = round_up(CL_DEV * row_limit, STEP)
    usual = min(most, round_up(9 * rows // (8 * owners), STEP))
    few = owners <= MAX_PERMUTES
    me = lax.axis_index("owner").astype(i32).reshape(1)
    ids_row = cluster_ids.reshape(1, rows)
    counts, rank = count_rows(ids_row, owners, clusters)
    unit = unit_rows(embeddings)
    owner_row, slot_row, bound, total, load = assign(me, exchange(counts), rank)

    sent = list(range(1, owners))
    seen = [0] + sent
    sent = sent + [0]
    packs = [tuple(sent[:2]), tuple(sent[2:4])]
    packs += [tuple(sent[i : i + GROUP]) for i in range(4, owners, GROUP)]
    share = owners // 16 if owners >= 16 else 1
    groups, at = [], 0
    for size in (5, 4, 4, 2):
        groups.append(seen[at : at + size * share])
        at += size * share
    groups.append(seen[at:])

    def compare(slots, apart):
        blocks = [None] * owners
        slot_in = slot_row
        for partners in packs:
            packed = pack(me, owner_row, slot_in, unit, partners, slots)
            slot_in, *packed = lax.optimization_barrier((slot_in, *packed))
            for r, block in zip(partners, packed):
                blocks[r] = block
        arrived = swap_apart(blocks) if apart else swap_together(blocks)
        state = ([], [], [], None)
        for group in groups[:-1]:
            state = score(bound, [arrived[r] for r in group], group, state)
        last = groups[-1]
        answers = finish(
            me, bound, total, [arrived[r] for r in last], last, groups[:-1], state
        )
        return restore(owner_row, slot_row, exchange(answers), slots)

    best, gap = compare(usual, few)
    if usual < most:
        best, gap = lax.cond(
            load[0, 0] <= usual, lambda: (best, gap), lambda: compare(most, False)
        )
    return best.reshape(rows), gap.reshape(rows)


def solution(mesh):
    return jax.shard_map(
        local,
        mesh=mesh,
        in_specs=(P(("groups", "owner"), None), P(("groups", "owner"))),
        out_specs=(P(("groups", "owner")), P(("groups", "owner"))),
        check_vma=False,
    )
```

```python
import functools

import jax
import jax.numpy as jnp
from jax import lax
from jax.experimental import pallas as pl
from jax.experimental.pallas import tpu as pltpu
from jax.sharding import PartitionSpec as P

CL_DEV = 4
VARIANTS = 32
STEP = 16
TILE = 256
LANES = 128
MAX_PERMUTES = 8
RANKS = 4096
MIB = 1 << 20

epsilon = 1e-06
f32 = jnp.float32
bf16 = jnp.bfloat16
i32 = jnp.int32
VMEM = pl.BlockSpec(memory_space=pltpu.VMEM)
SMEM = pl.BlockSpec(memory_space=pltpu.SMEM)


def iota(shape, axis):
    return lax.broadcasted_iota(i32, shape, axis)


def round_up(value, unit):
    return -(-value // unit) * unit


def nt_dot(a, b):
    return lax.dot_general(a, b, (((1,), (1,)), ((), ())), preferred_element_type=f32)


def mm(a, b):
    return jnp.dot(a, b, preferred_element_type=f32)


def to_bf16(mask):
    return mask.astype(f32).astype(bf16)


def count_kernel(me_ref, ids0_ref, ids1_ref, counts_ref, rank0_ref, rank1_ref):
    rows = ids0_ref.shape[1]
    chips, _, clusters = counts_ref.shape
    core = me_ref[0] & 1
    label = iota((clusters, TILE), 0)
    upto = to_bf16(iota((TILE, TILE), 0) <= iota((TILE, TILE), 1))
    totals = []
    for ids_ref, rank_ref in ((ids0_ref, rank0_ref), (ids1_ref, rank1_ref)):
        total = jnp.zeros((clusters, 1), f32)
        for b in range(rows // TILE):
            at = slice(b * TILE, (b + 1) * TILE)
            hot = ids_ref[:, at] == label
            prefix = mm(to_bf16(hot), upto)
            rank = jnp.sum(jnp.where(hot, prefix + total - 1.0, 0.0), axis=0, keepdims=True)
            rank_ref[:, at] = ids_ref[:, at] * RANKS + rank.astype(i32)
            total = total + prefix[:, TILE - 1 :]
        totals.append(total)
    ahead0 = jnp.where(core == 1, totals[1], 0.0)
    ahead1 = jnp.where(core == 0, totals[0], 0.0)
    for ids_ref, rank_ref, ahead in (
        (ids0_ref, rank0_ref, ahead0),
        (ids1_ref, rank1_ref, ahead1),
    ):
        for b in range(rows // TILE):
            at = slice(b * TILE, (b + 1) * TILE)
            more = jnp.where(ids_ref[:, at] == label, ahead, 0.0)
            rank_ref[:, at] += jnp.sum(more, axis=0, keepdims=True).astype(i32)
    square = (clusters, clusters)
    eye = iota(square, 0) == iota(square, 1)
    both = totals[0] + totals[1]
    total_row = jnp.sum(jnp.where(eye, both, 0.0), axis=0, keepdims=True).astype(i32)
    for chip in range(chips):
        counts_ref[chip] = total_row


def count_rows(me, ids0, ids1, chips, clusters):
    return pl.pallas_call(
        count_kernel,
        out_shape=(
            jax.ShapeDtypeStruct((chips, 1, clusters), i32),
            jax.ShapeDtypeStruct(ids0.shape, i32),
            jax.ShapeDtypeStruct(ids0.shape, i32),
        ),
        in_specs=[SMEM, VMEM, VMEM],
        out_specs=(VMEM,) * 3,
        compiler_params=pltpu.CompilerParams(vmem_limit_bytes=16 * MIB),
        name="count_rows",
    )(me, ids0, ids1)


def assign_kernel(
    me_ref,
    counts_ref,
    rank0_ref,
    rank1_ref,
    owner0_ref,
    owner1_ref,
    slot0_ref,
    slot1_ref,
    bound_ref,
    total_ref,
    load_ref,
):
    chips, _, clusters = counts_ref.shape
    owners = 2 * chips
    rows = rank0_ref.shape[1]
    shift = owners.bit_length() - 1
    me = me_ref[0]
    chip = me >> 1
    count = jnp.concatenate([counts_ref[s].astype(f32) for s in range(chips)], axis=0)
    count16 = count.astype(bf16)
    square = (clusters, clusters)
    sub, lane = iota(square, 0), iota(square, 1)
    total_row = jnp.sum(count, axis=0, keepdims=True)
    total_col = jnp.sum(jnp.where(sub == lane, total_row, 0.0), axis=1, keepdims=True)
    tie = total_row == total_col
    outranks_col = (total_row > total_col) | (tie & (lane < sub))
    outranks_row = (total_col > total_row) | (tie & (sub < lane))
    rank_col = jnp.sum(outranks_col.astype(f32), axis=1, keepdims=True).astype(i32)
    rank_row = jnp.sum(outranks_row.astype(f32), axis=0, keepdims=True).astype(i32)

    def owner_of(rank, variant):
        layer = rank >> shift
        within = rank & (owners - 1)
        flip = jnp.zeros_like(variant)
        for p in range(1, CL_DEV):
            bits = (variant >> (p - 1)) & 1
            if p < CL_DEV - 1:
                bits = bits + 2 * ((variant >> (p + CL_DEV - 2)) & 1)
            flip = flip + jnp.where(layer == p, bits, 0)
        within = within ^ flip
        return jnp.where((layer & 1) == 1, owners - 1 - within, within)

    wide = (clusters, VARIANTS * owners)
    variant = iota(wide, 1) >> shift
    tried = owner_of(rank_col, variant) == (iota(wide, 1) & (owners - 1))
    load = jnp.max(mm(count16, to_bf16(tried)), axis=0, keepdims=True)
    by_variant = (VARIANTS, VARIANTS * owners)
    worst = jnp.max(
        jnp.where((iota(by_variant, 1) >> shift) == iota(by_variant, 0), load, 0.0),
        axis=1,
        keepdims=True,
    )
    best = jnp.min(worst, axis=0, keepdims=True)
    chosen = jnp.min(
        jnp.where(worst == best, iota((VARIANTS, 1), 0), VARIANTS), axis=0, keepdims=True
    )
    owner_col = owner_of(rank_col, chosen + jnp.zeros_like(rank_col))
    owner_row = owner_of(rank_row, chosen + jnp.zeros_like(rank_row))
    layer_col, layer_row = rank_col >> shift, rank_row >> shift
    load_ref[...] = jnp.broadcast_to(best, load_ref.shape).astype(i32)

    mine = jnp.sum(jnp.where(iota(count.shape, 0) == chip, count, 0.0), axis=0, keepdims=True)
    earlier = (owner_row == owner_col) & (layer_row < layer_col)
    offset_col = jnp.sum(jnp.where(earlier, mine, 0.0), axis=1, keepdims=True)
    for rank_ref, owner_ref, slot_ref in (
        (rank0_ref, owner0_ref, slot0_ref),
        (rank1_ref, owner1_ref, slot1_ref),
    ):
        hot = (rank_ref[...] // RANKS) == iota((clusters, rows), 0)
        owner_ref[...] = jnp.sum(
            jnp.where(hot, owner_col.astype(f32), 0.0), axis=0, keepdims=True
        ).astype(i32)
        slot_ref[...] = jnp.sum(jnp.where(hot, offset_col, 0.0), axis=0, keepdims=True).astype(
            i32
        ) + (rank_ref[...] & (RANKS - 1))

    select = (owner_col == me) & (layer_col <= iota((clusters, LANES), 1))
    turn = iota((chips, chips), 1) == (iota((chips, chips), 0) ^ chip)
    turned = mm(to_bf16(turn), count16).astype(bf16)
    bound_ref[...] = mm(turned, to_bf16(select))
    own = (owner_row == me) & (layer_row == iota((8, clusters), 0))
    total_ref[...] = jnp.broadcast_to(
        jnp.sum(jnp.where(own, total_row, 0.0), axis=1, keepdims=True), total_ref.shape
    )


def assign(me, counts, rank0, rank1):
    chips, _, clusters = counts.shape
    line = jax.ShapeDtypeStruct(rank0.shape, i32)
    return pl.pallas_call(
        assign_kernel,
        out_shape=(
            line,
            line,
            line,
            line,
            jax.ShapeDtypeStruct((chips, LANES), f32),
            jax.ShapeDtypeStruct((8, LANES), f32),
            jax.ShapeDtypeStruct((1, LANES), i32),
        ),
        in_specs=[SMEM, VMEM, VMEM, VMEM],
        out_specs=(VMEM,) * 7,
        compiler_params=pltpu.CompilerParams(vmem_limit_bytes=16 * MIB),
        name="assign",
    )(me, counts, rank0, rank1)


def pack_kernel(
    partner, me_ref, owner0_ref, owner1_ref, slot0_ref, slot1_ref, unit0_ref, unit1_ref, out_ref
):
    slots = out_ref.shape[0]
    rows = unit0_ref.shape[0]
    target = me_ref[0] ^ (2 * partner)
    slot = iota((slots, rows), 0)
    total = None
    for owner_ref, slot_ref, unit_ref in (
        (owner0_ref, slot0_ref, unit0_ref),
        (owner1_ref, slot1_ref, unit1_ref),
    ):
        key = jnp.where(owner_ref[...] == target, slot_ref[...], -1)
        part = mm(to_bf16(slot == key), unit_ref[...])
        total = part if total is None else total + part
    out_ref[...] = total.astype(bf16)


def pack(me, places, units, partner, slots):
    width = units[0].shape[1]
    return pl.pallas_call(
        functools.partial(pack_kernel, partner),
        out_shape=jax.ShapeDtypeStruct((slots, width), bf16),
        in_specs=[SMEM] + [VMEM] * 6,
        out_specs=VMEM,
        compiler_params=pltpu.CompilerParams(vmem_limit_bytes=24 * MIB),
        cost_estimate=pl.CostEstimate(flops=slots, bytes_accessed=slots, transcendentals=0),
        name="pack_rows",
    )(me, *places, *units)


def unit_kernel(rows_ref, unit_ref):
    def body(b, carry):
        at = pl.ds(pl.multiple_of(b * TILE, TILE), TILE)
        x = rows_ref[at, :].astype(f32)
        scale = lax.rsqrt(jnp.sum(x * x, axis=1, keepdims=True) + epsilon)
        unit_ref[at, :] = (x * scale).astype(bf16)
        return carry

    lax.fori_loop(0, rows_ref.shape[0] // TILE, body, 0)


def unit_rows(embeddings):
    rows, width = embeddings.shape
    return pl.pallas_call(
        unit_kernel,
        out_shape=jax.ShapeDtypeStruct((rows, width), bf16),
        in_specs=[VMEM],
        out_specs=VMEM,
        compiler_params=pltpu.CompilerParams(vmem_limit_bytes=16 * MIB),
        cost_estimate=pl.CostEstimate(
            flops=8 * rows * width, bytes_accessed=4 * rows * width, transcendentals=rows
        ),
        name="unit_rows",
    )(embeddings)


def cluster_lanes(bound_ref, partners, slots, width):
    lane = iota((1, width), 1).astype(f32)
    result = jnp.where(lane < len(partners) * slots, 0.0, -1.0)
    for i, r in enumerate(partners):
        for k in range(CL_DEV):
            first = bound_ref[r : r + 1, k : k + 1] + float(i * slots)
            result = result + ((lane >= first) & (lane < float((i + 1) * slots))).astype(f32)
    return result


def cluster_rows(bound_ref, r, slots):
    slot = iota((slots, LANES), 0).astype(f32)
    result = jnp.zeros((slots, LANES), f32)
    for k in range(CL_DEV):
        result = result + (slot >= bound_ref[r : r + 1, k : k + 1]).astype(f32)
    return result


def score_group(new_ref, new_cids, olds, cid_row, slots_new):
    padded = new_ref.shape[0]
    groups = padded // LANES
    new = new_ref[...]

    def folded(scores, cids, skip_same):
        rows = scores.shape[0]
        row = iota((rows, LANES), 0)
        lane = iota((rows, LANES), 1)
        best, cols = None, []
        for g in range(groups):
            at = slice(g * LANES, (g + 1) * LANES)
            allowed = cids == cid_row[:, at]
            if skip_same:
                allowed = allowed & (row != lane + g * LANES)
            part = jnp.where(allowed, scores[:, at], -1.0)
            best = part if best is None else jnp.maximum(best, part)
            cols.append(jnp.max(part, axis=0, keepdims=True))
        return best, cols

    columns = None
    results = []
    for unit_ref, acc_ref, cid_ref in olds:
        scores = nt_dot(unit_ref[...], new)
        best, cols = folded(scores, cid_ref[...], False)
        columns = cols if columns is None else [jnp.maximum(a, b) for a, b in zip(columns, cols)]
        results.append((scores, jnp.maximum(acc_ref[...], best)))
    scores = nt_dot(new[0:slots_new], new)
    best, _ = folded(scores, new_cids, True)
    if columns is not None:
        row = iota((slots_new, LANES), 0)
        lane = iota((slots_new, LANES), 1)
        for g, col in enumerate(columns):
            best = jnp.maximum(best, jnp.where(row == lane + g * LANES, col, -1.0))
    results.append((scores, best))
    return results


def member_sums(cid_row, new):
    hot = to_bf16(cid_row == iota((8, cid_row.shape[1]), 0).astype(f32))
    return mm(hot, new)


def score_kernel(slots, partners, olds, bound_ref, *refs):
    fresh = len(partners)
    raw_refs, refs = refs[:fresh], refs[fresh:]
    old_refs = [refs[3 * i : 3 * i + 3] for i in range(olds)]
    refs = refs[3 * olds :]
    if olds:
        sums_ref, refs = refs[0], refs[1:]
    unit_ref, acc_ref, cid_ref, sums_out = refs[:4]
    old_accs = refs[4 : 4 + olds]
    new_ref = refs[4 + olds]
    rows = fresh * slots
    for i, r in enumerate(partners):
        at = slice(i * slots, (i + 1) * slots)
        new_ref[at, :] = raw_refs[i][...]
        cid_ref[at, :] = cluster_rows(bound_ref, r, slots)
    padded = new_ref.shape[0]
    if padded > rows:
        new_ref[rows:, :] = jnp.zeros((padded - rows, new_ref.shape[1]), bf16)
    unit_ref[...] = new_ref[0:rows, :]
    cid_row = cluster_lanes(bound_ref, partners, slots, padded)
    results = score_group(new_ref, cid_ref[...], old_refs, cid_row, rows)
    for (_, best), ref in zip(results, list(old_accs) + [acc_ref]):
        ref[...] = best
    sums = member_sums(cid_row, new_ref[...])
    sums_out[...] = sums + sums_ref[...] if olds else sums


def score(bound, blocks, partners, state):
    slots, width = blocks[0].shape
    units, accs, cids, sums = state
    rows = len(blocks) * slots
    padded = round_up(rows, LANES)
    old = [x for group in zip(units, accs, cids) for x in group]
    old_rows = sum(u.shape[0] for u in units)
    acc_shapes = [jax.ShapeDtypeStruct(a.shape, f32) for a in accs]
    out_shape = (
        jax.ShapeDtypeStruct((rows, width), bf16),
        jax.ShapeDtypeStruct((rows, LANES), f32),
        jax.ShapeDtypeStruct((rows, LANES), f32),
        jax.ShapeDtypeStruct((8, width), f32),
        *acc_shapes,
    )
    args = [bound, *blocks, *old] + ([sums] if units else [])
    out = pl.pallas_call(
        functools.partial(score_kernel, slots, partners, len(units)),
        out_shape=out_shape,
        in_specs=[VMEM] * len(args),
        out_specs=(VMEM,) * len(out_shape),
        scratch_shapes=[pltpu.VMEM((padded, width), bf16)],
        compiler_params=pltpu.CompilerParams(vmem_limit_bytes=(36 if slots < 400 else 58) * MIB),
        cost_estimate=pl.CostEstimate(
            flops=2 * (old_rows + rows) * padded * width,
            bytes_accessed=2 * (old_rows + rows) * width,
            transcendentals=rows,
        ),
        name="score_rows",
    )(*args)
    return units + [out[0]], list(out[4:]) + [out[1]], cids + [out[2]], out[3]


def finish_kernel(slots, partners, earlier, olds, me_ref, bound_ref, total_ref, *refs):
    fresh = len(partners)
    raw_refs, refs = refs[:fresh], refs[fresh:]
    old_refs = [refs[3 * i : 3 * i + 3] for i in range(olds)]
    sums_ref, out_ref, new_ref = refs[3 * olds :]
    chip = me_ref[0] >> 1
    rows = fresh * slots
    padded, width = new_ref.shape
    new_ref[rows:, :] = jnp.zeros((padded - rows, width), bf16)
    pieces = []
    for i, r in enumerate(partners):
        new_ref[i * slots : (i + 1) * slots, :] = raw_refs[i][...]
        pieces.append(cluster_rows(bound_ref, r, slots))
    new_cids = jnp.concatenate(pieces, axis=0)
    cid_row = cluster_lanes(bound_ref, partners, slots, padded)
    sums = sums_ref[...] + member_sums(cid_row, new_ref[...])
    centroid = (sums / jnp.maximum(total_ref[:, 0:1], 1.0)).astype(bf16)
    centroid = jnp.concatenate([centroid, jnp.zeros_like(centroid)], axis=0)
    new_ref[rows : rows + STEP, :] = centroid
    results = score_group(new_ref, new_cids, old_refs, cid_row, rows)
    half = out_ref.shape[2] // 2
    group, within = rows // LANES, rows % LANES
    eye = iota((slots, half), 0) == iota((slots, half), 1)
    all_cids = [old[2][...] for old in old_refs] + [new_cids]
    for (scores, acc), cids, names in zip(results, all_cids, earlier + [partners]):
        best = jnp.max(acc, axis=1, keepdims=True)
        lane = iota(cids.shape, 1).astype(f32)
        dots = scores[:, group * LANES : (group + 1) * LANES]
        gap = 1.0 - jnp.sum(
            jnp.where(lane == cids + float(within), dots, 0.0), axis=1, keepdims=True
        )
        for i, r in enumerate(names):
            at = slice(i * slots, (i + 1) * slots)
            for j, col in enumerate((best, gap)):
                line = jnp.sum(jnp.where(eye, col[at], 0.0), axis=0, keepdims=True)
                for core in range(2):
                    device = 2 * (r ^ chip) + core
                    out_ref[device, :, j * half : (j + 1) * half] = line


def finish(me, bound, total, blocks, partners, earlier, state):
    slots, width = blocks[0].shape
    owners = 2 * bound.shape[0]
    units, accs, cids, sums = state
    rows = len(blocks) * slots
    padded = round_up(rows + STEP, LANES)
    old = [x for group in zip(units, accs, cids) for x in group]
    args = [me, bound, total, *blocks, *old, sums]
    return pl.pallas_call(
        functools.partial(finish_kernel, slots, partners, earlier, len(units)),
        out_shape=jax.ShapeDtypeStruct((owners, 1, 2 * round_up(slots, LANES)), f32),
        in_specs=[SMEM] + [VMEM] * (len(args) - 1),
        out_specs=VMEM,
        scratch_shapes=[pltpu.VMEM((padded, width), bf16)],
        compiler_params=pltpu.CompilerParams(vmem_limit_bytes=(36 if slots < 400 else 58) * MIB),
        cost_estimate=pl.CostEstimate(
            flops=2 * owners * slots * padded * width,
            bytes_accessed=2 * owners * slots * width,
            transcendentals=rows,
        ),
        name="finish_rows",
    )(*args)


def restore_kernel(slots, owner_ref, slot_ref, back_ref, best_ref, gap_ref):
    rows = owner_ref.shape[1]
    owners, _, width = back_ref.shape
    half = width // 2
    from_owner = to_bf16(owner_ref[...] == iota((owners, rows), 0))
    from_owner = jnp.concatenate([from_owner] * 3, axis=0)
    at_slot = slot_ref[...] == iota((slots, rows), 0)
    back = jnp.concatenate([back_ref[s] for s in range(owners)], axis=0)
    part0 = back.astype(bf16)
    rest = back - part0.astype(f32)
    part1 = rest.astype(bf16)
    part2 = (rest - part1.astype(f32)).astype(bf16)
    parts = jnp.concatenate([part0, part1, part2], axis=0)
    for i, ref in enumerate((best_ref, gap_ref)):
        table = lax.dot_general(
            parts[:, i * half : i * half + slots],
            from_owner,
            (((0,), (0,)), ((), ())),
            preferred_element_type=f32,
        )
        ref[...] = jnp.sum(jnp.where(at_slot, table, 0.0), axis=0, keepdims=True)


def restore(owner_row, slot_row, back, slots):
    return pl.pallas_call(
        functools.partial(restore_kernel, slots),
        out_shape=(jax.ShapeDtypeStruct(owner_row.shape, f32),) * 2,
        in_specs=[VMEM] * 3,
        out_specs=(VMEM, VMEM),
        compiler_params=pltpu.CompilerParams(vmem_limit_bytes=28 * MIB),
        name="restore_rows",
    )(owner_row, slot_row, back)


def exchange(x):
    return lax.all_to_all(x, "owner", split_axis=0, concat_axis=0, tiled=True)


def exchange_chips(x):
    chips = lax.axis_size("owner") // 2
    cores = [[2 * chip + core for chip in range(chips)] for core in range(2)]
    return lax.all_to_all(
        x, "owner", split_axis=0, concat_axis=0, axis_index_groups=cores, tiled=True
    )


def swap(block, r):
    owners = lax.axis_size("owner")
    return lax.ppermute(block, "owner", [(s, s ^ (2 * r)) for s in range(owners)])


def swap_together(blocks):
    chips = len(blocks)
    order = jnp.arange(chips, dtype=i32) ^ (lax.axis_index("owner").astype(i32) >> 1)
    arrived = exchange_chips(jnp.stack(blocks)[order])[order]
    return [arrived[r] for r in range(chips)]


def swap_cores(x):
    owners = lax.axis_size("owner")
    return lax.ppermute(x, "owner", [(s, s ^ 1) for s in range(owners)])


def local(embeddings, cluster_ids):
    rows = embeddings.shape[0]
    owners = lax.axis_size("owner")
    chips = owners // 2
    clusters = CL_DEV * owners
    row_limit = 2 * rows // clusters
    most = round_up(2 * CL_DEV * row_limit, STEP)
    usual = min(most, round_up(17 * rows // (8 * owners), STEP))
    few = chips <= MAX_PERMUTES
    me = lax.axis_index("owner").astype(i32).reshape(1)
    ids0 = cluster_ids.reshape(1, rows)
    ids1 = swap_cores(ids0)
    other = swap_cores(embeddings)
    counts, rank0, rank1 = count_rows(me, ids0, ids1, chips, clusters)
    counts = exchange_chips(counts)
    units = (unit_rows(embeddings), unit_rows(other))
    *places, bound, total, load = assign(me, counts, rank0, rank1)
    owner_row, slot_row = places[0], places[2]

    half = chips // 2
    far = list(range(chips - 1, half - 1, -1))
    near = list(range(half - 1, 0, -1))
    sent = far[:2] + near + far[2:] + [0]
    share = max(half // 4, 1)
    groups = [[0] + near, far[: 2 * share], far[2 * share : 3 * share], far[3 * share :]]

    def compare(slots, apart):
        blocks = [None] * chips
        here = list(places)
        for r in sent:
            blocks[r] = pack(me, here, units, r, slots)
            here[0], blocks[r] = lax.optimization_barrier((here[0], blocks[r]))
        if apart:
            arrived = blocks[:1] + [None] * (chips - 1)
            for r in sent[:-1]:
                if r in far[2:]:
                    before = far[far.index(r) - 2]
                    blocks[r], arrived[before] = lax.optimization_barrier(
                        (blocks[r], arrived[before])
                    )
                arrived[r] = swap(blocks[r], r)
        else:
            arrived = swap_together(blocks)
        state = ([], [], [], None)
        for group in groups[:-1]:
            state = score(bound, [arrived[r] for r in group], group, state)
        last = groups[-1]
        answers = finish(
            me, bound, total, [arrived[r] for r in last], last, groups[:-1], state
        )
        return restore(owner_row, slot_row, exchange(answers), slots)

    best, gap = compare(usual, few)
    if usual < most:
        best, gap = lax.cond(
            load[0, 0] <= usual, lambda: (best, gap), lambda: compare(most, False)
        )
    return best.reshape(rows), gap.reshape(rows)


def solution(mesh):
    return jax.shard_map(
        local,
        mesh=mesh,
        in_specs=(P(("groups", "owner"), None), P(("groups", "owner"))),
        out_specs=(P(("groups", "owner")), P(("groups", "owner"))),
        check_vma=False,
    )
```

```python
import functools

import jax
import jax.numpy as jnp
from jax import lax
from jax.experimental import pallas as pl
from jax.experimental.pallas import tpu as pltpu
from jax.sharding import PartitionSpec as P

CL_DEV = 4
VARIANTS = 32
STEP = 16
TILE = 256
LANES = 128
MAX_PERMUTES = 8
RANKS = 4096
MIB = 1 << 20

epsilon = 1e-06
f32 = jnp.float32
bf16 = jnp.bfloat16
i32 = jnp.int32
VMEM = pl.BlockSpec(memory_space=pltpu.VMEM)
SMEM = pl.BlockSpec(memory_space=pltpu.SMEM)


def iota(shape, axis):
    return lax.broadcasted_iota(i32, shape, axis)


def round_up(value, unit):
    return -(-value // unit) * unit


def nt_dot(a, b):
    return lax.dot_general(a, b, (((1,), (1,)), ((), ())), preferred_element_type=f32)


def mm(a, b):
    return jnp.dot(a, b, preferred_element_type=f32)


def to_bf16(mask):
    return mask.astype(f32).astype(bf16)


def count_kernel(me_ref, ids0_ref, ids1_ref, counts_ref, rank0_ref, rank1_ref):
    rows = ids0_ref.shape[1]
    chips, _, clusters = counts_ref.shape
    core = me_ref[0] & 1
    label = iota((clusters, TILE), 0)
    upto = to_bf16(iota((TILE, TILE), 0) <= iota((TILE, TILE), 1))
    totals = []
    for ids_ref, rank_ref in ((ids0_ref, rank0_ref), (ids1_ref, rank1_ref)):
        total = jnp.zeros((clusters, 1), f32)
        for b in range(rows // TILE):
            at = slice(b * TILE, (b + 1) * TILE)
            hot = ids_ref[:, at] == label
            prefix = mm(to_bf16(hot), upto)
            rank = jnp.sum(jnp.where(hot, prefix + total - 1.0, 0.0), axis=0, keepdims=True)
            rank_ref[:, at] = ids_ref[:, at] * RANKS + rank.astype(i32)
            total = total + prefix[:, TILE - 1 :]
        totals.append(total)
    ahead0 = jnp.where(core == 1, totals[1], 0.0)
    ahead1 = jnp.where(core == 0, totals[0], 0.0)
    for ids_ref, rank_ref, ahead in (
        (ids0_ref, rank0_ref, ahead0),
        (ids1_ref, rank1_ref, ahead1),
    ):
        for b in range(rows // TILE):
            at = slice(b * TILE, (b + 1) * TILE)
            more = jnp.where(ids_ref[:, at] == label, ahead, 0.0)
            rank_ref[:, at] += jnp.sum(more, axis=0, keepdims=True).astype(i32)
    square = (clusters, clusters)
    eye = iota(square, 0) == iota(square, 1)
    both = totals[0] + totals[1]
    total_row = jnp.sum(jnp.where(eye, both, 0.0), axis=0, keepdims=True).astype(i32)
    for chip in range(chips):
        counts_ref[chip] = total_row


def count_rows(me, ids0, ids1, chips, clusters):
    return pl.pallas_call(
        count_kernel,
        out_shape=(
            jax.ShapeDtypeStruct((chips, 1, clusters), i32),
            jax.ShapeDtypeStruct(ids0.shape, i32),
            jax.ShapeDtypeStruct(ids0.shape, i32),
        ),
        in_specs=[SMEM, VMEM, VMEM],
        out_specs=(VMEM,) * 3,
        compiler_params=pltpu.CompilerParams(vmem_limit_bytes=16 * MIB),
        name="count_rows",
    )(me, ids0, ids1)


def assign_kernel(
    me_ref,
    counts_ref,
    rank0_ref,
    rank1_ref,
    owner0_ref,
    owner1_ref,
    slot0_ref,
    slot1_ref,
    bound_ref,
    total_ref,
    load_ref,
):
    chips, _, clusters = counts_ref.shape
    owners = 2 * chips
    rows = rank0_ref.shape[1]
    shift = owners.bit_length() - 1
    me = me_ref[0]
    chip = me >> 1
    count = jnp.concatenate([counts_ref[s].astype(f32) for s in range(chips)], axis=0)
    count16 = count.astype(bf16)
    square = (clusters, clusters)
    sub, lane = iota(square, 0), iota(square, 1)
    total_row = jnp.sum(count, axis=0, keepdims=True)
    total_col = jnp.sum(jnp.where(sub == lane, total_row, 0.0), axis=1, keepdims=True)
    tie = total_row == total_col
    outranks_col = (total_row > total_col) | (tie & (lane < sub))
    outranks_row = (total_col > total_row) | (tie & (sub < lane))
    rank_col = jnp.sum(outranks_col.astype(f32), axis=1, keepdims=True).astype(i32)
    rank_row = jnp.sum(outranks_row.astype(f32), axis=0, keepdims=True).astype(i32)

    def owner_of(rank, variant):
        layer = rank >> shift
        within = rank & (owners - 1)
        flip = jnp.zeros_like(variant)
        for p in range(1, CL_DEV):
            bits = (variant >> (p - 1)) & 1
            if p < CL_DEV - 1:
                bits = bits + 2 * ((variant >> (p + CL_DEV - 2)) & 1)
            flip = flip + jnp.where(layer == p, bits, 0)
        within = within ^ flip
        return jnp.where((layer & 1) == 1, owners - 1 - within, within)

    wide = (clusters, VARIANTS * owners)
    variant = iota(wide, 1) >> shift
    tried = owner_of(rank_col, variant) == (iota(wide, 1) & (owners - 1))
    load = jnp.max(mm(count16, to_bf16(tried)), axis=0, keepdims=True)
    by_variant = (VARIANTS, VARIANTS * owners)
    worst = jnp.max(
        jnp.where((iota(by_variant, 1) >> shift) == iota(by_variant, 0), load, 0.0),
        axis=1,
        keepdims=True,
    )
    best = jnp.min(worst, axis=0, keepdims=True)
    chosen = jnp.min(
        jnp.where(worst == best, iota((VARIANTS, 1), 0), VARIANTS), axis=0, keepdims=True
    )
    owner_col = owner_of(rank_col, chosen + jnp.zeros_like(rank_col))
    owner_row = owner_of(rank_row, chosen + jnp.zeros_like(rank_row))
    layer_col, layer_row = rank_col >> shift, rank_row >> shift
    load_ref[...] = jnp.broadcast_to(best, load_ref.shape).astype(i32)

    mine = jnp.sum(jnp.where(iota(count.shape, 0) == chip, count, 0.0), axis=0, keepdims=True)
    earlier = (owner_row == owner_col) & (layer_row < layer_col)
    offset_col = jnp.sum(jnp.where(earlier, mine, 0.0), axis=1, keepdims=True)
    for rank_ref, owner_ref, slot_ref in (
        (rank0_ref, owner0_ref, slot0_ref),
        (rank1_ref, owner1_ref, slot1_ref),
    ):
        hot = (rank_ref[...] // RANKS) == iota((clusters, rows), 0)
        owner_ref[...] = jnp.sum(
            jnp.where(hot, owner_col.astype(f32), 0.0), axis=0, keepdims=True
        ).astype(i32)
        slot_ref[...] = jnp.sum(jnp.where(hot, offset_col, 0.0), axis=0, keepdims=True).astype(
            i32
        ) + (rank_ref[...] & (RANKS - 1))

    select = (owner_col == me) & (layer_col <= iota((clusters, LANES), 1))
    turn = iota((chips, chips), 1) == (iota((chips, chips), 0) ^ chip)
    turned = mm(to_bf16(turn), count16).astype(bf16)
    bound_ref[...] = mm(turned, to_bf16(select))
    own = (owner_row == me) & (layer_row == iota((8, clusters), 0))
    total_ref[...] = jnp.broadcast_to(
        jnp.sum(jnp.where(own, total_row, 0.0), axis=1, keepdims=True), total_ref.shape
    )


def assign(me, counts, rank0, rank1):
    chips, _, clusters = counts.shape
    line = jax.ShapeDtypeStruct(rank0.shape, i32)
    return pl.pallas_call(
        assign_kernel,
        out_shape=(
            line,
            line,
            line,
            line,
            jax.ShapeDtypeStruct((chips, LANES), f32),
            jax.ShapeDtypeStruct((8, LANES), f32),
            jax.ShapeDtypeStruct((1, LANES), i32),
        ),
        in_specs=[SMEM, VMEM, VMEM, VMEM],
        out_specs=(VMEM,) * 7,
        compiler_params=pltpu.CompilerParams(vmem_limit_bytes=16 * MIB),
        name="assign",
    )(me, counts, rank0, rank1)


def pack_kernel(
    partner, me_ref, owner0_ref, owner1_ref, slot0_ref, slot1_ref, unit0_ref, unit1_ref, out_ref
):
    slots = out_ref.shape[0]
    rows = unit0_ref.shape[0]
    target = me_ref[0] ^ (2 * partner)
    slot = iota((slots, rows), 0)
    total = None
    for owner_ref, slot_ref, unit_ref in (
        (owner0_ref, slot0_ref, unit0_ref),
        (owner1_ref, slot1_ref, unit1_ref),
    ):
        key = jnp.where(owner_ref[...] == target, slot_ref[...], -1)
        part = mm(to_bf16(slot == key), unit_ref[...])
        total = part if total is None else total + part
    out_ref[...] = total.astype(bf16)


def pack(me, places, units, partner, slots):
    width = units[0].shape[1]
    return pl.pallas_call(
        functools.partial(pack_kernel, partner),
        out_shape=jax.ShapeDtypeStruct((slots, width), bf16),
        in_specs=[SMEM] + [VMEM] * 6,
        out_specs=VMEM,
        compiler_params=pltpu.CompilerParams(vmem_limit_bytes=24 * MIB),
        cost_estimate=pl.CostEstimate(flops=slots, bytes_accessed=slots, transcendentals=0),
        name="pack_rows",
    )(me, *places, *units)


def unit_kernel(rows_ref, unit_ref):
    def body(b, carry):
        at = pl.ds(pl.multiple_of(b * TILE, TILE), TILE)
        x = rows_ref[at, :].astype(f32)
        scale = lax.rsqrt(jnp.sum(x * x, axis=1, keepdims=True) + epsilon)
        unit_ref[at, :] = (x * scale).astype(bf16)
        return carry

    lax.fori_loop(0, rows_ref.shape[0] // TILE, body, 0)


def unit_rows(embeddings):
    rows, width = embeddings.shape
    return pl.pallas_call(
        unit_kernel,
        out_shape=jax.ShapeDtypeStruct((rows, width), bf16),
        in_specs=[VMEM],
        out_specs=VMEM,
        compiler_params=pltpu.CompilerParams(vmem_limit_bytes=16 * MIB),
        cost_estimate=pl.CostEstimate(
            flops=8 * rows * width, bytes_accessed=4 * rows * width, transcendentals=rows
        ),
        name="unit_rows",
    )(embeddings)


def cluster_lanes(bound_ref, partners, slots, width):
    lane = iota((1, width), 1).astype(f32)
    result = jnp.where(lane < len(partners) * slots, 0.0, -1.0)
    for i, r in enumerate(partners):
        for k in range(CL_DEV):
            first = bound_ref[r : r + 1, k : k + 1] + float(i * slots)
            result = result + ((lane >= first) & (lane < float((i + 1) * slots))).astype(f32)
    return result


def cluster_rows(bound_ref, r, slots):
    slot = iota((slots, LANES), 0).astype(f32)
    result = jnp.zeros((slots, LANES), f32)
    for k in range(CL_DEV):
        result = result + (slot >= bound_ref[r : r + 1, k : k + 1]).astype(f32)
    return result


def score_group(new_ref, new_cids, olds, cid_row, slots_new):
    padded = new_ref.shape[0]
    groups = padded // LANES
    new = new_ref[...]

    def folded(scores, cids, skip_same):
        rows = scores.shape[0]
        row = iota((rows, LANES), 0)
        lane = iota((rows, LANES), 1)
        best, cols = None, []
        for g in range(groups):
            at = slice(g * LANES, (g + 1) * LANES)
            allowed = cids == cid_row[:, at]
            if skip_same:
                allowed = allowed & (row != lane + g * LANES)
            part = jnp.where(allowed, scores[:, at], -1.0)
            best = part if best is None else jnp.maximum(best, part)
            cols.append(jnp.max(part, axis=0, keepdims=True))
        return best, cols

    columns = None
    results = []
    for unit_ref, acc_ref, cid_ref in olds:
        scores = nt_dot(unit_ref[...], new)
        best, cols = folded(scores, cid_ref[...], False)
        columns = cols if columns is None else [jnp.maximum(a, b) for a, b in zip(columns, cols)]
        results.append((scores, jnp.maximum(acc_ref[...], best)))
    scores = nt_dot(new[0:slots_new], new)
    best, _ = folded(scores, new_cids, True)
    if columns is not None:
        row = iota((slots_new, LANES), 0)
        lane = iota((slots_new, LANES), 1)
        for g, col in enumerate(columns):
            best = jnp.maximum(best, jnp.where(row == lane + g * LANES, col, -1.0))
    results.append((scores, best))
    return results


def member_sums(cid_row, new):
    hot = to_bf16(cid_row == iota((8, cid_row.shape[1]), 0).astype(f32))
    return mm(hot, new)


def score_kernel(slots, partners, olds, bound_ref, *refs):
    fresh = len(partners)
    raw_refs, refs = refs[:fresh], refs[fresh:]
    old_refs = [refs[3 * i : 3 * i + 3] for i in range(olds)]
    refs = refs[3 * olds :]
    if olds:
        sums_ref, refs = refs[0], refs[1:]
    unit_ref, acc_ref, cid_ref, sums_out = refs[:4]
    old_accs = refs[4 : 4 + olds]
    new_ref = refs[4 + olds]
    rows = fresh * slots
    for i, r in enumerate(partners):
        at = slice(i * slots, (i + 1) * slots)
        new_ref[at, :] = raw_refs[i][...]
        cid_ref[at, :] = cluster_rows(bound_ref, r, slots)
    padded = new_ref.shape[0]
    if padded > rows:
        new_ref[rows:, :] = jnp.zeros((padded - rows, new_ref.shape[1]), bf16)
    unit_ref[...] = new_ref[0:rows, :]
    cid_row = cluster_lanes(bound_ref, partners, slots, padded)
    results = score_group(new_ref, cid_ref[...], old_refs, cid_row, rows)
    for (_, best), ref in zip(results, list(old_accs) + [acc_ref]):
        ref[...] = best
    sums = member_sums(cid_row, new_ref[...])
    sums_out[...] = sums + sums_ref[...] if olds else sums


def score(bound, blocks, partners, state):
    slots, width = blocks[0].shape
    units, accs, cids, sums = state
    rows = len(blocks) * slots
    padded = round_up(rows, LANES)
    old = [x for group in zip(units, accs, cids) for x in group]
    old_rows = sum(u.shape[0] for u in units)
    acc_shapes = [jax.ShapeDtypeStruct(a.shape, f32) for a in accs]
    out_shape = (
        jax.ShapeDtypeStruct((rows, width), bf16),
        jax.ShapeDtypeStruct((rows, LANES), f32),
        jax.ShapeDtypeStruct((rows, LANES), f32),
        jax.ShapeDtypeStruct((8, width), f32),
        *acc_shapes,
    )
    args = [bound, *blocks, *old] + ([sums] if units else [])
    out = pl.pallas_call(
        functools.partial(score_kernel, slots, partners, len(units)),
        out_shape=out_shape,
        in_specs=[VMEM] * len(args),
        out_specs=(VMEM,) * len(out_shape),
        scratch_shapes=[pltpu.VMEM((padded, width), bf16)],
        compiler_params=pltpu.CompilerParams(vmem_limit_bytes=(36 if slots < 400 else 58) * MIB),
        cost_estimate=pl.CostEstimate(
            flops=2 * (old_rows + rows) * padded * width,
            bytes_accessed=2 * (old_rows + rows) * width,
            transcendentals=rows,
        ),
        name="score_rows",
    )(*args)
    return units + [out[0]], list(out[4:]) + [out[1]], cids + [out[2]], out[3]


def finish_kernel(slots, partners, earlier, olds, me_ref, bound_ref, total_ref, *refs):
    fresh = len(partners)
    raw_refs, refs = refs[:fresh], refs[fresh:]
    old_refs = [refs[3 * i : 3 * i + 3] for i in range(olds)]
    sums_ref, out_ref, new_ref = refs[3 * olds :]
    chip = me_ref[0] >> 1
    rows = fresh * slots
    padded, width = new_ref.shape
    new_ref[rows:, :] = jnp.zeros((padded - rows, width), bf16)
    pieces = []
    for i, r in enumerate(partners):
        new_ref[i * slots : (i + 1) * slots, :] = raw_refs[i][...]
        pieces.append(cluster_rows(bound_ref, r, slots))
    new_cids = jnp.concatenate(pieces, axis=0)
    cid_row = cluster_lanes(bound_ref, partners, slots, padded)
    sums = sums_ref[...] + member_sums(cid_row, new_ref[...])
    centroid = (sums / jnp.maximum(total_ref[:, 0:1], 1.0)).astype(bf16)
    centroid = jnp.concatenate([centroid, jnp.zeros_like(centroid)], axis=0)
    new_ref[rows : rows + STEP, :] = centroid
    results = score_group(new_ref, new_cids, old_refs, cid_row, rows)
    half = out_ref.shape[2] // 2
    group, within = rows // LANES, rows % LANES
    eye = iota((slots, half), 0) == iota((slots, half), 1)
    all_cids = [old[2][...] for old in old_refs] + [new_cids]
    for (scores, acc), cids, names in zip(results, all_cids, earlier + [partners]):
        best = jnp.max(acc, axis=1, keepdims=True)
        lane = iota(cids.shape, 1).astype(f32)
        dots = scores[:, group * LANES : (group + 1) * LANES]
        gap = 1.0 - jnp.sum(
            jnp.where(lane == cids + float(within), dots, 0.0), axis=1, keepdims=True
        )
        for i, r in enumerate(names):
            at = slice(i * slots, (i + 1) * slots)
            for j, col in enumerate((best, gap)):
                line = jnp.sum(jnp.where(eye, col[at], 0.0), axis=0, keepdims=True)
                for core in range(2):
                    device = 2 * (r ^ chip) + core
                    out_ref[device, :, j * half : (j + 1) * half] = line


def finish(me, bound, total, blocks, partners, earlier, state):
    slots, width = blocks[0].shape
    owners = 2 * bound.shape[0]
    units, accs, cids, sums = state
    rows = len(blocks) * slots
    padded = round_up(rows + STEP, LANES)
    old = [x for group in zip(units, accs, cids) for x in group]
    args = [me, bound, total, *blocks, *old, sums]
    return pl.pallas_call(
        functools.partial(finish_kernel, slots, partners, earlier, len(units)),
        out_shape=jax.ShapeDtypeStruct((owners, 1, 2 * round_up(slots, LANES)), f32),
        in_specs=[SMEM] + [VMEM] * (len(args) - 1),
        out_specs=VMEM,
        scratch_shapes=[pltpu.VMEM((padded, width), bf16)],
        compiler_params=pltpu.CompilerParams(vmem_limit_bytes=(36 if slots < 400 else 58) * MIB),
        cost_estimate=pl.CostEstimate(
            flops=2 * owners * slots * padded * width,
            bytes_accessed=2 * owners * slots * width,
            transcendentals=rows,
        ),
        name="finish_rows",
    )(*args)


def restore_kernel(slots, owner_ref, slot_ref, back_ref, best_ref, gap_ref):
    rows = owner_ref.shape[1]
    owners, _, width = back_ref.shape
    half = width // 2
    from_owner = to_bf16(owner_ref[...] == iota((owners, rows), 0))
    from_owner = jnp.concatenate([from_owner] * 3, axis=0)
    at_slot = slot_ref[...] == iota((slots, rows), 0)
    back = jnp.concatenate([back_ref[s] for s in range(owners)], axis=0)
    part0 = back.astype(bf16)
    rest = back - part0.astype(f32)
    part1 = rest.astype(bf16)
    part2 = (rest - part1.astype(f32)).astype(bf16)
    parts = jnp.concatenate([part0, part1, part2], axis=0)
    for i, ref in enumerate((best_ref, gap_ref)):
        table = lax.dot_general(
            parts[:, i * half : i * half + slots],
            from_owner,
            (((0,), (0,)), ((), ())),
            preferred_element_type=f32,
        )
        ref[...] = jnp.sum(jnp.where(at_slot, table, 0.0), axis=0, keepdims=True)


def restore(owner_row, slot_row, back, slots):
    return pl.pallas_call(
        functools.partial(restore_kernel, slots),
        out_shape=(jax.ShapeDtypeStruct(owner_row.shape, f32),) * 2,
        in_specs=[VMEM] * 3,
        out_specs=(VMEM, VMEM),
        compiler_params=pltpu.CompilerParams(vmem_limit_bytes=28 * MIB),
        name="restore_rows",
    )(owner_row, slot_row, back)


def exchange(x):
    return lax.all_to_all(x, "owner", split_axis=0, concat_axis=0, tiled=True)


def exchange_chips(x):
    chips = lax.axis_size("owner") // 2
    cores = [[2 * chip + core for chip in range(chips)] for core in range(2)]
    return lax.all_to_all(
        x, "owner", split_axis=0, concat_axis=0, axis_index_groups=cores, tiled=True
    )


def swap(block, r):
    owners = lax.axis_size("owner")
    return lax.ppermute(block, "owner", [(s, s ^ (2 * r)) for s in range(owners)])


def swap_together(blocks):
    chips = len(blocks)
    order = jnp.arange(chips, dtype=i32) ^ (lax.axis_index("owner").astype(i32) >> 1)
    arrived = exchange_chips(jnp.stack(blocks)[order])[order]
    return [arrived[r] for r in range(chips)]


def swap_cores(x):
    owners = lax.axis_size("owner")
    return lax.ppermute(x, "owner", [(s, s ^ 1) for s in range(owners)])


def local(embeddings, cluster_ids):
    rows = embeddings.shape[0]
    owners = lax.axis_size("owner")
    chips = owners // 2
    clusters = CL_DEV * owners
    row_limit = 2 * rows // clusters
    most = round_up(2 * CL_DEV * row_limit, STEP)
    usual = min(most, round_up(17 * rows // (8 * owners), STEP))
    few = chips <= MAX_PERMUTES
    me = lax.axis_index("owner").astype(i32).reshape(1)
    ids0 = cluster_ids.reshape(1, rows)
    ids1 = swap_cores(ids0)
    mine, ids1 = lax.optimization_barrier((embeddings, ids1))
    other = swap_cores(mine)
    counts, rank0, rank1 = count_rows(me, ids0, ids1, chips, clusters)
    counts = exchange_chips(counts)
    units = (unit_rows(embeddings), unit_rows(other))
    counts, *units = lax.optimization_barrier((counts, *units))
    *places, bound, total, load = assign(me, counts, rank0, rank1)
    owner_row, slot_row = places[0], places[2]

    half = chips // 2
    far = list(range(chips - 1, half - 1, -1))
    near = list(range(half - 1, 0, -1))
    sent = near + far + [0]
    share = max(half // 4, 1)
    groups = [[0] + near, far[: 2 * share], far[2 * share : 3 * share], far[3 * share :]]

    def compare(slots, apart):
        blocks = [None] * chips
        here = list(places)
        for r in sent:
            blocks[r] = pack(me, here, units, r, slots)
            here[0], blocks[r] = lax.optimization_barrier((here[0], blocks[r]))
        if apart:
            arrived = blocks[:1] + [None] * (chips - 1)
            for r in sent[:-1]:
                if r in far[2:]:
                    before = near[far.index(r) - 2]
                    blocks[r], arrived[before] = lax.optimization_barrier(
                        (blocks[r], arrived[before])
                    )
                arrived[r] = swap(blocks[r], r)
        else:
            arrived = swap_together(blocks)
        state = ([], [], [], None)
        for group in groups[:-1]:
            state = score(bound, [arrived[r] for r in group], group, state)
        last = groups[-1]
        answers = finish(
            me, bound, total, [arrived[r] for r in last], last, groups[:-1], state
        )
        return restore(owner_row, slot_row, exchange(answers), slots)

    best, gap = compare(usual, few)
    if usual < most:
        best, gap = lax.cond(
            load[0, 0] <= usual, lambda: (best, gap), lambda: compare(most, False)
        )
    return best.reshape(rows), gap.reshape(rows)


def solution(mesh):
    return jax.shard_map(
        local,
        mesh=mesh,
        in_specs=(P(("groups", "owner"), None), P(("groups", "owner"))),
        out_specs=(P(("groups", "owner")), P(("groups", "owner"))),
        check_vma=False,
    )
```

```python
import functools

import jax
import jax.numpy as jnp
from jax import lax
from jax.experimental import pallas as pl
from jax.experimental.pallas import tpu as pltpu
from jax.sharding import PartitionSpec as P

CL_DEV = 4
VARIANTS = 32
STEP = 16
TILE = 256
LANES = 128
MAX_PERMUTES = 8
RANKS = 4096
MIB = 1 << 20

epsilon = 1e-06
f32 = jnp.float32
bf16 = jnp.bfloat16
i32 = jnp.int32
VMEM = pl.BlockSpec(memory_space=pltpu.VMEM)
SMEM = pl.BlockSpec(memory_space=pltpu.SMEM)


def iota(shape, axis):
    return lax.broadcasted_iota(i32, shape, axis)


def round_up(value, unit):
    return -(-value // unit) * unit


def nt_dot(a, b):
    return lax.dot_general(a, b, (((1,), (1,)), ((), ())), preferred_element_type=f32)


def mm(a, b):
    return jnp.dot(a, b, preferred_element_type=f32)


def to_bf16(mask):
    return mask.astype(f32).astype(bf16)


def count_kernel(me_ref, ids0_ref, ids1_ref, counts_ref, rank0_ref, rank1_ref):
    rows = ids0_ref.shape[1]
    chips, _, clusters = counts_ref.shape
    core = me_ref[0] & 1
    label = iota((clusters, TILE), 0)
    upto = to_bf16(iota((TILE, TILE), 0) <= iota((TILE, TILE), 1))
    totals = []
    for ids_ref, rank_ref in ((ids0_ref, rank0_ref), (ids1_ref, rank1_ref)):
        total = jnp.zeros((clusters, 1), f32)
        for b in range(rows // TILE):
            at = slice(b * TILE, (b + 1) * TILE)
            hot = ids_ref[:, at] == label
            prefix = mm(to_bf16(hot), upto)
            rank = jnp.sum(jnp.where(hot, prefix + total - 1.0, 0.0), axis=0, keepdims=True)
            rank_ref[:, at] = ids_ref[:, at] * RANKS + rank.astype(i32)
            total = total + prefix[:, TILE - 1 :]
        totals.append(total)
    ahead0 = jnp.where(core == 1, totals[1], 0.0)
    ahead1 = jnp.where(core == 0, totals[0], 0.0)
    for ids_ref, rank_ref, ahead in (
        (ids0_ref, rank0_ref, ahead0),
        (ids1_ref, rank1_ref, ahead1),
    ):
        for b in range(rows // TILE):
            at = slice(b * TILE, (b + 1) * TILE)
            more = jnp.where(ids_ref[:, at] == label, ahead, 0.0)
            rank_ref[:, at] += jnp.sum(more, axis=0, keepdims=True).astype(i32)
    square = (clusters, clusters)
    eye = iota(square, 0) == iota(square, 1)
    both = totals[0] + totals[1]
    total_row = jnp.sum(jnp.where(eye, both, 0.0), axis=0, keepdims=True).astype(i32)
    for chip in range(chips):
        counts_ref[chip] = total_row


def count_rows(me, ids0, ids1, chips, clusters):
    return pl.pallas_call(
        count_kernel,
        out_shape=(
            jax.ShapeDtypeStruct((chips, 1, clusters), i32),
            jax.ShapeDtypeStruct(ids0.shape, i32),
            jax.ShapeDtypeStruct(ids0.shape, i32),
        ),
        in_specs=[SMEM, VMEM, VMEM],
        out_specs=(VMEM,) * 3,
        compiler_params=pltpu.CompilerParams(vmem_limit_bytes=16 * MIB),
        name="count_rows",
    )(me, ids0, ids1)


def assign_kernel(
    me_ref,
    counts_ref,
    rank0_ref,
    rank1_ref,
    owner0_ref,
    owner1_ref,
    slot0_ref,
    slot1_ref,
    bound_ref,
    total_ref,
    load_ref,
):
    chips, _, clusters = counts_ref.shape
    owners = 2 * chips
    rows = rank0_ref.shape[1]
    shift = owners.bit_length() - 1
    me = me_ref[0]
    chip = me >> 1
    count = jnp.concatenate([counts_ref[s].astype(f32) for s in range(chips)], axis=0)
    count16 = count.astype(bf16)
    square = (clusters, clusters)
    sub, lane = iota(square, 0), iota(square, 1)
    total_row = jnp.sum(count, axis=0, keepdims=True)
    total_col = jnp.sum(jnp.where(sub == lane, total_row, 0.0), axis=1, keepdims=True)
    tie = total_row == total_col
    outranks_col = (total_row > total_col) | (tie & (lane < sub))
    outranks_row = (total_col > total_row) | (tie & (sub < lane))
    rank_col = jnp.sum(outranks_col.astype(f32), axis=1, keepdims=True).astype(i32)
    rank_row = jnp.sum(outranks_row.astype(f32), axis=0, keepdims=True).astype(i32)

    def owner_of(rank, variant):
        layer = rank >> shift
        within = rank & (owners - 1)
        flip = jnp.zeros_like(variant)
        for p in range(1, CL_DEV):
            bits = (variant >> (p - 1)) & 1
            if p < CL_DEV - 1:
                bits = bits + 2 * ((variant >> (p + CL_DEV - 2)) & 1)
            flip = flip + jnp.where(layer == p, bits, 0)
        within = within ^ flip
        return jnp.where((layer & 1) == 1, owners - 1 - within, within)

    wide = (clusters, VARIANTS * owners)
    variant = iota(wide, 1) >> shift
    tried = owner_of(rank_col, variant) == (iota(wide, 1) & (owners - 1))
    load = jnp.max(mm(count16, to_bf16(tried)), axis=0, keepdims=True)
    by_variant = (VARIANTS, VARIANTS * owners)
    worst = jnp.max(
        jnp.where((iota(by_variant, 1) >> shift) == iota(by_variant, 0), load, 0.0),
        axis=1,
        keepdims=True,
    )
    best = jnp.min(worst, axis=0, keepdims=True)
    chosen = jnp.min(
        jnp.where(worst == best, iota((VARIANTS, 1), 0), VARIANTS), axis=0, keepdims=True
    )
    owner_col = owner_of(rank_col, chosen + jnp.zeros_like(rank_col))
    owner_row = owner_of(rank_row, chosen + jnp.zeros_like(rank_row))
    layer_col, layer_row = rank_col >> shift, rank_row >> shift
    load_ref[...] = jnp.broadcast_to(best, load_ref.shape).astype(i32)

    mine = jnp.sum(jnp.where(iota(count.shape, 0) == chip, count, 0.0), axis=0, keepdims=True)
    earlier = (owner_row == owner_col) & (layer_row < layer_col)
    offset_col = jnp.sum(jnp.where(earlier, mine, 0.0), axis=1, keepdims=True)
    for rank_ref, owner_ref, slot_ref in (
        (rank0_ref, owner0_ref, slot0_ref),
        (rank1_ref, owner1_ref, slot1_ref),
    ):
        hot = (rank_ref[...] // RANKS) == iota((clusters, rows), 0)
        owner_ref[...] = jnp.sum(
            jnp.where(hot, owner_col.astype(f32), 0.0), axis=0, keepdims=True
        ).astype(i32)
        slot_ref[...] = jnp.sum(jnp.where(hot, offset_col, 0.0), axis=0, keepdims=True).astype(
            i32
        ) + (rank_ref[...] & (RANKS - 1))

    select = (owner_col == me) & (layer_col <= iota((clusters, LANES), 1))
    turn = iota((chips, chips), 1) == (iota((chips, chips), 0) ^ chip)
    turned = mm(to_bf16(turn), count16).astype(bf16)
    bound_ref[...] = mm(turned, to_bf16(select))
    own = (owner_row == me) & (layer_row == iota((8, clusters), 0))
    total_ref[...] = jnp.broadcast_to(
        jnp.sum(jnp.where(own, total_row, 0.0), axis=1, keepdims=True), total_ref.shape
    )


def assign(me, counts, rank0, rank1):
    chips, _, clusters = counts.shape
    line = jax.ShapeDtypeStruct(rank0.shape, i32)
    return pl.pallas_call(
        assign_kernel,
        out_shape=(
            line,
            line,
            line,
            line,
            jax.ShapeDtypeStruct((chips, LANES), f32),
            jax.ShapeDtypeStruct((8, LANES), f32),
            jax.ShapeDtypeStruct((1, LANES), i32),
        ),
        in_specs=[SMEM, VMEM, VMEM, VMEM],
        out_specs=(VMEM,) * 7,
        compiler_params=pltpu.CompilerParams(vmem_limit_bytes=16 * MIB),
        name="assign",
    )(me, counts, rank0, rank1)


def pack_kernel(
    partner, me_ref, owner0_ref, owner1_ref, slot0_ref, slot1_ref, rows0_ref, rows1_ref, out_ref
):
    slots = out_ref.shape[0]
    rows = rows0_ref.shape[0]
    target = me_ref[0] ^ (2 * partner)
    slot = iota((slots, rows), 0)
    total = None
    for owner_ref, slot_ref, rows_ref in (
        (owner0_ref, slot0_ref, rows0_ref),
        (owner1_ref, slot1_ref, rows1_ref),
    ):
        key = jnp.where(owner_ref[...] == target, slot_ref[...], -1)
        part = mm(to_bf16(slot == key), rows_ref[...])
        total = part if total is None else total + part
    out_ref[...] = total.astype(bf16)


def pack(me, places, both, partner, slots):
    width = both[0].shape[1]
    return pl.pallas_call(
        functools.partial(pack_kernel, partner),
        out_shape=jax.ShapeDtypeStruct((slots, width), bf16),
        in_specs=[SMEM] + [VMEM] * 6,
        out_specs=VMEM,
        compiler_params=pltpu.CompilerParams(vmem_limit_bytes=24 * MIB),
        cost_estimate=pl.CostEstimate(flops=slots, bytes_accessed=slots, transcendentals=0),
        name="pack_rows",
    )(me, *places, *both)


def unit_rows(ref):
    x = ref[...].astype(f32)
    scale = lax.rsqrt(jnp.sum(x * x, axis=1, keepdims=True) + epsilon)
    return (x * scale).astype(bf16)


def cluster_lanes(bound_ref, partners, slots, width):
    lane = iota((1, width), 1).astype(f32)
    result = jnp.where(lane < len(partners) * slots, 0.0, -1.0)
    for i, r in enumerate(partners):
        for k in range(CL_DEV):
            first = bound_ref[r : r + 1, k : k + 1] + float(i * slots)
            result = result + ((lane >= first) & (lane < float((i + 1) * slots))).astype(f32)
    return result


def cluster_rows(bound_ref, r, slots):
    slot = iota((slots, LANES), 0).astype(f32)
    result = jnp.zeros((slots, LANES), f32)
    for k in range(CL_DEV):
        result = result + (slot >= bound_ref[r : r + 1, k : k + 1]).astype(f32)
    return result


def score_group(new_ref, new_cids, olds, cid_row, slots_new):
    padded = new_ref.shape[0]
    groups = padded // LANES
    new = new_ref[...]

    def folded(scores, cids, skip_same):
        rows = scores.shape[0]
        row = iota((rows, LANES), 0)
        lane = iota((rows, LANES), 1)
        best, cols = None, []
        for g in range(groups):
            at = slice(g * LANES, (g + 1) * LANES)
            allowed = cids == cid_row[:, at]
            if skip_same:
                allowed = allowed & (row != lane + g * LANES)
            part = jnp.where(allowed, scores[:, at], -1.0)
            best = part if best is None else jnp.maximum(best, part)
            cols.append(jnp.max(part, axis=0, keepdims=True))
        return best, cols

    columns = None
    results = []
    for unit_ref, acc_ref, cid_ref in olds:
        scores = nt_dot(unit_ref[...], new)
        best, cols = folded(scores, cid_ref[...], False)
        columns = cols if columns is None else [jnp.maximum(a, b) for a, b in zip(columns, cols)]
        results.append((scores, jnp.maximum(acc_ref[...], best)))
    scores = nt_dot(new[0:slots_new], new)
    best, _ = folded(scores, new_cids, True)
    if columns is not None:
        row = iota((slots_new, LANES), 0)
        lane = iota((slots_new, LANES), 1)
        for g, col in enumerate(columns):
            best = jnp.maximum(best, jnp.where(row == lane + g * LANES, col, -1.0))
    results.append((scores, best))
    return results


def member_sums(cid_row, new):
    hot = to_bf16(cid_row == iota((8, cid_row.shape[1]), 0).astype(f32))
    return mm(hot, new)


def score_kernel(slots, partners, olds, bound_ref, *refs):
    fresh = len(partners)
    raw_refs, refs = refs[:fresh], refs[fresh:]
    old_refs = [refs[3 * i : 3 * i + 3] for i in range(olds)]
    refs = refs[3 * olds :]
    if olds:
        sums_ref, refs = refs[0], refs[1:]
    unit_ref, acc_ref, cid_ref, sums_out = refs[:4]
    old_accs = refs[4 : 4 + olds]
    new_ref = refs[4 + olds]
    rows = fresh * slots
    for i, r in enumerate(partners):
        at = slice(i * slots, (i + 1) * slots)
        new_ref[at, :] = unit_rows(raw_refs[i])
        cid_ref[at, :] = cluster_rows(bound_ref, r, slots)
    padded = new_ref.shape[0]
    if padded > rows:
        new_ref[rows:, :] = jnp.zeros((padded - rows, new_ref.shape[1]), bf16)
    unit_ref[...] = new_ref[0:rows, :]
    cid_row = cluster_lanes(bound_ref, partners, slots, padded)
    results = score_group(new_ref, cid_ref[...], old_refs, cid_row, rows)
    for (_, best), ref in zip(results, list(old_accs) + [acc_ref]):
        ref[...] = best
    sums = member_sums(cid_row, new_ref[...])
    sums_out[...] = sums + sums_ref[...] if olds else sums


def score(bound, blocks, partners, state):
    slots, width = blocks[0].shape
    units, accs, cids, sums = state
    rows = len(blocks) * slots
    padded = round_up(rows, LANES)
    old = [x for group in zip(units, accs, cids) for x in group]
    old_rows = sum(u.shape[0] for u in units)
    acc_shapes = [jax.ShapeDtypeStruct(a.shape, f32) for a in accs]
    out_shape = (
        jax.ShapeDtypeStruct((rows, width), bf16),
        jax.ShapeDtypeStruct((rows, LANES), f32),
        jax.ShapeDtypeStruct((rows, LANES), f32),
        jax.ShapeDtypeStruct((8, width), f32),
        *acc_shapes,
    )
    args = [bound, *blocks, *old] + ([sums] if units else [])
    out = pl.pallas_call(
        functools.partial(score_kernel, slots, partners, len(units)),
        out_shape=out_shape,
        in_specs=[VMEM] * len(args),
        out_specs=(VMEM,) * len(out_shape),
        scratch_shapes=[pltpu.VMEM((padded, width), bf16)],
        compiler_params=pltpu.CompilerParams(vmem_limit_bytes=(36 if slots < 400 else 58) * MIB),
        cost_estimate=pl.CostEstimate(
            flops=2 * (old_rows + rows) * padded * width,
            bytes_accessed=2 * (old_rows + rows) * width,
            transcendentals=rows,
        ),
        name="score_rows",
    )(*args)
    return units + [out[0]], list(out[4:]) + [out[1]], cids + [out[2]], out[3]


def finish_kernel(slots, partners, earlier, olds, me_ref, bound_ref, total_ref, *refs):
    fresh = len(partners)
    raw_refs, refs = refs[:fresh], refs[fresh:]
    old_refs = [refs[3 * i : 3 * i + 3] for i in range(olds)]
    sums_ref, out_ref, new_ref = refs[3 * olds :]
    chip = me_ref[0] >> 1
    rows = fresh * slots
    padded, width = new_ref.shape
    new_ref[rows:, :] = jnp.zeros((padded - rows, width), bf16)
    pieces = []
    for i, r in enumerate(partners):
        new_ref[i * slots : (i + 1) * slots, :] = unit_rows(raw_refs[i])
        pieces.append(cluster_rows(bound_ref, r, slots))
    new_cids = jnp.concatenate(pieces, axis=0)
    cid_row = cluster_lanes(bound_ref, partners, slots, padded)
    sums = sums_ref[...] + member_sums(cid_row, new_ref[...])
    centroid = (sums / jnp.maximum(total_ref[:, 0:1], 1.0)).astype(bf16)
    centroid = jnp.concatenate([centroid, jnp.zeros_like(centroid)], axis=0)
    new_ref[rows : rows + STEP, :] = centroid
    results = score_group(new_ref, new_cids, old_refs, cid_row, rows)
    half = out_ref.shape[2] // 2
    group, within = rows // LANES, rows % LANES
    eye = iota((slots, half), 0) == iota((slots, half), 1)
    all_cids = [old[2][...] for old in old_refs] + [new_cids]
    for (scores, acc), cids, names in zip(results, all_cids, earlier + [partners]):
        best = jnp.max(acc, axis=1, keepdims=True)
        lane = iota(cids.shape, 1).astype(f32)
        dots = scores[:, group * LANES : (group + 1) * LANES]
        gap = 1.0 - jnp.sum(
            jnp.where(lane == cids + float(within), dots, 0.0), axis=1, keepdims=True
        )
        for i, r in enumerate(names):
            at = slice(i * slots, (i + 1) * slots)
            for j, col in enumerate((best, gap)):
                line = jnp.sum(jnp.where(eye, col[at], 0.0), axis=0, keepdims=True)
                for core in range(2):
                    device = 2 * (r ^ chip) + core
                    out_ref[device, :, j * half : (j + 1) * half] = line


def finish(me, bound, total, blocks, partners, earlier, state):
    slots, width = blocks[0].shape
    owners = 2 * bound.shape[0]
    units, accs, cids, sums = state
    rows = len(blocks) * slots
    padded = round_up(rows + STEP, LANES)
    old = [x for group in zip(units, accs, cids) for x in group]
    args = [me, bound, total, *blocks, *old, sums]
    return pl.pallas_call(
        functools.partial(finish_kernel, slots, partners, earlier, len(units)),
        out_shape=jax.ShapeDtypeStruct((owners, 1, 2 * round_up(slots, LANES)), f32),
        in_specs=[SMEM] + [VMEM] * (len(args) - 1),
        out_specs=VMEM,
        scratch_shapes=[pltpu.VMEM((padded, width), bf16)],
        compiler_params=pltpu.CompilerParams(vmem_limit_bytes=(36 if slots < 400 else 58) * MIB),
        cost_estimate=pl.CostEstimate(
            flops=2 * owners * slots * padded * width,
            bytes_accessed=2 * owners * slots * width,
            transcendentals=rows,
        ),
        name="finish_rows",
    )(*args)


def restore_kernel(slots, owner_ref, slot_ref, back_ref, best_ref, gap_ref):
    rows = owner_ref.shape[1]
    owners, _, width = back_ref.shape
    half = width // 2
    from_owner = to_bf16(owner_ref[...] == iota((owners, rows), 0))
    from_owner = jnp.concatenate([from_owner] * 3, axis=0)
    at_slot = slot_ref[...] == iota((slots, rows), 0)
    back = jnp.concatenate([back_ref[s] for s in range(owners)], axis=0)
    part0 = back.astype(bf16)
    rest = back - part0.astype(f32)
    part1 = rest.astype(bf16)
    part2 = (rest - part1.astype(f32)).astype(bf16)
    parts = jnp.concatenate([part0, part1, part2], axis=0)
    for i, ref in enumerate((best_ref, gap_ref)):
        table = lax.dot_general(
            parts[:, i * half : i * half + slots],
            from_owner,
            (((0,), (0,)), ((), ())),
            preferred_element_type=f32,
        )
        ref[...] = jnp.sum(jnp.where(at_slot, table, 0.0), axis=0, keepdims=True)


def restore(owner_row, slot_row, back, slots):
    return pl.pallas_call(
        functools.partial(restore_kernel, slots),
        out_shape=(jax.ShapeDtypeStruct(owner_row.shape, f32),) * 2,
        in_specs=[VMEM] * 3,
        out_specs=(VMEM, VMEM),
        compiler_params=pltpu.CompilerParams(vmem_limit_bytes=28 * MIB),
        name="restore_rows",
    )(owner_row, slot_row, back)


def exchange(x):
    return lax.all_to_all(x, "owner", split_axis=0, concat_axis=0, tiled=True)


def exchange_chips(x):
    chips = lax.axis_size("owner") // 2
    cores = [[2 * chip + core for chip in range(chips)] for core in range(2)]
    return lax.all_to_all(
        x, "owner", split_axis=0, concat_axis=0, axis_index_groups=cores, tiled=True
    )


def swap(block, r):
    owners = lax.axis_size("owner")
    return lax.ppermute(block, "owner", [(s, s ^ (2 * r)) for s in range(owners)])


def swap_together(blocks):
    chips = len(blocks)
    order = jnp.arange(chips, dtype=i32) ^ (lax.axis_index("owner").astype(i32) >> 1)
    arrived = exchange_chips(jnp.stack(blocks)[order])[order]
    return [arrived[r] for r in range(chips)]


def swap_cores(x):
    owners = lax.axis_size("owner")
    return lax.ppermute(x, "owner", [(s, s ^ 1) for s in range(owners)])


def local(embeddings, cluster_ids):
    rows = embeddings.shape[0]
    owners = lax.axis_size("owner")
    chips = owners // 2
    clusters = CL_DEV * owners
    row_limit = 2 * rows // clusters
    most = round_up(2 * CL_DEV * row_limit, STEP)
    usual = min(most, round_up(17 * rows // (8 * owners), STEP))
    few = chips <= MAX_PERMUTES
    me = lax.axis_index("owner").astype(i32).reshape(1)
    ids0 = cluster_ids.reshape(1, rows)
    ids1 = swap_cores(ids0)
    mine, ids1 = lax.optimization_barrier((embeddings, ids1))
    other = swap_cores(mine)
    counts, rank0, rank1 = count_rows(me, ids0, ids1, chips, clusters)
    counts = exchange_chips(counts)
    both = (embeddings, other)
    *places, bound, total, load = assign(me, counts, rank0, rank1)
    owner_row, slot_row = places[0], places[2]

    half = chips // 2
    far = list(range(chips - 1, half - 1, -1))
    near = list(range(half - 1, 0, -1))
    sent = far[:2] + near + far[2:] + [0]
    share = max(half // 4, 1)
    groups = [[0] + near, far[: 2 * share], far[2 * share : 3 * share], far[3 * share :]]

    def compare(slots, apart):
        blocks = [None] * chips
        here = list(places)
        for r in sent:
            blocks[r] = pack(me, here, both, r, slots)
            here[0], blocks[r] = lax.optimization_barrier((here[0], blocks[r]))
        if apart:
            arrived = blocks[:1] + [None] * (chips - 1)
            for r in sent[:-1]:
                if r in far[2:]:
                    before = far[far.index(r) - 2]
                    blocks[r], arrived[before] = lax.optimization_barrier(
                        (blocks[r], arrived[before])
                    )
                arrived[r] = swap(blocks[r], r)
        else:
            arrived = swap_together(blocks)
        state = ([], [], [], None)
        for group in groups[:-1]:
            state = score(bound, [arrived[r] for r in group], group, state)
        last = groups[-1]
        answers = finish(
            me, bound, total, [arrived[r] for r in last], last, groups[:-1], state
        )
        return restore(owner_row, slot_row, exchange(answers), slots)

    best, gap = compare(usual, few)
    if usual < most:
        best, gap = lax.cond(
            load[0, 0] <= usual, lambda: (best, gap), lambda: compare(most, False)
        )
    return best.reshape(rows), gap.reshape(rows)


def solution(mesh):
    return jax.shard_map(
        local,
        mesh=mesh,
        in_specs=(P(("groups", "owner"), None), P(("groups", "owner"))),
        out_specs=(P(("groups", "owner")), P(("groups", "owner"))),
        check_vma=False,
    )
```

```python
import functools

import jax
import jax.numpy as jnp
from jax import lax
from jax.experimental import pallas as pl
from jax.experimental.pallas import tpu as pltpu
from jax.sharding import PartitionSpec as P

CL_DEV = 4
VARIANTS = 32
STEP = 16
TILE = 256
LANES = 128
MAX_PERMUTES = 8
RANKS = 4096
MIB = 1 << 20

epsilon = 1e-06
f32 = jnp.float32
bf16 = jnp.bfloat16
i32 = jnp.int32
VMEM = pl.BlockSpec(memory_space=pltpu.VMEM)
SMEM = pl.BlockSpec(memory_space=pltpu.SMEM)


def iota(shape, axis):
    return lax.broadcasted_iota(i32, shape, axis)


def round_up(value, unit):
    return -(-value // unit) * unit


def nt_dot(a, b):
    return lax.dot_general(a, b, (((1,), (1,)), ((), ())), preferred_element_type=f32)


def mm(a, b):
    return jnp.dot(a, b, preferred_element_type=f32)


def to_bf16(mask):
    return mask.astype(f32).astype(bf16)


def count_kernel(me_ref, ids0_ref, ids1_ref, counts_ref, rank0_ref, rank1_ref):
    rows = ids0_ref.shape[1]
    chips, _, clusters = counts_ref.shape
    core = me_ref[0] & 1
    label = iota((clusters, TILE), 0)
    upto = to_bf16(iota((TILE, TILE), 0) <= iota((TILE, TILE), 1))
    totals = []
    for ids_ref, rank_ref in ((ids0_ref, rank0_ref), (ids1_ref, rank1_ref)):
        total = jnp.zeros((clusters, 1), f32)
        for b in range(rows // TILE):
            at = slice(b * TILE, (b + 1) * TILE)
            hot = ids_ref[:, at] == label
            prefix = mm(to_bf16(hot), upto)
            rank = jnp.sum(jnp.where(hot, prefix + total - 1.0, 0.0), axis=0, keepdims=True)
            rank_ref[:, at] = ids_ref[:, at] * RANKS + rank.astype(i32)
            total = total + prefix[:, TILE - 1 :]
        totals.append(total)
    ahead0 = jnp.where(core == 1, totals[1], 0.0)
    ahead1 = jnp.where(core == 0, totals[0], 0.0)
    for ids_ref, rank_ref, ahead in (
        (ids0_ref, rank0_ref, ahead0),
        (ids1_ref, rank1_ref, ahead1),
    ):
        for b in range(rows // TILE):
            at = slice(b * TILE, (b + 1) * TILE)
            more = jnp.where(ids_ref[:, at] == label, ahead, 0.0)
            rank_ref[:, at] += jnp.sum(more, axis=0, keepdims=True).astype(i32)
    square = (clusters, clusters)
    eye = iota(square, 0) == iota(square, 1)
    both = totals[0] + totals[1]
    total_row = jnp.sum(jnp.where(eye, both, 0.0), axis=0, keepdims=True).astype(i32)
    for chip in range(chips):
        counts_ref[chip] = total_row


def count_rows(me, ids0, ids1, chips, clusters):
    return pl.pallas_call(
        count_kernel,
        out_shape=(
            jax.ShapeDtypeStruct((chips, 1, clusters), i32),
            jax.ShapeDtypeStruct(ids0.shape, i32),
            jax.ShapeDtypeStruct(ids0.shape, i32),
        ),
        in_specs=[SMEM, VMEM, VMEM],
        out_specs=(VMEM,) * 3,
        compiler_params=pltpu.CompilerParams(vmem_limit_bytes=16 * MIB),
        cost_estimate=pl.CostEstimate(flops=8_000_000_000, bytes_accessed=1 << 20, transcendentals=0),
        name="count_rows",
    )(me, ids0, ids1)


def assign_kernel(
    me_ref,
    counts_ref,
    rank0_ref,
    rank1_ref,
    owner0_ref,
    owner1_ref,
    slot0_ref,
    slot1_ref,
    bound_ref,
    total_ref,
    load_ref,
):
    chips, _, clusters = counts_ref.shape
    owners = 2 * chips
    rows = rank0_ref.shape[1]
    shift = owners.bit_length() - 1
    me = me_ref[0]
    chip = me >> 1
    count = jnp.concatenate([counts_ref[s].astype(f32) for s in range(chips)], axis=0)
    count16 = count.astype(bf16)
    square = (clusters, clusters)
    sub, lane = iota(square, 0), iota(square, 1)
    total_row = jnp.sum(count, axis=0, keepdims=True)
    total_col = jnp.sum(jnp.where(sub == lane, total_row, 0.0), axis=1, keepdims=True)
    tie = total_row == total_col
    outranks_col = (total_row > total_col) | (tie & (lane < sub))
    outranks_row = (total_col > total_row) | (tie & (sub < lane))
    rank_col = jnp.sum(outranks_col.astype(f32), axis=1, keepdims=True).astype(i32)
    rank_row = jnp.sum(outranks_row.astype(f32), axis=0, keepdims=True).astype(i32)

    def owner_of(rank, variant):
        layer = rank >> shift
        within = rank & (owners - 1)
        flip = jnp.zeros_like(variant)
        for p in range(1, CL_DEV):
            bits = (variant >> (p - 1)) & 1
            if p < CL_DEV - 1:
                bits = bits + 2 * ((variant >> (p + CL_DEV - 2)) & 1)
            flip = flip + jnp.where(layer == p, bits, 0)
        within = within ^ flip
        return jnp.where((layer & 1) == 1, owners - 1 - within, within)

    wide = (clusters, VARIANTS * owners)
    variant = iota(wide, 1) >> shift
    tried = owner_of(rank_col, variant) == (iota(wide, 1) & (owners - 1))
    load = jnp.max(mm(count16, to_bf16(tried)), axis=0, keepdims=True)
    by_variant = (VARIANTS, VARIANTS * owners)
    worst = jnp.max(
        jnp.where((iota(by_variant, 1) >> shift) == iota(by_variant, 0), load, 0.0),
        axis=1,
        keepdims=True,
    )
    best = jnp.min(worst, axis=0, keepdims=True)
    chosen = jnp.min(
        jnp.where(worst == best, iota((VARIANTS, 1), 0), VARIANTS), axis=0, keepdims=True
    )
    owner_col = owner_of(rank_col, chosen + jnp.zeros_like(rank_col))
    owner_row = owner_of(rank_row, chosen + jnp.zeros_like(rank_row))
    layer_col, layer_row = rank_col >> shift, rank_row >> shift
    load_ref[...] = jnp.broadcast_to(best, load_ref.shape).astype(i32)

    mine = jnp.sum(jnp.where(iota(count.shape, 0) == chip, count, 0.0), axis=0, keepdims=True)
    earlier = (owner_row == owner_col) & (layer_row < layer_col)
    offset_col = jnp.sum(jnp.where(earlier, mine, 0.0), axis=1, keepdims=True)
    for rank_ref, owner_ref, slot_ref in (
        (rank0_ref, owner0_ref, slot0_ref),
        (rank1_ref, owner1_ref, slot1_ref),
    ):
        hot = (rank_ref[...] // RANKS) == iota((clusters, rows), 0)
        owner_ref[...] = jnp.sum(
            jnp.where(hot, owner_col.astype(f32), 0.0), axis=0, keepdims=True
        ).astype(i32)
        slot_ref[...] = jnp.sum(jnp.where(hot, offset_col, 0.0), axis=0, keepdims=True).astype(
            i32
        ) + (rank_ref[...] & (RANKS - 1))

    select = (owner_col == me) & (layer_col <= iota((clusters, LANES), 1))
    turn = iota((chips, chips), 1) == (iota((chips, chips), 0) ^ chip)
    turned = mm(to_bf16(turn), count16).astype(bf16)
    bound_ref[...] = mm(turned, to_bf16(select))
    own = (owner_row == me) & (layer_row == iota((8, clusters), 0))
    total_ref[...] = jnp.broadcast_to(
        jnp.sum(jnp.where(own, total_row, 0.0), axis=1, keepdims=True), total_ref.shape
    )


def assign(me, counts, rank0, rank1):
    chips, _, clusters = counts.shape
    line = jax.ShapeDtypeStruct(rank0.shape, i32)
    return pl.pallas_call(
        assign_kernel,
        out_shape=(
            line,
            line,
            line,
            line,
            jax.ShapeDtypeStruct((chips, LANES), f32),
            jax.ShapeDtypeStruct((8, LANES), f32),
            jax.ShapeDtypeStruct((1, LANES), i32),
        ),
        in_specs=[SMEM, VMEM, VMEM, VMEM],
        out_specs=(VMEM,) * 7,
        compiler_params=pltpu.CompilerParams(vmem_limit_bytes=16 * MIB),
        name="assign",
    )(me, counts, rank0, rank1)


def pack_kernel(
    partner, me_ref, owner0_ref, owner1_ref, slot0_ref, slot1_ref, rows0_ref, rows1_ref, out_ref
):
    slots = out_ref.shape[0]
    rows = rows0_ref.shape[0]
    target = me_ref[0] ^ (2 * partner)
    slot = iota((slots, rows), 0)
    total = None
    for owner_ref, slot_ref, rows_ref in (
        (owner0_ref, slot0_ref, rows0_ref),
        (owner1_ref, slot1_ref, rows1_ref),
    ):
        key = jnp.where(owner_ref[...] == target, slot_ref[...], -1)
        part = mm(to_bf16(slot == key), rows_ref[...])
        total = part if total is None else total + part
    out_ref[...] = total.astype(bf16)


def pack(me, places, both, partner, slots):
    width = both[0].shape[1]
    return pl.pallas_call(
        functools.partial(pack_kernel, partner),
        out_shape=jax.ShapeDtypeStruct((slots, width), bf16),
        in_specs=[SMEM] + [VMEM] * 6,
        out_specs=VMEM,
        compiler_params=pltpu.CompilerParams(vmem_limit_bytes=24 * MIB),
        cost_estimate=pl.CostEstimate(flops=slots, bytes_accessed=slots, transcendentals=0),
        name="pack_rows",
    )(me, *places, *both)


def unit_rows(ref):
    x = ref[...].astype(f32)
    scale = lax.rsqrt(jnp.sum(x * x, axis=1, keepdims=True) + epsilon)
    return (x * scale).astype(bf16)


def cluster_lanes(bound_ref, partners, slots, width):
    lane = iota((1, width), 1).astype(f32)
    result = jnp.where(lane < len(partners) * slots, 0.0, -1.0)
    for i, r in enumerate(partners):
        for k in range(CL_DEV):
            first = bound_ref[r : r + 1, k : k + 1] + float(i * slots)
            result = result + ((lane >= first) & (lane < float((i + 1) * slots))).astype(f32)
    return result


def cluster_rows(bound_ref, r, slots):
    slot = iota((slots, LANES), 0).astype(f32)
    result = jnp.zeros((slots, LANES), f32)
    for k in range(CL_DEV):
        result = result + (slot >= bound_ref[r : r + 1, k : k + 1]).astype(f32)
    return result


def score_group(new_ref, new_cids, olds, cid_row, slots_new):
    padded = new_ref.shape[0]
    groups = padded // LANES
    new = new_ref[...]

    def folded(scores, cids, skip_same):
        rows = scores.shape[0]
        row = iota((rows, LANES), 0)
        lane = iota((rows, LANES), 1)
        best, cols = None, []
        for g in range(groups):
            at = slice(g * LANES, (g + 1) * LANES)
            allowed = cids == cid_row[:, at]
            if skip_same:
                allowed = allowed & (row != lane + g * LANES)
            part = jnp.where(allowed, scores[:, at], -1.0)
            best = part if best is None else jnp.maximum(best, part)
            cols.append(jnp.max(part, axis=0, keepdims=True))
        return best, cols

    columns = None
    results = []
    for unit_ref, acc_ref, cid_ref in olds:
        scores = nt_dot(unit_ref[...], new)
        best, cols = folded(scores, cid_ref[...], False)
        columns = cols if columns is None else [jnp.maximum(a, b) for a, b in zip(columns, cols)]
        results.append((scores, jnp.maximum(acc_ref[...], best)))
    scores = nt_dot(new[0:slots_new], new)
    best, _ = folded(scores, new_cids, True)
    if columns is not None:
        row = iota((slots_new, LANES), 0)
        lane = iota((slots_new, LANES), 1)
        for g, col in enumerate(columns):
            best = jnp.maximum(best, jnp.where(row == lane + g * LANES, col, -1.0))
    results.append((scores, best))
    return results


def member_sums(cid_row, new):
    hot = to_bf16(cid_row == iota((8, cid_row.shape[1]), 0).astype(f32))
    return mm(hot, new)


def score_kernel(slots, partners, olds, bound_ref, *refs):
    fresh = len(partners)
    raw_refs, refs = refs[:fresh], refs[fresh:]
    old_refs = [refs[3 * i : 3 * i + 3] for i in range(olds)]
    refs = refs[3 * olds :]
    if olds:
        sums_ref, refs = refs[0], refs[1:]
    unit_ref, acc_ref, cid_ref, sums_out = refs[:4]
    old_accs = refs[4 : 4 + olds]
    new_ref = refs[4 + olds]
    rows = fresh * slots
    for i, r in enumerate(partners):
        at = slice(i * slots, (i + 1) * slots)
        new_ref[at, :] = unit_rows(raw_refs[i])
        cid_ref[at, :] = cluster_rows(bound_ref, r, slots)
    padded = new_ref.shape[0]
    if padded > rows:
        new_ref[rows:, :] = jnp.zeros((padded - rows, new_ref.shape[1]), bf16)
    unit_ref[...] = new_ref[0:rows, :]
    cid_row = cluster_lanes(bound_ref, partners, slots, padded)
    results = score_group(new_ref, cid_ref[...], old_refs, cid_row, rows)
    for (_, best), ref in zip(results, list(old_accs) + [acc_ref]):
        ref[...] = best
    sums = member_sums(cid_row, new_ref[...])
    sums_out[...] = sums + sums_ref[...] if olds else sums


def score(bound, blocks, partners, state):
    slots, width = blocks[0].shape
    units, accs, cids, sums = state
    rows = len(blocks) * slots
    padded = round_up(rows, LANES)
    old = [x for group in zip(units, accs, cids) for x in group]
    old_rows = sum(u.shape[0] for u in units)
    acc_shapes = [jax.ShapeDtypeStruct(a.shape, f32) for a in accs]
    out_shape = (
        jax.ShapeDtypeStruct((rows, width), bf16),
        jax.ShapeDtypeStruct((rows, LANES), f32),
        jax.ShapeDtypeStruct((rows, LANES), f32),
        jax.ShapeDtypeStruct((8, width), f32),
        *acc_shapes,
    )
    args = [bound, *blocks, *old] + ([sums] if units else [])
    out = pl.pallas_call(
        functools.partial(score_kernel, slots, partners, len(units)),
        out_shape=out_shape,
        in_specs=[VMEM] * len(args),
        out_specs=(VMEM,) * len(out_shape),
        scratch_shapes=[pltpu.VMEM((padded, width), bf16)],
        compiler_params=pltpu.CompilerParams(vmem_limit_bytes=(36 if slots < 400 else 58) * MIB),
        cost_estimate=pl.CostEstimate(
            flops=2 * (old_rows + rows) * padded,
            bytes_accessed=2 * (old_rows + rows),
            transcendentals=rows,
        ),
        name="score_rows",
    )(*args)
    return units + [out[0]], list(out[4:]) + [out[1]], cids + [out[2]], out[3]


def finish_kernel(slots, partners, earlier, olds, me_ref, bound_ref, total_ref, *refs):
    fresh = len(partners)
    raw_refs, refs = refs[:fresh], refs[fresh:]
    old_refs = [refs[3 * i : 3 * i + 3] for i in range(olds)]
    sums_ref, out_ref, new_ref = refs[3 * olds :]
    chip = me_ref[0] >> 1
    rows = fresh * slots
    padded, width = new_ref.shape
    new_ref[rows:, :] = jnp.zeros((padded - rows, width), bf16)
    pieces = []
    for i, r in enumerate(partners):
        new_ref[i * slots : (i + 1) * slots, :] = unit_rows(raw_refs[i])
        pieces.append(cluster_rows(bound_ref, r, slots))
    new_cids = jnp.concatenate(pieces, axis=0)
    cid_row = cluster_lanes(bound_ref, partners, slots, padded)
    sums = sums_ref[...] + member_sums(cid_row, new_ref[...])
    centroid = (sums / jnp.maximum(total_ref[:, 0:1], 1.0)).astype(bf16)
    centroid = jnp.concatenate([centroid, jnp.zeros_like(centroid)], axis=0)
    new_ref[rows : rows + STEP, :] = centroid
    results = score_group(new_ref, new_cids, old_refs, cid_row, rows)
    half = out_ref.shape[2] // 2
    group, within = rows // LANES, rows % LANES
    eye = iota((LANES, LANES), 0) == iota((LANES, LANES), 1)
    all_cids = [old[2][...] for old in old_refs] + [new_cids]
    for (scores, acc), cids, names in zip(results, all_cids, earlier + [partners]):
        best = jnp.max(acc, axis=1, keepdims=True)
        lane = iota(cids.shape, 1).astype(f32)
        dots = scores[:, group * LANES : (group + 1) * LANES]
        gap = 1.0 - jnp.sum(
            jnp.where(lane == cids + float(within), dots, 0.0), axis=1, keepdims=True
        )
        for i, r in enumerate(names):
            at = slice(i * slots, (i + 1) * slots)
            for j, col in enumerate((best, gap)):
                for first in range(0, slots, LANES):
                    size = min(LANES, slots - first)
                    piece = col[at][first : first + size]
                    line = jnp.sum(jnp.where(eye[:size], piece, 0.0), axis=0, keepdims=True)
                    lanes = slice(j * half + first, j * half + first + LANES)
                    for core in range(2):
                        out_ref[2 * (r ^ chip) + core, :, lanes] = line


def finish(me, bound, total, blocks, partners, earlier, state):
    slots, width = blocks[0].shape
    owners = 2 * bound.shape[0]
    units, accs, cids, sums = state
    rows = len(blocks) * slots
    padded = round_up(rows + STEP, LANES)
    old = [x for group in zip(units, accs, cids) for x in group]
    args = [me, bound, total, *blocks, *old, sums]
    return pl.pallas_call(
        functools.partial(finish_kernel, slots, partners, earlier, len(units)),
        out_shape=jax.ShapeDtypeStruct((owners, 1, 2 * round_up(slots, LANES)), f32),
        in_specs=[SMEM] + [VMEM] * (len(args) - 1),
        out_specs=VMEM,
        scratch_shapes=[pltpu.VMEM((padded, width), bf16)],
        compiler_params=pltpu.CompilerParams(vmem_limit_bytes=(36 if slots < 400 else 58) * MIB),
        cost_estimate=pl.CostEstimate(
            flops=2 * owners * slots * padded * width,
            bytes_accessed=2 * owners * slots * width,
            transcendentals=rows,
        ),
        name="finish_rows",
    )(*args)


def restore_kernel(slots, owner_ref, slot_ref, back_ref, best_ref, gap_ref):
    rows = owner_ref.shape[1]
    owners, _, width = back_ref.shape
    half = width // 2
    from_owner = to_bf16(owner_ref[...] == iota((owners, rows), 0))
    from_owner = jnp.concatenate([from_owner] * 3, axis=0)
    at_slot = slot_ref[...] == iota((slots, rows), 0)
    back = jnp.concatenate([back_ref[s] for s in range(owners)], axis=0)
    part0 = back.astype(bf16)
    rest = back - part0.astype(f32)
    part1 = rest.astype(bf16)
    part2 = (rest - part1.astype(f32)).astype(bf16)
    parts = jnp.concatenate([part0, part1, part2], axis=0)
    for i, ref in enumerate((best_ref, gap_ref)):
        table = lax.dot_general(
            parts[:, i * half : i * half + slots],
            from_owner,
            (((0,), (0,)), ((), ())),
            preferred_element_type=f32,
        )
        ref[...] = jnp.sum(jnp.where(at_slot, table, 0.0), axis=0, keepdims=True)


def restore(owner_row, slot_row, back, slots):
    return pl.pallas_call(
        functools.partial(restore_kernel, slots),
        out_shape=(jax.ShapeDtypeStruct(owner_row.shape, f32),) * 2,
        in_specs=[VMEM] * 3,
        out_specs=(VMEM, VMEM),
        compiler_params=pltpu.CompilerParams(vmem_limit_bytes=28 * MIB),
        name="restore_rows",
    )(owner_row, slot_row, back)


def exchange(x):
    return lax.all_to_all(x, "owner", split_axis=0, concat_axis=0, tiled=True)


def exchange_chips(x):
    chips = lax.axis_size("owner") // 2
    cores = [[2 * chip + core for chip in range(chips)] for core in range(2)]
    return lax.all_to_all(
        x, "owner", split_axis=0, concat_axis=0, axis_index_groups=cores, tiled=True
    )


def swap(block, r):
    owners = lax.axis_size("owner")
    return lax.ppermute(block, "owner", [(s, s ^ (2 * r)) for s in range(owners)])


def swap_together(blocks):
    chips = len(blocks)
    order = jnp.arange(chips, dtype=i32) ^ (lax.axis_index("owner").astype(i32) >> 1)
    arrived = exchange_chips(jnp.stack(blocks)[order])[order]
    return [arrived[r] for r in range(chips)]


def swap_cores(x):
    owners = lax.axis_size("owner")
    return lax.ppermute(x, "owner", [(s, s ^ 1) for s in range(owners)])


def local(embeddings, cluster_ids):
    rows = embeddings.shape[0]
    owners = lax.axis_size("owner")
    chips = owners // 2
    clusters = CL_DEV * owners
    row_limit = 2 * rows // clusters
    most = round_up(2 * CL_DEV * row_limit, STEP)
    usual = min(most, round_up(17 * rows // (8 * owners), STEP))
    few = chips <= MAX_PERMUTES
    me = lax.axis_index("owner").astype(i32).reshape(1)
    ids0 = cluster_ids.reshape(1, rows)
    ids1 = swap_cores(ids0)
    mine, ids1 = lax.optimization_barrier((embeddings, ids1))
    other = swap_cores(mine)
    counts, rank0, rank1 = count_rows(me, ids0, ids1, chips, clusters)
    counts = exchange_chips(counts)
    both = (embeddings, other)
    *places, bound, total, load = assign(me, counts, rank0, rank1)
    owner_row, slot_row = places[0], places[2]

    half = chips // 2
    far = list(range(chips - 1, half - 1, -1))
    near = list(range(half - 1, 0, -1))
    sent = far[:2] + near + far[2:] + [0]
    share = max(half // 4, 1)
    groups = [[0] + near, far[: 2 * share], far[2 * share : 3 * share], far[3 * share :]]

    def compare(slots, apart):
        blocks = [None] * chips
        here = list(places)
        for r in sent:
            blocks[r] = pack(me, here, both, r, slots)
            here[0], blocks[r] = lax.optimization_barrier((here[0], blocks[r]))
        if apart:
            arrived = blocks[:1] + [None] * (chips - 1)
            for r in sent[:-1]:
                if r in far[2:]:
                    before = far[far.index(r) - 2]
                    blocks[r], arrived[before] = lax.optimization_barrier(
                        (blocks[r], arrived[before])
                    )
                arrived[r] = swap(blocks[r], r)
        else:
            arrived = swap_together(blocks)
        state = ([], [], [], None)
        for group in groups[:-1]:
            state = score(bound, [arrived[r] for r in group], group, state)
        last = groups[-1]
        answers = finish(
            me, bound, total, [arrived[r] for r in last], last, groups[:-1], state
        )
        return restore(owner_row, slot_row, exchange(answers), slots)

    best, gap = compare(usual, few)
    if usual < most:
        best, gap = lax.cond(
            load[0, 0] <= usual, lambda: (best, gap), lambda: compare(most, False)
        )
    return best.reshape(rows), gap.reshape(rows)


def solution(mesh):
    return jax.shard_map(
        local,
        mesh=mesh,
        in_specs=(P(("groups", "owner"), None), P(("groups", "owner"))),
        out_specs=(P(("groups", "owner")), P(("groups", "owner"))),
        check_vma=False,
    )
```

```python
import functools

import jax
import jax.numpy as jnp
from jax import lax
from jax.experimental import pallas as pl
from jax.experimental.pallas import tpu as pltpu
from jax.sharding import PartitionSpec as P

CL_DEV = 4
VARIANTS = 32
STEP = 16
TILE = 256
LANES = 128
MAX_PERMUTES = 8
RANKS = 4096
MIB = 1 << 20

epsilon = 1e-06
f32 = jnp.float32
bf16 = jnp.bfloat16
i32 = jnp.int32
VMEM = pl.BlockSpec(memory_space=pltpu.VMEM)
SMEM = pl.BlockSpec(memory_space=pltpu.SMEM)


def iota(shape, axis):
    return lax.broadcasted_iota(i32, shape, axis)


def round_up(value, unit):
    return -(-value // unit) * unit


def nt_dot(a, b):
    return lax.dot_general(a, b, (((1,), (1,)), ((), ())), preferred_element_type=f32)


def mm(a, b):
    return jnp.dot(a, b, preferred_element_type=f32)


def to_bf16(mask):
    return mask.astype(f32).astype(bf16)


def count_kernel(me_ref, ids0_ref, ids1_ref, counts_ref, rank0_ref, rank1_ref):
    rows = ids0_ref.shape[1]
    chips, _, clusters = counts_ref.shape
    core = me_ref[0] & 1
    label = iota((clusters, TILE), 0)
    upto = to_bf16(iota((TILE, TILE), 0) <= iota((TILE, TILE), 1))
    totals = []
    for ids_ref, rank_ref in ((ids0_ref, rank0_ref), (ids1_ref, rank1_ref)):
        total = jnp.zeros((clusters, 1), f32)
        for b in range(rows // TILE):
            at = slice(b * TILE, (b + 1) * TILE)
            hot = ids_ref[:, at] == label
            prefix = mm(to_bf16(hot), upto)
            rank = jnp.sum(jnp.where(hot, prefix + total - 1.0, 0.0), axis=0, keepdims=True)
            rank_ref[:, at] = ids_ref[:, at] * RANKS + rank.astype(i32)
            total = total + prefix[:, TILE - 1 :]
        totals.append(total)
    ahead0 = jnp.where(core == 1, totals[1], 0.0)
    ahead1 = jnp.where(core == 0, totals[0], 0.0)
    for ids_ref, rank_ref, ahead in (
        (ids0_ref, rank0_ref, ahead0),
        (ids1_ref, rank1_ref, ahead1),
    ):
        for b in range(rows // TILE):
            at = slice(b * TILE, (b + 1) * TILE)
            more = jnp.where(ids_ref[:, at] == label, ahead, 0.0)
            rank_ref[:, at] += jnp.sum(more, axis=0, keepdims=True).astype(i32)
    square = (clusters, clusters)
    eye = iota(square, 0) == iota(square, 1)
    both = totals[0] + totals[1]
    total_row = jnp.sum(jnp.where(eye, both, 0.0), axis=0, keepdims=True).astype(i32)
    for chip in range(chips):
        counts_ref[chip] = total_row


def count_rows(me, ids0, ids1, chips, clusters):
    return pl.pallas_call(
        count_kernel,
        out_shape=(
            jax.ShapeDtypeStruct((chips, 1, clusters), i32),
            jax.ShapeDtypeStruct(ids0.shape, i32),
            jax.ShapeDtypeStruct(ids0.shape, i32),
        ),
        in_specs=[SMEM, VMEM, VMEM],
        out_specs=(VMEM,) * 3,
        compiler_params=pltpu.CompilerParams(vmem_limit_bytes=16 * MIB),
        cost_estimate=pl.CostEstimate(flops=8_000_000_000, bytes_accessed=1 << 20, transcendentals=0),
        name="count_rows",
    )(me, ids0, ids1)


def assign_kernel(
    me_ref,
    counts_ref,
    rank0_ref,
    rank1_ref,
    owner0_ref,
    owner1_ref,
    slot0_ref,
    slot1_ref,
    bound_ref,
    total_ref,
    load_ref,
):
    chips, _, clusters = counts_ref.shape
    owners = 2 * chips
    rows = rank0_ref.shape[1]
    shift = owners.bit_length() - 1
    me = me_ref[0]
    chip = me >> 1
    count = jnp.concatenate([counts_ref[s].astype(f32) for s in range(chips)], axis=0)
    count16 = count.astype(bf16)
    square = (clusters, clusters)
    sub, lane = iota(square, 0), iota(square, 1)
    total_row = jnp.sum(count, axis=0, keepdims=True)
    total_col = jnp.sum(jnp.where(sub == lane, total_row, 0.0), axis=1, keepdims=True)
    tie = total_row == total_col
    outranks_col = (total_row > total_col) | (tie & (lane < sub))
    outranks_row = (total_col > total_row) | (tie & (sub < lane))
    rank_col = jnp.sum(outranks_col.astype(f32), axis=1, keepdims=True).astype(i32)
    rank_row = jnp.sum(outranks_row.astype(f32), axis=0, keepdims=True).astype(i32)

    def owner_of(rank, variant):
        layer = rank >> shift
        within = rank & (owners - 1)
        flip = jnp.zeros_like(variant)
        for p in range(1, CL_DEV):
            bits = (variant >> (p - 1)) & 1
            if p < CL_DEV - 1:
                bits = bits + 2 * ((variant >> (p + CL_DEV - 2)) & 1)
            flip = flip + jnp.where(layer == p, bits, 0)
        within = within ^ flip
        return jnp.where((layer & 1) == 1, owners - 1 - within, within)

    wide = (clusters, VARIANTS * owners)
    variant = iota(wide, 1) >> shift
    tried = owner_of(rank_col, variant) == (iota(wide, 1) & (owners - 1))
    load = jnp.max(mm(count16, to_bf16(tried)), axis=0, keepdims=True)
    by_variant = (VARIANTS, VARIANTS * owners)
    worst = jnp.max(
        jnp.where((iota(by_variant, 1) >> shift) == iota(by_variant, 0), load, 0.0),
        axis=1,
        keepdims=True,
    )
    best = jnp.min(worst, axis=0, keepdims=True)
    chosen = jnp.min(
        jnp.where(worst == best, iota((VARIANTS, 1), 0), VARIANTS), axis=0, keepdims=True
    )
    owner_col = owner_of(rank_col, chosen + jnp.zeros_like(rank_col))
    owner_row = owner_of(rank_row, chosen + jnp.zeros_like(rank_row))
    layer_col, layer_row = rank_col >> shift, rank_row >> shift
    load_ref[...] = jnp.broadcast_to(best, load_ref.shape).astype(i32)

    mine = jnp.sum(jnp.where(iota(count.shape, 0) == chip, count, 0.0), axis=0, keepdims=True)
    earlier = (owner_row == owner_col) & (layer_row < layer_col)
    offset_col = jnp.sum(jnp.where(earlier, mine, 0.0), axis=1, keepdims=True)
    for rank_ref, owner_ref, slot_ref in (
        (rank0_ref, owner0_ref, slot0_ref),
        (rank1_ref, owner1_ref, slot1_ref),
    ):
        hot = (rank_ref[...] // RANKS) == iota((clusters, rows), 0)
        owner_ref[...] = jnp.sum(
            jnp.where(hot, owner_col.astype(f32), 0.0), axis=0, keepdims=True
        ).astype(i32)
        slot_ref[...] = jnp.sum(jnp.where(hot, offset_col, 0.0), axis=0, keepdims=True).astype(
            i32
        ) + (rank_ref[...] & (RANKS - 1))

    select = (owner_col == me) & (layer_col <= iota((clusters, LANES), 1))
    turn = iota((chips, chips), 1) == (iota((chips, chips), 0) ^ chip)
    turned = mm(to_bf16(turn), count16).astype(bf16)
    bound_ref[...] = mm(turned, to_bf16(select))
    own = (owner_row == me) & (layer_row == iota((8, clusters), 0))
    total_ref[...] = jnp.broadcast_to(
        jnp.sum(jnp.where(own, total_row, 0.0), axis=1, keepdims=True), total_ref.shape
    )


def assign(me, counts, rank0, rank1):
    chips, _, clusters = counts.shape
    line = jax.ShapeDtypeStruct(rank0.shape, i32)
    return pl.pallas_call(
        assign_kernel,
        out_shape=(
            line,
            line,
            line,
            line,
            jax.ShapeDtypeStruct((chips, LANES), f32),
            jax.ShapeDtypeStruct((8, LANES), f32),
            jax.ShapeDtypeStruct((1, LANES), i32),
        ),
        in_specs=[SMEM, VMEM, VMEM, VMEM],
        out_specs=(VMEM,) * 7,
        compiler_params=pltpu.CompilerParams(vmem_limit_bytes=16 * MIB),
        name="assign",
    )(me, counts, rank0, rank1)


def pack_kernel(
    partner, me_ref, owner0_ref, owner1_ref, slot0_ref, slot1_ref, rows0_ref, rows1_ref, out_ref
):
    slots = out_ref.shape[0]
    rows = rows0_ref.shape[0]
    target = me_ref[0] ^ (2 * partner)
    slot = iota((slots, rows), 0)
    total = None
    for owner_ref, slot_ref, rows_ref in (
        (owner0_ref, slot0_ref, rows0_ref),
        (owner1_ref, slot1_ref, rows1_ref),
    ):
        key = jnp.where(owner_ref[...] == target, slot_ref[...], -1)
        part = mm(to_bf16(slot == key), rows_ref[...])
        total = part if total is None else total + part
    out_ref[...] = total.astype(bf16)


def pack(me, places, both, partner, slots):
    width = both[0].shape[1]
    return pl.pallas_call(
        functools.partial(pack_kernel, partner),
        out_shape=jax.ShapeDtypeStruct((slots, width), bf16),
        in_specs=[SMEM] + [VMEM] * 6,
        out_specs=VMEM,
        compiler_params=pltpu.CompilerParams(vmem_limit_bytes=24 * MIB),
        cost_estimate=pl.CostEstimate(flops=slots, bytes_accessed=slots, transcendentals=0),
        name="pack_rows",
    )(me, *places, *both)


def unit_rows(ref):
    x = ref[...].astype(f32)
    scale = lax.rsqrt(jnp.sum(x * x, axis=1, keepdims=True) + epsilon)
    return (x * scale).astype(bf16)


def cluster_lanes(bound_ref, partners, slots, width):
    lane = iota((1, width), 1).astype(f32)
    result = jnp.where(lane < len(partners) * slots, 0.0, -1.0)
    for i, r in enumerate(partners):
        for k in range(CL_DEV):
            first = bound_ref[r : r + 1, k : k + 1] + float(i * slots)
            result = result + ((lane >= first) & (lane < float((i + 1) * slots))).astype(f32)
    return result


def cluster_rows(bound_ref, r, slots):
    slot = iota((slots, LANES), 0).astype(f32)
    result = jnp.zeros((slots, LANES), f32)
    for k in range(CL_DEV):
        result = result + (slot >= bound_ref[r : r + 1, k : k + 1]).astype(f32)
    return result


def score_group(new_ref, new_cids, olds, cid_row, slots_new):
    padded = new_ref.shape[0]
    groups = padded // LANES
    new = new_ref[...]

    def folded(scores, cids, skip_same):
        rows = scores.shape[0]
        row = iota((rows, LANES), 0)
        lane = iota((rows, LANES), 1)
        best, cols = None, []
        for g in range(groups):
            at = slice(g * LANES, (g + 1) * LANES)
            allowed = cids == cid_row[:, at]
            if skip_same:
                allowed = allowed & (row != lane + g * LANES)
            part = jnp.where(allowed, scores[:, at], -1.0)
            best = part if best is None else jnp.maximum(best, part)
            cols.append(jnp.max(part, axis=0, keepdims=True))
        return best, cols

    columns = None
    results = []
    for unit_ref, acc_ref, cid_ref in olds:
        scores = nt_dot(unit_ref[0 : acc_ref.shape[0], :], new)
        best, cols = folded(scores, cid_ref[...], False)
        columns = cols if columns is None else [jnp.maximum(a, b) for a, b in zip(columns, cols)]
        results.append(jnp.maximum(acc_ref[...], best))
    scores = nt_dot(new[0:slots_new], new)
    best, _ = folded(scores, new_cids, True)
    if columns is not None:
        row = iota((slots_new, LANES), 0)
        lane = iota((slots_new, LANES), 1)
        for g, col in enumerate(columns):
            best = jnp.maximum(best, jnp.where(row == lane + g * LANES, col, -1.0))
    results.append(best)
    return results


def member_sums(cid_row, new):
    hot = to_bf16(cid_row == iota((8, cid_row.shape[1]), 0).astype(f32))
    return mm(hot, new)


def score_kernel(slots, partners, olds, bound_ref, *refs):
    fresh = len(partners)
    raw_refs, refs = refs[:fresh], refs[fresh:]
    old_refs = [refs[3 * i : 3 * i + 3] for i in range(olds)]
    refs = refs[3 * olds :]
    if olds:
        sums_ref, refs = refs[0], refs[1:]
    unit_ref, acc_ref, cid_ref, sums_out = refs[:4]
    old_accs = refs[4 : 4 + olds]
    new_ref = refs[4 + olds]
    rows = fresh * slots
    for i, r in enumerate(partners):
        at = slice(i * slots, (i + 1) * slots)
        new_ref[at, :] = unit_rows(raw_refs[i])
        cid_ref[at, :] = cluster_rows(bound_ref, r, slots)
    padded = new_ref.shape[0]
    if padded > rows:
        new_ref[rows:, :] = jnp.zeros((padded - rows, new_ref.shape[1]), bf16)
    unit_ref[...] = new_ref[...]
    cid_row = cluster_lanes(bound_ref, partners, slots, padded)
    results = score_group(new_ref, cid_ref[...], old_refs, cid_row, rows)
    for best, ref in zip(results, list(old_accs) + [acc_ref]):
        ref[...] = best
    sums = member_sums(cid_row, new_ref[...])
    sums_out[...] = sums + sums_ref[...] if olds else sums


def score(bound, blocks, partners, state):
    slots, width = blocks[0].shape
    units, accs, cids, sums = state
    rows = len(blocks) * slots
    padded = round_up(rows, LANES)
    old = [x for group in zip(units, accs, cids) for x in group]
    old_rows = sum(a.shape[0] for a in accs)
    acc_shapes = [jax.ShapeDtypeStruct(a.shape, f32) for a in accs]
    out_shape = (
        jax.ShapeDtypeStruct((padded, width), bf16),
        jax.ShapeDtypeStruct((rows, LANES), f32),
        jax.ShapeDtypeStruct((rows, LANES), f32),
        jax.ShapeDtypeStruct((8, width), f32),
        *acc_shapes,
    )
    args = [bound, *blocks, *old] + ([sums] if units else [])
    out = pl.pallas_call(
        functools.partial(score_kernel, slots, partners, len(units)),
        out_shape=out_shape,
        in_specs=[VMEM] * len(args),
        out_specs=(VMEM,) * len(out_shape),
        scratch_shapes=[pltpu.VMEM((padded, width), bf16)],
        compiler_params=pltpu.CompilerParams(vmem_limit_bytes=(36 if slots < 400 else 58) * MIB),
        cost_estimate=pl.CostEstimate(
            flops=2 * (old_rows + rows) * padded,
            bytes_accessed=2 * (old_rows + rows),
            transcendentals=rows,
        ),
        name="score_rows",
    )(*args)
    return units + [out[0]], list(out[4:]) + [out[1]], cids + [out[2]], out[3]


def diagonal():
    return iota((LANES, LANES), 0) == iota((LANES, LANES), 1)


def to_line(col, first):
    piece = col[first : first + LANES]
    return jnp.sum(jnp.where(diagonal()[: piece.shape[0]], piece, 0.0), axis=0, keepdims=True)


def line_kernel(slots, names, bound_ref, *refs):
    count = len(names)
    for i, partners in enumerate(names):
        acc_ref, best_ref, cid_ref = refs[i], refs[count + 2 * i], refs[count + 2 * i + 1]
        best = jnp.max(acc_ref[...], axis=1, keepdims=True)
        for first in range(0, best_ref.shape[1], LANES):
            best_ref[:, first : first + LANES] = to_line(best, first)
        cid_ref[...] = cluster_lanes(bound_ref, partners, slots, cid_ref.shape[1])


def lines(bound, names, slots, accs):
    widths = [round_up(acc.shape[0], LANES) for acc in accs]
    out = pl.pallas_call(
        functools.partial(line_kernel, slots, names),
        out_shape=tuple(jax.ShapeDtypeStruct((1, w), f32) for w in widths for _ in range(2)),
        in_specs=[VMEM] * (1 + len(accs)),
        out_specs=(VMEM,) * (2 * len(accs)),
        compiler_params=pltpu.CompilerParams(vmem_limit_bytes=16 * MIB),
        name="line_rows",
    )(bound, *accs)
    return out[0::2], out[1::2]


def finish_kernel(slots, partners, earlier, me_ref, bound_ref, total_ref, *refs):
    fresh = len(partners)
    olds = len(earlier)
    raw_refs, refs = refs[:fresh], refs[fresh:]
    old_refs = [refs[3 * i : 3 * i + 3] for i in range(olds)]
    sums_ref, out_ref, new_ref = refs[3 * olds :]
    chip = me_ref[0] >> 1
    rows = fresh * slots
    padded, width = new_ref.shape
    half = out_ref.shape[2] // 2
    new_ref[rows:, :] = jnp.zeros((padded - rows, width), bf16)
    pieces = []
    for i, r in enumerate(partners):
        new_ref[i * slots : (i + 1) * slots, :] = unit_rows(raw_refs[i])
        pieces.append(cluster_rows(bound_ref, r, slots))
    new_cids = jnp.concatenate(pieces, axis=0)
    cid_row = cluster_lanes(bound_ref, partners, slots, padded)
    sums = sums_ref[...] + member_sums(cid_row, new_ref[...])
    centroid = (sums / jnp.maximum(total_ref[:, 0:1], 1.0)).astype(bf16)
    centroid = jnp.concatenate([centroid, jnp.zeros_like(centroid)], axis=0)
    new_ref[rows : rows + STEP, :] = centroid
    left = new_ref[0 : rows + STEP, :]
    label = iota((8, LANES), 0).astype(f32)
    row = iota((rows, LANES), 0)
    lane = iota((rows, LANES), 1)

    def write(names, best_line, gap_line):
        for i, r in enumerate(names):
            at = slice(i * slots, (i + 1) * slots)
            for j, line in enumerate((best_line, gap_line)):
                piece = line[:, at]
                for core in range(2):
                    out_ref[2 * (r ^ chip) + core, :, j * half : j * half + slots] = piece

    best_new = jnp.full((rows, LANES), -1.0, f32)
    for names, (unit_ref, best_ref, cid_ref) in zip(earlier, old_refs):
        scores = nt_dot(left, unit_ref[...])
        bests, gaps = [], []
        for first in range(0, unit_ref.shape[0], LANES):
            at = slice(first, first + LANES)
            cids = cid_ref[:, at]
            part = jnp.where(new_cids == cids, scores[0:rows, at], -1.0)
            best_new = jnp.maximum(best_new, part)
            bests.append(jnp.maximum(best_ref[:, at], jnp.max(part, axis=0, keepdims=True)))
            dots = jnp.where(label == cids, scores[rows : rows + 8, at], 0.0)
            gaps.append(1.0 - jnp.sum(dots, axis=0, keepdims=True))
        write(names, jnp.concatenate(bests, axis=1), jnp.concatenate(gaps, axis=1))
    scores = nt_dot(left, new_ref[...])
    gaps = []
    for first in range(0, padded, LANES):
        at = slice(first, first + LANES)
        cids = cid_row[:, at]
        allowed = (new_cids == cids) & (row != lane + first)
        best_new = jnp.maximum(best_new, jnp.where(allowed, scores[0:rows, at], -1.0))
        dots = jnp.where(label == cids, scores[rows : rows + 8, at], 0.0)
        gaps.append(1.0 - jnp.sum(dots, axis=0, keepdims=True))
    best = jnp.max(best_new, axis=1, keepdims=True)
    bests = [to_line(best, first) for first in range(0, rows, LANES)]
    write(partners, jnp.concatenate(bests, axis=1), jnp.concatenate(gaps, axis=1))


def finish(me, bound, total, blocks, partners, earlier, state):
    slots, width = blocks[0].shape
    owners = 2 * bound.shape[0]
    units, accs, _, sums = state
    rows = len(blocks) * slots
    padded = round_up(rows + STEP, LANES)
    best_lines, cid_lines = lines(bound, earlier, slots, accs)
    old = [x for group in zip(units, best_lines, cid_lines) for x in group]
    args = [me, bound, total, *blocks, *old, sums]
    return pl.pallas_call(
        functools.partial(finish_kernel, slots, partners, earlier),
        out_shape=jax.ShapeDtypeStruct((owners, 1, 2 * round_up(slots, LANES)), f32),
        in_specs=[SMEM] + [VMEM] * (len(args) - 1),
        out_specs=VMEM,
        scratch_shapes=[pltpu.VMEM((padded, width), bf16)],
        compiler_params=pltpu.CompilerParams(vmem_limit_bytes=(36 if slots < 400 else 58) * MIB),
        cost_estimate=pl.CostEstimate(
            flops=2 * owners * slots * padded * width,
            bytes_accessed=2 * owners * slots * width,
            transcendentals=rows,
        ),
        name="finish_rows",
    )(*args)


def restore_kernel(slots, owner_ref, slot_ref, back_ref, best_ref, gap_ref):
    rows = owner_ref.shape[1]
    owners, _, width = back_ref.shape
    half = width // 2
    from_owner = to_bf16(owner_ref[...] == iota((owners, rows), 0))
    from_owner = jnp.concatenate([from_owner] * 3, axis=0)
    at_slot = slot_ref[...] == iota((slots, rows), 0)
    back = jnp.concatenate([back_ref[s] for s in range(owners)], axis=0)
    part0 = back.astype(bf16)
    rest = back - part0.astype(f32)
    part1 = rest.astype(bf16)
    part2 = (rest - part1.astype(f32)).astype(bf16)
    parts = jnp.concatenate([part0, part1, part2], axis=0)
    for i, ref in enumerate((best_ref, gap_ref)):
        table = lax.dot_general(
            parts[:, i * half : i * half + slots],
            from_owner,
            (((0,), (0,)), ((), ())),
            preferred_element_type=f32,
        )
        ref[...] = jnp.sum(jnp.where(at_slot, table, 0.0), axis=0, keepdims=True)


def restore(owner_row, slot_row, back, slots):
    return pl.pallas_call(
        functools.partial(restore_kernel, slots),
        out_shape=(jax.ShapeDtypeStruct(owner_row.shape, f32),) * 2,
        in_specs=[VMEM] * 3,
        out_specs=(VMEM, VMEM),
        compiler_params=pltpu.CompilerParams(vmem_limit_bytes=28 * MIB),
        name="restore_rows",
    )(owner_row, slot_row, back)


def exchange(x):
    return lax.all_to_all(x, "owner", split_axis=0, concat_axis=0, tiled=True)


def exchange_chips(x):
    chips = lax.axis_size("owner") // 2
    cores = [[2 * chip + core for chip in range(chips)] for core in range(2)]
    return lax.all_to_all(
        x, "owner", split_axis=0, concat_axis=0, axis_index_groups=cores, tiled=True
    )


def swap(block, r):
    owners = lax.axis_size("owner")
    return lax.ppermute(block, "owner", [(s, s ^ (2 * r)) for s in range(owners)])


def swap_together(blocks):
    chips = len(blocks)
    order = jnp.arange(chips, dtype=i32) ^ (lax.axis_index("owner").astype(i32) >> 1)
    arrived = exchange_chips(jnp.stack(blocks)[order])[order]
    return [arrived[r] for r in range(chips)]


def swap_cores(x):
    owners = lax.axis_size("owner")
    return lax.ppermute(x, "owner", [(s, s ^ 1) for s in range(owners)])


def local(embeddings, cluster_ids):
    rows = embeddings.shape[0]
    owners = lax.axis_size("owner")
    chips = owners // 2
    clusters = CL_DEV * owners
    row_limit = 2 * rows // clusters
    most = round_up(2 * CL_DEV * row_limit, STEP)
    usual = min(most, round_up(17 * rows // (8 * owners), STEP))
    few = chips <= MAX_PERMUTES
    me = lax.axis_index("owner").astype(i32).reshape(1)
    ids0 = cluster_ids.reshape(1, rows)
    ids1 = swap_cores(ids0)
    mine, ids1 = lax.optimization_barrier((embeddings, ids1))
    other = swap_cores(mine)
    counts, rank0, rank1 = count_rows(me, ids0, ids1, chips, clusters)
    counts = exchange_chips(counts)
    both = (embeddings, other)
    *places, bound, total, load = assign(me, counts, rank0, rank1)
    owner_row, slot_row = places[0], places[2]

    half = chips // 2
    far = list(range(chips - 1, half - 1, -1))
    near = list(range(half - 1, 0, -1))
    sent = far[:2] + near + far[2:] + [0]
    share = max(half // 4, 1)
    groups = [[0] + near, far[: 2 * share], far[2 * share : 3 * share], far[3 * share :]]

    def compare(slots, apart):
        blocks = [None] * chips
        here = list(places)
        for r in sent:
            blocks[r] = pack(me, here, both, r, slots)
            here[0], blocks[r] = lax.optimization_barrier((here[0], blocks[r]))
        if apart:
            arrived = blocks[:1] + [None] * (chips - 1)
            for r in sent[:-1]:
                if r in far[2:]:
                    before = far[far.index(r) - 2]
                    blocks[r], arrived[before] = lax.optimization_barrier(
                        (blocks[r], arrived[before])
                    )
                arrived[r] = swap(blocks[r], r)
        else:
            arrived = swap_together(blocks)
        state = ([], [], [], None)
        for group in groups[:-1]:
            state = score(bound, [arrived[r] for r in group], group, state)
        last = groups[-1]
        answers = finish(
            me, bound, total, [arrived[r] for r in last], last, groups[:-1], state
        )
        return restore(owner_row, slot_row, exchange(answers), slots)

    best, gap = compare(usual, few)
    if usual < most:
        best, gap = lax.cond(
            load[0, 0] <= usual, lambda: (best, gap), lambda: compare(most, False)
        )
    return best.reshape(rows), gap.reshape(rows)


def solution(mesh):
    return jax.shard_map(
        local,
        mesh=mesh,
        in_specs=(P(("groups", "owner"), None), P(("groups", "owner"))),
        out_specs=(P(("groups", "owner")), P(("groups", "owner"))),
        check_vma=False,
    )
```

```python
import functools

import jax
import jax.numpy as jnp
from jax import lax
from jax.experimental import pallas as pl
from jax.experimental.pallas import tpu as pltpu
from jax.sharding import PartitionSpec as P

CL_DEV = 4
VARIANTS = 32
STEP = 16
TILE = 256
LANES = 128
MAX_PERMUTES = 8
RANKS = 4096
MIB = 1 << 20

epsilon = 1e-06
f32 = jnp.float32
bf16 = jnp.bfloat16
i32 = jnp.int32
VMEM = pl.BlockSpec(memory_space=pltpu.VMEM)
SMEM = pl.BlockSpec(memory_space=pltpu.SMEM)


def iota(shape, axis):
    return lax.broadcasted_iota(i32, shape, axis)


def round_up(value, unit):
    return -(-value // unit) * unit


def nt_dot(a, b):
    return lax.dot_general(a, b, (((1,), (1,)), ((), ())), preferred_element_type=f32)


def mm(a, b):
    return jnp.dot(a, b, preferred_element_type=f32)


def to_bf16(mask):
    return mask.astype(f32).astype(bf16)


def rank_rows(ids_ref, rank_ref, clusters):
    label = iota((clusters, TILE), 0)
    upto = to_bf16(iota((TILE, TILE), 0) <= iota((TILE, TILE), 1))
    total = jnp.zeros((clusters, 1), f32)
    for first in range(0, ids_ref.shape[1], TILE):
        at = slice(first, first + TILE)
        hot = ids_ref[:, at] == label
        prefix = mm(to_bf16(hot), upto)
        rank = jnp.sum(jnp.where(hot, prefix + total - 1.0, 0.0), axis=0, keepdims=True)
        rank_ref[:, at] = ids_ref[:, at] * RANKS + rank.astype(i32)
        total = total + prefix[:, TILE - 1 :]
    return total


def own_kernel(ids_ref, rank_ref, total_ref):
    total = rank_rows(ids_ref, rank_ref, total_ref.shape[0])
    total_ref[...] = jnp.broadcast_to(total, total_ref.shape)


def rank_own(ids, clusters):
    return pl.pallas_call(
        own_kernel,
        out_shape=(
            jax.ShapeDtypeStruct(ids.shape, i32),
            jax.ShapeDtypeStruct((clusters, LANES), f32),
        ),
        in_specs=[VMEM],
        out_specs=(VMEM, VMEM),
        compiler_params=pltpu.CompilerParams(vmem_limit_bytes=16 * MIB),
        cost_estimate=pl.CostEstimate(flops=1_000_000_000, bytes_accessed=1 << 20, transcendentals=0),
        name="rank_own",
    )(ids)


def count_kernel(
    me_ref, ids1_ref, own_ref, total_ref, counts_ref, rank0_ref, rank1_ref
):
    rows = ids1_ref.shape[1]
    chips, _, clusters = counts_ref.shape
    core = me_ref[0] & 1
    label = iota((clusters, TILE), 0)
    total0 = total_ref[:, 0:1]
    total1 = rank_rows(ids1_ref, rank1_ref, clusters)
    square = (clusters, clusters)
    eye = iota(square, 0) == iota(square, 1)
    total_row = jnp.sum(jnp.where(eye, total0 + total1, 0.0), axis=0, keepdims=True).astype(i32)
    for chip in range(chips):
        counts_ref[chip] = total_row
    for from_ref, rank_ref, ahead in (
        (own_ref, rank0_ref, jnp.where(core == 1, total1, 0.0)),
        (rank1_ref, rank1_ref, jnp.where(core == 0, total0, 0.0)),
    ):
        for first in range(0, rows, TILE):
            at = slice(first, first + TILE)
            rank = from_ref[:, at]
            more = jnp.where((rank // RANKS) == label, ahead, 0.0)
            rank_ref[:, at] = rank + jnp.sum(more, axis=0, keepdims=True).astype(i32)


def count_rows(me, ids1, own, total, chips, clusters):
    return pl.pallas_call(
        count_kernel,
        out_shape=(
            jax.ShapeDtypeStruct((chips, 1, clusters), i32),
            jax.ShapeDtypeStruct(ids1.shape, i32),
            jax.ShapeDtypeStruct(ids1.shape, i32),
        ),
        in_specs=[SMEM, VMEM, VMEM, VMEM],
        out_specs=(VMEM,) * 3,
        compiler_params=pltpu.CompilerParams(vmem_limit_bytes=16 * MIB),
        cost_estimate=pl.CostEstimate(flops=8_000_000_000, bytes_accessed=1 << 20, transcendentals=0),
        name="count_rows",
    )(me, ids1, own, total)


def assign_kernel(
    me_ref,
    counts_ref,
    rank0_ref,
    rank1_ref,
    owner0_ref,
    owner1_ref,
    slot0_ref,
    slot1_ref,
    bound_ref,
    total_ref,
    load_ref,
):
    chips, _, clusters = counts_ref.shape
    owners = 2 * chips
    rows = rank0_ref.shape[1]
    shift = owners.bit_length() - 1
    me = me_ref[0]
    chip = me >> 1
    count = jnp.concatenate([counts_ref[s].astype(f32) for s in range(chips)], axis=0)
    count16 = count.astype(bf16)
    square = (clusters, clusters)
    sub, lane = iota(square, 0), iota(square, 1)
    total_row = jnp.sum(count, axis=0, keepdims=True)
    total_col = jnp.sum(jnp.where(sub == lane, total_row, 0.0), axis=1, keepdims=True)
    tie = total_row == total_col
    outranks_col = (total_row > total_col) | (tie & (lane < sub))
    outranks_row = (total_col > total_row) | (tie & (sub < lane))
    rank_col = jnp.sum(outranks_col.astype(f32), axis=1, keepdims=True).astype(i32)
    rank_row = jnp.sum(outranks_row.astype(f32), axis=0, keepdims=True).astype(i32)

    layer_col, layer_row = rank_col >> shift, rank_row >> shift

    def plain(rank, layer):
        return (rank & (owners - 1)) ^ jnp.where((layer & 1) == 1, owners - 1, 0)

    def flip(p, variant):
        bits = (variant >> (p - 1)) & 1
        if p < CL_DEV - 1:
            bits = bits + 2 * ((variant >> (p + CL_DEV - 2)) & 1)
        return bits

    lanes = iota((1, VARIANTS * owners), 1)
    target = lanes & (owners - 1)
    for p in range(1, CL_DEV):
        swapped = (lanes & (owners - 1)) ^ flip(p, lanes >> shift)
        target = jnp.where(layer_col == p, swapped, target)
    tried = plain(rank_col, layer_col) == target
    load = jnp.max(mm(count16, to_bf16(tried)), axis=0, keepdims=True)
    by_variant = (VARIANTS, VARIANTS * owners)
    worst = jnp.max(
        jnp.where((iota(by_variant, 1) >> shift) == iota(by_variant, 0), load, 0.0),
        axis=1,
        keepdims=True,
    )
    best = jnp.min(worst, axis=0, keepdims=True)
    chosen = jnp.min(
        jnp.where(worst == best, iota((VARIANTS, 1), 0), VARIANTS), axis=0, keepdims=True
    )

    def owner_of(rank, layer):
        swaps = jnp.zeros_like(rank)
        for p in range(1, CL_DEV):
            swaps = jnp.where(layer == p, flip(p, chosen), swaps)
        return plain(rank, layer) ^ swaps

    owner_col = owner_of(rank_col, layer_col)
    owner_row = owner_of(rank_row, layer_row)
    load_ref[...] = jnp.broadcast_to(best, load_ref.shape).astype(i32)

    mine = jnp.sum(jnp.where(iota(count.shape, 0) == chip, count, 0.0), axis=0, keepdims=True)
    earlier = (owner_row == owner_col) & (layer_row < layer_col)
    offset_col = jnp.sum(jnp.where(earlier, mine, 0.0), axis=1, keepdims=True)
    for rank_ref, owner_ref, slot_ref in (
        (rank0_ref, owner0_ref, slot0_ref),
        (rank1_ref, owner1_ref, slot1_ref),
    ):
        hot = (rank_ref[...] // RANKS) == iota((clusters, rows), 0)
        owner_ref[...] = jnp.sum(
            jnp.where(hot, owner_col.astype(f32), 0.0), axis=0, keepdims=True
        ).astype(i32)
        slot_ref[...] = jnp.sum(jnp.where(hot, offset_col, 0.0), axis=0, keepdims=True).astype(
            i32
        ) + (rank_ref[...] & (RANKS - 1))

    select = (owner_col == me) & (layer_col <= iota((clusters, LANES), 1))
    turn = iota((chips, chips), 1) == (iota((chips, chips), 0) ^ chip)
    turned = mm(to_bf16(turn), count16).astype(bf16)
    bound_ref[...] = mm(turned, to_bf16(select))
    own = (owner_row == me) & (layer_row == iota((8, clusters), 0))
    total_ref[...] = jnp.broadcast_to(
        jnp.sum(jnp.where(own, total_row, 0.0), axis=1, keepdims=True), total_ref.shape
    )


def assign(me, counts, rank0, rank1):
    chips, _, clusters = counts.shape
    line = jax.ShapeDtypeStruct(rank0.shape, i32)
    return pl.pallas_call(
        assign_kernel,
        out_shape=(
            line,
            line,
            line,
            line,
            jax.ShapeDtypeStruct((chips, LANES), f32),
            jax.ShapeDtypeStruct((8, LANES), f32),
            jax.ShapeDtypeStruct((1, LANES), i32),
        ),
        in_specs=[SMEM, VMEM, VMEM, VMEM],
        out_specs=(VMEM,) * 7,
        compiler_params=pltpu.CompilerParams(vmem_limit_bytes=16 * MIB),
        name="assign",
    )(me, counts, rank0, rank1)


def pack_kernel(
    partner, me_ref, owner0_ref, owner1_ref, slot0_ref, slot1_ref, rows0_ref, rows1_ref, out_ref
):
    slots = out_ref.shape[0]
    rows = rows0_ref.shape[0]
    target = me_ref[0] ^ (2 * partner)
    slot = iota((slots, rows), 0)
    total = None
    for owner_ref, slot_ref, rows_ref in (
        (owner0_ref, slot0_ref, rows0_ref),
        (owner1_ref, slot1_ref, rows1_ref),
    ):
        key = jnp.where(owner_ref[...] == target, slot_ref[...], -1)
        part = mm(to_bf16(slot == key), rows_ref[...])
        total = part if total is None else total + part
    out_ref[...] = total.astype(bf16)


def pack(me, places, both, partner, slots):
    width = both[0].shape[1]
    return pl.pallas_call(
        functools.partial(pack_kernel, partner),
        out_shape=jax.ShapeDtypeStruct((slots, width), bf16),
        in_specs=[SMEM] + [VMEM] * 6,
        out_specs=VMEM,
        compiler_params=pltpu.CompilerParams(vmem_limit_bytes=24 * MIB),
        cost_estimate=pl.CostEstimate(flops=slots, bytes_accessed=slots, transcendentals=0),
        name="pack_rows",
    )(me, *places, *both)


def unit_rows(ref):
    x = ref[...].astype(f32)
    scale = lax.rsqrt(jnp.sum(x * x, axis=1, keepdims=True) + epsilon)
    return (x * scale).astype(bf16)


def cluster_lanes(bound_ref, partners, slots, width):
    lane = iota((1, width), 1).astype(f32)
    result = jnp.where(lane < len(partners) * slots, 0.0, -1.0)
    for i, r in enumerate(partners):
        for k in range(CL_DEV):
            first = bound_ref[r : r + 1, k : k + 1] + float(i * slots)
            result = result + ((lane >= first) & (lane < float((i + 1) * slots))).astype(f32)
    return result


def cluster_rows(bound_ref, r, slots):
    slot = iota((slots, LANES), 0).astype(f32)
    result = jnp.zeros((slots, LANES), f32)
    for k in range(CL_DEV):
        result = result + (slot >= bound_ref[r : r + 1, k : k + 1]).astype(f32)
    return result


def score_group(new_ref, new_cids, olds, cid_row, slots_new):
    padded = new_ref.shape[0]
    groups = padded // LANES
    new = new_ref[...]

    def folded(scores, cids, skip_same):
        rows = scores.shape[0]
        row = iota((rows, LANES), 0)
        lane = iota((rows, LANES), 1)
        best, cols = None, []
        for g in range(groups):
            at = slice(g * LANES, (g + 1) * LANES)
            allowed = cids == cid_row[:, at]
            if skip_same:
                allowed = allowed & (row != lane + g * LANES)
            part = jnp.where(allowed, scores[:, at], -1.0)
            best = part if best is None else jnp.maximum(best, part)
            cols.append(jnp.max(part, axis=0, keepdims=True))
        return best, cols

    columns = None
    results = []
    for unit_ref, acc_ref, cid_ref in olds:
        scores = nt_dot(unit_ref[0 : acc_ref.shape[0], :], new)
        best, cols = folded(scores, cid_ref[...], False)
        columns = cols if columns is None else [jnp.maximum(a, b) for a, b in zip(columns, cols)]
        results.append(jnp.maximum(acc_ref[...], best))
    scores = nt_dot(new[0:slots_new], new)
    best, _ = folded(scores, new_cids, True)
    if columns is not None:
        row = iota((slots_new, LANES), 0)
        lane = iota((slots_new, LANES), 1)
        for g, col in enumerate(columns):
            best = jnp.maximum(best, jnp.where(row == lane + g * LANES, col, -1.0))
    results.append(best)
    return results


def member_sums(cid_row, new):
    hot = to_bf16(cid_row == iota((8, cid_row.shape[1]), 0).astype(f32))
    return mm(hot, new)


def score_kernel(slots, partners, olds, bound_ref, *refs):
    fresh = len(partners)
    raw_refs, refs = refs[:fresh], refs[fresh:]
    old_refs = [refs[3 * i : 3 * i + 3] for i in range(olds)]
    refs = refs[3 * olds :]
    if olds:
        sums_ref, refs = refs[0], refs[1:]
    unit_ref, acc_ref, cid_ref, sums_out = refs[:4]
    old_accs = refs[4 : 4 + olds]
    new_ref = refs[4 + olds]
    rows = fresh * slots
    for i, r in enumerate(partners):
        at = slice(i * slots, (i + 1) * slots)
        new_ref[at, :] = unit_rows(raw_refs[i])
        cid_ref[at, :] = cluster_rows(bound_ref, r, slots)
    padded = new_ref.shape[0]
    if padded > rows:
        new_ref[rows:, :] = jnp.zeros((padded - rows, new_ref.shape[1]), bf16)
    unit_ref[...] = new_ref[...]
    cid_row = cluster_lanes(bound_ref, partners, slots, padded)
    results = score_group(new_ref, cid_ref[...], old_refs, cid_row, rows)
    for best, ref in zip(results, list(old_accs) + [acc_ref]):
        ref[...] = best
    sums = member_sums(cid_row, new_ref[...])
    sums_out[...] = sums + sums_ref[...] if olds else sums


def score(bound, blocks, partners, state):
    slots, width = blocks[0].shape
    units, accs, cids, sums = state
    rows = len(blocks) * slots
    padded = round_up(rows, LANES)
    old = [x for group in zip(units, accs, cids) for x in group]
    old_rows = sum(a.shape[0] for a in accs)
    acc_shapes = [jax.ShapeDtypeStruct(a.shape, f32) for a in accs]
    out_shape = (
        jax.ShapeDtypeStruct((padded, width), bf16),
        jax.ShapeDtypeStruct((rows, LANES), f32),
        jax.ShapeDtypeStruct((rows, LANES), f32),
        jax.ShapeDtypeStruct((8, width), f32),
        *acc_shapes,
    )
    args = [bound, *blocks, *old] + ([sums] if units else [])
    out = pl.pallas_call(
        functools.partial(score_kernel, slots, partners, len(units)),
        out_shape=out_shape,
        in_specs=[VMEM] * len(args),
        out_specs=(VMEM,) * len(out_shape),
        scratch_shapes=[pltpu.VMEM((padded, width), bf16)],
        compiler_params=pltpu.CompilerParams(vmem_limit_bytes=(36 if slots < 400 else 58) * MIB),
        cost_estimate=pl.CostEstimate(
            flops=2 * (old_rows + rows) * padded,
            bytes_accessed=2 * (old_rows + rows),
            transcendentals=rows,
        ),
        name="score_rows",
    )(*args)
    return units + [out[0]], list(out[4:]) + [out[1]], cids + [out[2]], out[3]


def diagonal():
    return iota((LANES, LANES), 0) == iota((LANES, LANES), 1)


def to_line(col, first):
    piece = col[first : first + LANES]
    return jnp.sum(jnp.where(diagonal()[: piece.shape[0]], piece, 0.0), axis=0, keepdims=True)


def line_kernel(slots, names, bound_ref, *refs):
    count = len(names)
    for i, partners in enumerate(names):
        acc_ref, best_ref, cid_ref = refs[i], refs[count + 2 * i], refs[count + 2 * i + 1]
        best = jnp.max(acc_ref[...], axis=1, keepdims=True)
        for first in range(0, best_ref.shape[1], LANES):
            best_ref[:, first : first + LANES] = to_line(best, first)
        cid_ref[...] = cluster_lanes(bound_ref, partners, slots, cid_ref.shape[1])


def lines(bound, names, slots, accs):
    widths = [round_up(acc.shape[0], LANES) for acc in accs]
    out = pl.pallas_call(
        functools.partial(line_kernel, slots, names),
        out_shape=tuple(jax.ShapeDtypeStruct((1, w), f32) for w in widths for _ in range(2)),
        in_specs=[VMEM] * (1 + len(accs)),
        out_specs=(VMEM,) * (2 * len(accs)),
        compiler_params=pltpu.CompilerParams(vmem_limit_bytes=16 * MIB),
        name="line_rows",
    )(bound, *accs)
    return out[0::2], out[1::2]


def finish_kernel(slots, partners, earlier, me_ref, bound_ref, total_ref, *refs):
    fresh = len(partners)
    olds = len(earlier)
    raw_refs, refs = refs[:fresh], refs[fresh:]
    old_refs = [refs[3 * i : 3 * i + 3] for i in range(olds)]
    sums_ref, out_ref, new_ref = refs[3 * olds :]
    chip = me_ref[0] >> 1
    rows = fresh * slots
    padded, width = new_ref.shape
    half = out_ref.shape[2] // 2
    new_ref[rows:, :] = jnp.zeros((padded - rows, width), bf16)
    pieces = []
    for i, r in enumerate(partners):
        new_ref[i * slots : (i + 1) * slots, :] = unit_rows(raw_refs[i])
        pieces.append(cluster_rows(bound_ref, r, slots))
    new_cids = jnp.concatenate(pieces, axis=0)
    cid_row = cluster_lanes(bound_ref, partners, slots, padded)
    sums = sums_ref[...] + member_sums(cid_row, new_ref[...])
    centroid = (sums / jnp.maximum(total_ref[:, 0:1], 1.0)).astype(bf16)
    centroid = jnp.concatenate([centroid, jnp.zeros_like(centroid)], axis=0)
    new_ref[rows : rows + STEP, :] = centroid
    left = new_ref[0 : rows + STEP, :]
    label = iota((8, LANES), 0).astype(f32)
    row = iota((rows, LANES), 0)
    lane = iota((rows, LANES), 1)

    def write(names, best_line, gap_line):
        for i, r in enumerate(names):
            at = slice(i * slots, (i + 1) * slots)
            for j, line in enumerate((best_line, gap_line)):
                piece = line[:, at]
                for core in range(2):
                    out_ref[2 * (r ^ chip) + core, :, j * half : j * half + slots] = piece

    best_new = jnp.full((rows, LANES), -1.0, f32)
    for names, (unit_ref, best_ref, cid_ref) in zip(earlier, old_refs):
        scores = nt_dot(left, unit_ref[...])
        bests, gaps = [], []
        for first in range(0, unit_ref.shape[0], LANES):
            at = slice(first, first + LANES)
            cids = cid_ref[:, at]
            part = jnp.where(new_cids == cids, scores[0:rows, at], -1.0)
            best_new = jnp.maximum(best_new, part)
            bests.append(jnp.maximum(best_ref[:, at], jnp.max(part, axis=0, keepdims=True)))
            dots = jnp.where(label == cids, scores[rows : rows + 8, at], 0.0)
            gaps.append(1.0 - jnp.sum(dots, axis=0, keepdims=True))
        write(names, jnp.concatenate(bests, axis=1), jnp.concatenate(gaps, axis=1))
    scores = nt_dot(left, new_ref[...])
    gaps = []
    for first in range(0, padded, LANES):
        at = slice(first, first + LANES)
        cids = cid_row[:, at]
        allowed = (new_cids == cids) & (row != lane + first)
        best_new = jnp.maximum(best_new, jnp.where(allowed, scores[0:rows, at], -1.0))
        dots = jnp.where(label == cids, scores[rows : rows + 8, at], 0.0)
        gaps.append(1.0 - jnp.sum(dots, axis=0, keepdims=True))
    best = jnp.max(best_new, axis=1, keepdims=True)
    bests = [to_line(best, first) for first in range(0, rows, LANES)]
    write(partners, jnp.concatenate(bests, axis=1), jnp.concatenate(gaps, axis=1))


def finish(me, bound, total, blocks, partners, earlier, state):
    slots, width = blocks[0].shape
    owners = 2 * bound.shape[0]
    units, accs, _, sums = state
    rows = len(blocks) * slots
    padded = round_up(rows + STEP, LANES)
    best_lines, cid_lines = lines(bound, earlier, slots, accs)
    old = [x for group in zip(units, best_lines, cid_lines) for x in group]
    args = [me, bound, total, *blocks, *old, sums]
    return pl.pallas_call(
        functools.partial(finish_kernel, slots, partners, earlier),
        out_shape=jax.ShapeDtypeStruct((owners, 1, 2 * round_up(slots, LANES)), f32),
        in_specs=[SMEM] + [VMEM] * (len(args) - 1),
        out_specs=VMEM,
        scratch_shapes=[pltpu.VMEM((padded, width), bf16)],
        compiler_params=pltpu.CompilerParams(vmem_limit_bytes=(36 if slots < 400 else 58) * MIB),
        cost_estimate=pl.CostEstimate(
            flops=2 * owners * slots * padded * width,
            bytes_accessed=2 * owners * slots * width,
            transcendentals=rows,
        ),
        name="finish_rows",
    )(*args)


def restore_kernel(slots, owner_ref, slot_ref, back_ref, best_ref, gap_ref):
    rows = owner_ref.shape[1]
    owners, _, width = back_ref.shape
    half = width // 2
    from_owner = to_bf16(owner_ref[...] == iota((owners, rows), 0))
    from_owner = jnp.concatenate([from_owner] * 3, axis=0)
    at_slot = slot_ref[...] == iota((slots, rows), 0)
    back = jnp.concatenate([back_ref[s] for s in range(owners)], axis=0)
    part0 = back.astype(bf16)
    rest = back - part0.astype(f32)
    part1 = rest.astype(bf16)
    part2 = (rest - part1.astype(f32)).astype(bf16)
    parts = jnp.concatenate([part0, part1, part2], axis=0)
    for i, ref in enumerate((best_ref, gap_ref)):
        table = lax.dot_general(
            parts[:, i * half : i * half + slots],
            from_owner,
            (((0,), (0,)), ((), ())),
            preferred_element_type=f32,
        )
        ref[...] = jnp.sum(jnp.where(at_slot, table, 0.0), axis=0, keepdims=True)


def restore(owner_row, slot_row, back, slots):
    return pl.pallas_call(
        functools.partial(restore_kernel, slots),
        out_shape=(jax.ShapeDtypeStruct(owner_row.shape, f32),) * 2,
        in_specs=[VMEM] * 3,
        out_specs=(VMEM, VMEM),
        compiler_params=pltpu.CompilerParams(vmem_limit_bytes=28 * MIB),
        name="restore_rows",
    )(owner_row, slot_row, back)


def exchange(x):
    return lax.all_to_all(x, "owner", split_axis=0, concat_axis=0, tiled=True)


def exchange_chips(x):
    chips = lax.axis_size("owner") // 2
    cores = [[2 * chip + core for chip in range(chips)] for core in range(2)]
    return lax.all_to_all(
        x, "owner", split_axis=0, concat_axis=0, axis_index_groups=cores, tiled=True
    )


def swap(block, r):
    owners = lax.axis_size("owner")
    return lax.ppermute(block, "owner", [(s, s ^ (2 * r)) for s in range(owners)])


def swap_together(blocks):
    chips = len(blocks)
    order = jnp.arange(chips, dtype=i32) ^ (lax.axis_index("owner").astype(i32) >> 1)
    arrived = exchange_chips(jnp.stack(blocks)[order])[order]
    return [arrived[r] for r in range(chips)]


def swap_cores(x):
    owners = lax.axis_size("owner")
    return lax.ppermute(x, "owner", [(s, s ^ 1) for s in range(owners)])


def local(embeddings, cluster_ids):
    rows = embeddings.shape[0]
    owners = lax.axis_size("owner")
    chips = owners // 2
    clusters = CL_DEV * owners
    row_limit = 2 * rows // clusters
    most = round_up(2 * CL_DEV * row_limit, STEP)
    usual = min(most, round_up(17 * rows // (8 * owners), STEP))
    few = chips <= MAX_PERMUTES
    me = lax.axis_index("owner").astype(i32).reshape(1)
    ids0 = cluster_ids.reshape(1, rows)
    ids1 = swap_cores(ids0)
    own, own_total = rank_own(ids0, clusters)
    mine, ids1, own = lax.optimization_barrier((embeddings, ids1, own))
    other = swap_cores(mine)
    counts, rank0, rank1 = count_rows(me, ids1, own, own_total, chips, clusters)
    counts = exchange_chips(counts)
    both = (embeddings, other)
    *places, bound, total, load = assign(me, counts, rank0, rank1)
    owner_row, slot_row = places[0], places[2]

    half = chips // 2
    far = list(range(chips - 1, half - 1, -1))
    near = list(range(half - 1, 0, -1))
    sent = far[:2] + near + far[2:] + [0]
    share = max(half // 4, 1)
    groups = [[0] + near, far[: 2 * share], far[2 * share : 3 * share], far[3 * share :]]

    def compare(slots, apart):
        blocks = [None] * chips
        here = list(places)
        for r in sent:
            blocks[r] = pack(me, here, both, r, slots)
            here[0], blocks[r] = lax.optimization_barrier((here[0], blocks[r]))
        if apart:
            arrived = blocks[:1] + [None] * (chips - 1)
            for r in sent[:-1]:
                if r in far[2:]:
                    before = far[far.index(r) - 2]
                    blocks[r], arrived[before] = lax.optimization_barrier(
                        (blocks[r], arrived[before])
                    )
                arrived[r] = swap(blocks[r], r)
        else:
            arrived = swap_together(blocks)
        state = ([], [], [], None)
        for group in groups[:-1]:
            state = score(bound, [arrived[r] for r in group], group, state)
        last = groups[-1]
        answers = finish(
            me, bound, total, [arrived[r] for r in last], last, groups[:-1], state
        )
        return restore(owner_row, slot_row, exchange(answers), slots)

    best, gap = compare(usual, few)
    if usual < most:
        best, gap = lax.cond(
            load[0, 0] <= usual, lambda: (best, gap), lambda: compare(most, False)
        )
    return best.reshape(rows), gap.reshape(rows)


def solution(mesh):
    return jax.shard_map(
        local,
        mesh=mesh,
        in_specs=(P(("groups", "owner"), None), P(("groups", "owner"))),
        out_specs=(P(("groups", "owner")), P(("groups", "owner"))),
        check_vma=False,
    )
```

```python
import functools

import jax
import jax.numpy as jnp
from jax import lax
from jax.experimental import pallas as pl
from jax.experimental.pallas import tpu as pltpu
from jax.sharding import PartitionSpec as P

CL_DEV = 4
VARIANTS = 32
STEP = 16
TILE = 256
LANES = 128
MAX_PERMUTES = 8
RANKS = 4096
MIB = 1 << 20

epsilon = 1e-06
f32 = jnp.float32
bf16 = jnp.bfloat16
i32 = jnp.int32
VMEM = pl.BlockSpec(memory_space=pltpu.VMEM)
SMEM = pl.BlockSpec(memory_space=pltpu.SMEM)


def iota(shape, axis):
    return lax.broadcasted_iota(i32, shape, axis)


def round_up(value, unit):
    return -(-value // unit) * unit


def nt_dot(a, b):
    return lax.dot_general(a, b, (((1,), (1,)), ((), ())), preferred_element_type=f32)


def mm(a, b):
    return jnp.dot(a, b, preferred_element_type=f32)


def to_bf16(mask):
    return mask.astype(f32).astype(bf16)


def rank_rows(ids_ref, rank_ref, clusters):
    label = iota((clusters, TILE), 0)
    upto = to_bf16(iota((TILE, TILE), 0) <= iota((TILE, TILE), 1))
    total = jnp.zeros((clusters, 1), f32)
    for first in range(0, ids_ref.shape[1], TILE):
        at = slice(first, first + TILE)
        hot = ids_ref[:, at] == label
        prefix = mm(to_bf16(hot), upto)
        rank = jnp.sum(jnp.where(hot, prefix + total - 1.0, 0.0), axis=0, keepdims=True)
        rank_ref[:, at] = ids_ref[:, at] * RANKS + rank.astype(i32)
        total = total + prefix[:, TILE - 1 :]
    return total


def own_kernel(ids_ref, rank_ref, total_ref):
    total = rank_rows(ids_ref, rank_ref, total_ref.shape[0])
    total_ref[...] = jnp.broadcast_to(total, total_ref.shape)


def rank_own(ids, clusters):
    return pl.pallas_call(
        own_kernel,
        out_shape=(
            jax.ShapeDtypeStruct(ids.shape, i32),
            jax.ShapeDtypeStruct((clusters, LANES), f32),
        ),
        in_specs=[VMEM],
        out_specs=(VMEM, VMEM),
        compiler_params=pltpu.CompilerParams(vmem_limit_bytes=16 * MIB),
        cost_estimate=pl.CostEstimate(flops=1_000_000_000, bytes_accessed=1 << 20, transcendentals=0),
        name="rank_own",
    )(ids)


def count_kernel(
    me_ref, ids1_ref, own_ref, total_ref, counts_ref, rank0_ref, rank1_ref
):
    rows = ids1_ref.shape[1]
    chips, _, clusters = counts_ref.shape
    core = me_ref[0] & 1
    label = iota((clusters, TILE), 0)
    total0 = total_ref[:, 0:1]
    total1 = rank_rows(ids1_ref, rank1_ref, clusters)
    square = (clusters, clusters)
    eye = iota(square, 0) == iota(square, 1)
    total_row = jnp.sum(jnp.where(eye, total0 + total1, 0.0), axis=0, keepdims=True).astype(i32)
    for chip in range(chips):
        counts_ref[chip] = total_row
    for from_ref, rank_ref, ahead in (
        (own_ref, rank0_ref, jnp.where(core == 1, total1, 0.0)),
        (rank1_ref, rank1_ref, jnp.where(core == 0, total0, 0.0)),
    ):
        for first in range(0, rows, TILE):
            at = slice(first, first + TILE)
            rank = from_ref[:, at]
            more = jnp.where((rank // RANKS) == label, ahead, 0.0)
            rank_ref[:, at] = rank + jnp.sum(more, axis=0, keepdims=True).astype(i32)


def count_rows(me, ids1, own, total, chips, clusters):
    return pl.pallas_call(
        count_kernel,
        out_shape=(
            jax.ShapeDtypeStruct((chips, 1, clusters), i32),
            jax.ShapeDtypeStruct(ids1.shape, i32),
            jax.ShapeDtypeStruct(ids1.shape, i32),
        ),
        in_specs=[SMEM, VMEM, VMEM, VMEM],
        out_specs=(VMEM,) * 3,
        compiler_params=pltpu.CompilerParams(vmem_limit_bytes=16 * MIB),
        cost_estimate=pl.CostEstimate(flops=8_000_000_000, bytes_accessed=1 << 20, transcendentals=0),
        name="count_rows",
    )(me, ids1, own, total)


def assign_kernel(
    me_ref,
    counts_ref,
    rank0_ref,
    rank1_ref,
    owner0_ref,
    owner1_ref,
    slot0_ref,
    slot1_ref,
    bound_ref,
    total_ref,
    load_ref,
):
    chips, _, clusters = counts_ref.shape
    owners = 2 * chips
    rows = rank0_ref.shape[1]
    shift = owners.bit_length() - 1
    me = me_ref[0]
    chip = me >> 1
    count = jnp.concatenate([counts_ref[s].astype(f32) for s in range(chips)], axis=0)
    count16 = count.astype(bf16)
    square = (clusters, clusters)
    sub, lane = iota(square, 0), iota(square, 1)
    total_row = jnp.sum(count, axis=0, keepdims=True)
    total_col = jnp.sum(jnp.where(sub == lane, total_row, 0.0), axis=1, keepdims=True)
    tie = total_row == total_col
    outranks_col = (total_row > total_col) | (tie & (lane < sub))
    outranks_row = (total_col > total_row) | (tie & (sub < lane))
    rank_col = jnp.sum(outranks_col.astype(f32), axis=1, keepdims=True).astype(i32)
    rank_row = jnp.sum(outranks_row.astype(f32), axis=0, keepdims=True).astype(i32)

    layer_col, layer_row = rank_col >> shift, rank_row >> shift

    def plain(rank, layer):
        return (rank & (owners - 1)) ^ jnp.where((layer & 1) == 1, owners - 1, 0)

    def flip(p, variant):
        bits = (variant >> (p - 1)) & 1
        if p < CL_DEV - 1:
            bits = bits + 2 * ((variant >> (p + CL_DEV - 2)) & 1)
        return bits

    lanes = iota((1, VARIANTS * owners), 1)
    target = lanes & (owners - 1)
    for p in range(1, CL_DEV):
        swapped = (lanes & (owners - 1)) ^ flip(p, lanes >> shift)
        target = jnp.where(layer_col == p, swapped, target)
    tried = plain(rank_col, layer_col) == target
    load = jnp.max(mm(count16, to_bf16(tried)), axis=0, keepdims=True)
    by_variant = (VARIANTS, VARIANTS * owners)
    worst = jnp.max(
        jnp.where((iota(by_variant, 1) >> shift) == iota(by_variant, 0), load, 0.0),
        axis=1,
        keepdims=True,
    )
    best = jnp.min(worst, axis=0, keepdims=True)
    chosen = jnp.min(
        jnp.where(worst == best, iota((VARIANTS, 1), 0), VARIANTS), axis=0, keepdims=True
    )

    def owner_of(rank, layer):
        swaps = jnp.zeros_like(rank)
        for p in range(1, CL_DEV):
            swaps = jnp.where(layer == p, flip(p, chosen), swaps)
        return plain(rank, layer) ^ swaps

    owner_col = owner_of(rank_col, layer_col)
    owner_row = owner_of(rank_row, layer_row)
    load_ref[...] = jnp.broadcast_to(best, load_ref.shape).astype(i32)

    mine = jnp.sum(jnp.where(iota(count.shape, 0) == chip, count, 0.0), axis=0, keepdims=True)
    earlier = (owner_row == owner_col) & (layer_row < layer_col)
    offset_col = jnp.sum(jnp.where(earlier, mine, 0.0), axis=1, keepdims=True)
    for rank_ref, owner_ref, slot_ref in (
        (rank0_ref, owner0_ref, slot0_ref),
        (rank1_ref, owner1_ref, slot1_ref),
    ):
        hot = (rank_ref[...] // RANKS) == iota((clusters, rows), 0)
        owner_ref[...] = jnp.sum(
            jnp.where(hot, owner_col.astype(f32), 0.0), axis=0, keepdims=True
        ).astype(i32)
        slot_ref[...] = jnp.sum(jnp.where(hot, offset_col, 0.0), axis=0, keepdims=True).astype(
            i32
        ) + (rank_ref[...] & (RANKS - 1))

    select = (owner_col == me) & (layer_col <= iota((clusters, LANES), 1))
    turn = iota((chips, chips), 1) == (iota((chips, chips), 0) ^ chip)
    turned = mm(to_bf16(turn), count16).astype(bf16)
    bound_ref[...] = mm(turned, to_bf16(select))
    own = (owner_row == me) & (layer_row == iota((8, clusters), 0))
    total_ref[...] = jnp.broadcast_to(
        jnp.sum(jnp.where(own, total_row, 0.0), axis=1, keepdims=True), total_ref.shape
    )


def assign(me, counts, rank0, rank1):
    chips, _, clusters = counts.shape
    line = jax.ShapeDtypeStruct(rank0.shape, i32)
    return pl.pallas_call(
        assign_kernel,
        out_shape=(
            line,
            line,
            line,
            line,
            jax.ShapeDtypeStruct((chips, LANES), f32),
            jax.ShapeDtypeStruct((8, LANES), f32),
            jax.ShapeDtypeStruct((1, LANES), i32),
        ),
        in_specs=[SMEM, VMEM, VMEM, VMEM],
        out_specs=(VMEM,) * 7,
        compiler_params=pltpu.CompilerParams(vmem_limit_bytes=16 * MIB),
        name="assign",
    )(me, counts, rank0, rank1)


def pack_kernel(
    partner, me_ref, owner0_ref, owner1_ref, slot0_ref, slot1_ref, rows0_ref, rows1_ref, out_ref
):
    slots = out_ref.shape[0]
    rows = rows0_ref.shape[0]
    target = me_ref[0] ^ (2 * partner)
    slot = iota((slots, rows), 0)
    total = None
    for owner_ref, slot_ref, rows_ref in (
        (owner0_ref, slot0_ref, rows0_ref),
        (owner1_ref, slot1_ref, rows1_ref),
    ):
        key = jnp.where(owner_ref[...] == target, slot_ref[...], -1)
        part = mm(to_bf16(slot == key), rows_ref[...])
        total = part if total is None else total + part
    out_ref[...] = total.astype(bf16)


def pack(me, places, both, partner, slots):
    width = both[0].shape[1]
    return pl.pallas_call(
        functools.partial(pack_kernel, partner),
        out_shape=jax.ShapeDtypeStruct((slots, width), bf16),
        in_specs=[SMEM] + [VMEM] * 6,
        out_specs=VMEM,
        compiler_params=pltpu.CompilerParams(vmem_limit_bytes=24 * MIB),
        cost_estimate=pl.CostEstimate(flops=slots, bytes_accessed=slots, transcendentals=0),
        name="pack_rows",
    )(me, *places, *both)


def unit_rows(ref):
    x = ref[...].astype(f32)
    scale = lax.rsqrt(jnp.sum(x * x, axis=1, keepdims=True) + epsilon)
    return (x * scale).astype(bf16)


def cluster_lanes(bound_ref, partners, slots, width):
    lane = iota((1, width), 1).astype(f32)
    result = jnp.where(lane < len(partners) * slots, 0.0, -1.0)
    for i, r in enumerate(partners):
        for k in range(CL_DEV):
            first = bound_ref[r : r + 1, k : k + 1] + float(i * slots)
            result = result + ((lane >= first) & (lane < float((i + 1) * slots))).astype(f32)
    return result


def cluster_rows(bound_ref, r, slots):
    slot = iota((slots, LANES), 0).astype(f32)
    result = jnp.zeros((slots, LANES), f32)
    for k in range(CL_DEV):
        result = result + (slot >= bound_ref[r : r + 1, k : k + 1]).astype(f32)
    return result


def score_group(new_ref, new_cids, olds, cid_row, slots_new):
    padded = new_ref.shape[0]
    groups = padded // LANES
    new = new_ref[...]

    def folded(scores, cids, skip_same):
        rows = scores.shape[0]
        row = iota((rows, LANES), 0)
        lane = iota((rows, LANES), 1)
        best, cols = None, []
        for g in range(groups):
            at = slice(g * LANES, (g + 1) * LANES)
            allowed = cids == cid_row[:, at]
            if skip_same:
                allowed = allowed & (row != lane + g * LANES)
            part = jnp.where(allowed, scores[:, at], -1.0)
            best = part if best is None else jnp.maximum(best, part)
            cols.append(jnp.max(part, axis=0, keepdims=True))
        return best, cols

    columns = None
    results = []
    for unit_ref, acc_ref, cid_ref in olds:
        scores = nt_dot(unit_ref[0 : acc_ref.shape[0], :], new)
        best, cols = folded(scores, cid_ref[...], False)
        columns = cols if columns is None else [jnp.maximum(a, b) for a, b in zip(columns, cols)]
        results.append(jnp.maximum(acc_ref[...], best))
    scores = nt_dot(new[0:slots_new], new)
    best, _ = folded(scores, new_cids, True)
    if columns is not None:
        row = iota((slots_new, LANES), 0)
        lane = iota((slots_new, LANES), 1)
        for g, col in enumerate(columns):
            best = jnp.maximum(best, jnp.where(row == lane + g * LANES, col, -1.0))
    results.append(best)
    return results


def member_sums(cid_row, new):
    hot = to_bf16(cid_row == iota((8, cid_row.shape[1]), 0).astype(f32))
    return mm(hot, new)


def score_kernel(slots, partners, olds, bound_ref, *refs):
    fresh = len(partners)
    raw_refs, refs = refs[:fresh], refs[fresh:]
    old_refs = [refs[3 * i : 3 * i + 3] for i in range(olds)]
    refs = refs[3 * olds :]
    if olds:
        sums_ref, refs = refs[0], refs[1:]
    unit_ref, acc_ref, cid_ref, sums_out = refs[:4]
    old_accs = refs[4 : 4 + olds]
    new_ref = refs[4 + olds]
    rows = fresh * slots
    for i, r in enumerate(partners):
        at = slice(i * slots, (i + 1) * slots)
        new_ref[at, :] = unit_rows(raw_refs[i])
        cid_ref[at, :] = cluster_rows(bound_ref, r, slots)
    padded = new_ref.shape[0]
    if padded > rows:
        new_ref[rows:, :] = jnp.zeros((padded - rows, new_ref.shape[1]), bf16)
    unit_ref[...] = new_ref[...]
    cid_row = cluster_lanes(bound_ref, partners, slots, padded)
    results = score_group(new_ref, cid_ref[...], old_refs, cid_row, rows)
    for best, ref in zip(results, list(old_accs) + [acc_ref]):
        ref[...] = best
    sums = member_sums(cid_row, new_ref[...])
    sums_out[...] = sums + sums_ref[...] if olds else sums


def score(bound, blocks, partners, state):
    slots, width = blocks[0].shape
    units, accs, cids, sums = state
    rows = len(blocks) * slots
    padded = round_up(rows, LANES)
    old = [x for group in zip(units, accs, cids) for x in group]
    old_rows = sum(a.shape[0] for a in accs)
    acc_shapes = [jax.ShapeDtypeStruct(a.shape, f32) for a in accs]
    out_shape = (
        jax.ShapeDtypeStruct((padded, width), bf16),
        jax.ShapeDtypeStruct((rows, LANES), f32),
        jax.ShapeDtypeStruct((rows, LANES), f32),
        jax.ShapeDtypeStruct((8, width), f32),
        *acc_shapes,
    )
    args = [bound, *blocks, *old] + ([sums] if units else [])
    out = pl.pallas_call(
        functools.partial(score_kernel, slots, partners, len(units)),
        out_shape=out_shape,
        in_specs=[VMEM] * len(args),
        out_specs=(VMEM,) * len(out_shape),
        scratch_shapes=[pltpu.VMEM((padded, width), bf16)],
        compiler_params=pltpu.CompilerParams(vmem_limit_bytes=(36 if slots < 400 else 58) * MIB),
        cost_estimate=pl.CostEstimate(
            flops=2 * (old_rows + rows) * padded,
            bytes_accessed=2 * (old_rows + rows),
            transcendentals=rows,
        ),
        name="score_rows",
    )(*args)
    return units + [out[0]], list(out[4:]) + [out[1]], cids + [out[2]], out[3]


def diagonal():
    return iota((LANES, LANES), 0) == iota((LANES, LANES), 1)


def to_line(col, first):
    piece = col[first : first + LANES]
    return jnp.sum(jnp.where(diagonal()[: piece.shape[0]], piece, 0.0), axis=0, keepdims=True)


def line_kernel(slots, names, bound_ref, *refs):
    count = len(names)
    for i, partners in enumerate(names):
        acc_ref, best_ref, cid_ref = refs[i], refs[count + 2 * i], refs[count + 2 * i + 1]
        best = jnp.max(acc_ref[...], axis=1, keepdims=True)
        for first in range(0, best_ref.shape[1], LANES):
            best_ref[:, first : first + LANES] = to_line(best, first)
        cid_ref[...] = cluster_lanes(bound_ref, partners, slots, cid_ref.shape[1])


def lines(bound, names, slots, accs):
    widths = [round_up(acc.shape[0], LANES) for acc in accs]
    out = pl.pallas_call(
        functools.partial(line_kernel, slots, names),
        out_shape=tuple(jax.ShapeDtypeStruct((1, w), f32) for w in widths for _ in range(2)),
        in_specs=[VMEM] * (1 + len(accs)),
        out_specs=(VMEM,) * (2 * len(accs)),
        compiler_params=pltpu.CompilerParams(vmem_limit_bytes=16 * MIB),
        name="line_rows",
    )(bound, *accs)
    return out[0::2], out[1::2]


def finish_kernel(slots, partners, earlier, me_ref, bound_ref, total_ref, *refs):
    fresh = len(partners)
    olds = len(earlier)
    raw_refs, refs = refs[:fresh], refs[fresh:]
    old_refs = [refs[3 * i : 3 * i + 3] for i in range(olds)]
    sums_ref, out_ref, new_ref = refs[3 * olds :]
    chip = me_ref[0] >> 1
    rows = fresh * slots
    padded, width = new_ref.shape
    half = out_ref.shape[2] // 2
    new_ref[rows:, :] = jnp.zeros((padded - rows, width), bf16)
    pieces = []
    for i, r in enumerate(partners):
        new_ref[i * slots : (i + 1) * slots, :] = unit_rows(raw_refs[i])
        pieces.append(cluster_rows(bound_ref, r, slots))
    new_cids = jnp.concatenate(pieces, axis=0)
    cid_row = cluster_lanes(bound_ref, partners, slots, padded)
    sums = sums_ref[...] + member_sums(cid_row, new_ref[...])
    centroid = (sums / jnp.maximum(total_ref[:, 0:1], 1.0)).astype(bf16)
    centroid = jnp.concatenate([centroid, jnp.zeros_like(centroid)], axis=0)
    new_ref[rows : rows + STEP, :] = centroid
    left = new_ref[0 : rows + STEP, :]
    label = iota((8, LANES), 0).astype(f32)
    row = iota((rows, LANES), 0)
    lane = iota((rows, LANES), 1)

    def write(names, best_line, gap_line):
        for i, r in enumerate(names):
            at = slice(i * slots, (i + 1) * slots)
            for j, line in enumerate((best_line, gap_line)):
                piece = line[:, at]
                for core in range(2):
                    out_ref[2 * (r ^ chip) + core, :, j * half : j * half + slots] = piece

    best_new = jnp.full((rows, LANES), -1.0, f32)
    for names, (unit_ref, best_ref, cid_ref) in zip(earlier, old_refs):
        scores = nt_dot(left, unit_ref[...])
        bests, gaps = [], []
        for first in range(0, unit_ref.shape[0], LANES):
            at = slice(first, first + LANES)
            cids = cid_ref[:, at]
            part = jnp.where(new_cids == cids, scores[0:rows, at], -1.0)
            best_new = jnp.maximum(best_new, part)
            bests.append(jnp.maximum(best_ref[:, at], jnp.max(part, axis=0, keepdims=True)))
            dots = jnp.where(label == cids, scores[rows : rows + 8, at], 0.0)
            gaps.append(1.0 - jnp.sum(dots, axis=0, keepdims=True))
        write(names, jnp.concatenate(bests, axis=1), jnp.concatenate(gaps, axis=1))
    scores = nt_dot(left, new_ref[...])
    gaps = []
    for first in range(0, padded, LANES):
        at = slice(first, first + LANES)
        cids = cid_row[:, at]
        allowed = (new_cids == cids) & (row != lane + first)
        best_new = jnp.maximum(best_new, jnp.where(allowed, scores[0:rows, at], -1.0))
        dots = jnp.where(label == cids, scores[rows : rows + 8, at], 0.0)
        gaps.append(1.0 - jnp.sum(dots, axis=0, keepdims=True))
    best = jnp.max(best_new, axis=1, keepdims=True)
    bests = [to_line(best, first) for first in range(0, rows, LANES)]
    write(partners, jnp.concatenate(bests, axis=1), jnp.concatenate(gaps, axis=1))


def finish(me, bound, total, blocks, partners, earlier, state):
    slots, width = blocks[0].shape
    owners = 2 * bound.shape[0]
    units, accs, _, sums = state
    rows = len(blocks) * slots
    padded = round_up(rows + STEP, LANES)
    best_lines, cid_lines = lines(bound, earlier, slots, accs)
    old = [x for group in zip(units, best_lines, cid_lines) for x in group]
    args = [me, bound, total, *blocks, *old, sums]
    return pl.pallas_call(
        functools.partial(finish_kernel, slots, partners, earlier),
        out_shape=jax.ShapeDtypeStruct((owners, 1, 2 * round_up(slots, LANES)), f32),
        in_specs=[SMEM] + [VMEM] * (len(args) - 1),
        out_specs=VMEM,
        scratch_shapes=[pltpu.VMEM((padded, width), bf16)],
        compiler_params=pltpu.CompilerParams(vmem_limit_bytes=(36 if slots < 400 else 58) * MIB),
        cost_estimate=pl.CostEstimate(
            flops=2 * owners * slots * padded * width,
            bytes_accessed=2 * owners * slots * width,
            transcendentals=rows,
        ),
        name="finish_rows",
    )(*args)


def restore_kernel(slots, owner_ref, slot_ref, back_ref, best_ref, gap_ref):
    rows = owner_ref.shape[1]
    owners, _, width = back_ref.shape
    half = width // 2
    from_owner = to_bf16(owner_ref[...] == iota((owners, rows), 0))
    from_owner = jnp.concatenate([from_owner] * 3, axis=0)
    at_slot = slot_ref[...] == iota((slots, rows), 0)
    back = jnp.concatenate([back_ref[s] for s in range(owners)], axis=0)
    part0 = back.astype(bf16)
    rest = back - part0.astype(f32)
    part1 = rest.astype(bf16)
    part2 = (rest - part1.astype(f32)).astype(bf16)
    parts = jnp.concatenate([part0, part1, part2], axis=0)
    for i, ref in enumerate((best_ref, gap_ref)):
        table = lax.dot_general(
            parts[:, i * half : i * half + slots],
            from_owner,
            (((0,), (0,)), ((), ())),
            preferred_element_type=f32,
        )
        ref[...] = jnp.sum(jnp.where(at_slot, table, 0.0), axis=0, keepdims=True)


def restore(owner_row, slot_row, back, slots):
    return pl.pallas_call(
        functools.partial(restore_kernel, slots),
        out_shape=(jax.ShapeDtypeStruct(owner_row.shape, f32),) * 2,
        in_specs=[VMEM] * 3,
        out_specs=(VMEM, VMEM),
        compiler_params=pltpu.CompilerParams(vmem_limit_bytes=28 * MIB),
        name="restore_rows",
    )(owner_row, slot_row, back)


def exchange(x):
    return lax.all_to_all(x, "owner", split_axis=0, concat_axis=0, tiled=True)


def exchange_chips(x):
    chips = lax.axis_size("owner") // 2
    cores = [[2 * chip + core for chip in range(chips)] for core in range(2)]
    return lax.all_to_all(
        x, "owner", split_axis=0, concat_axis=0, axis_index_groups=cores, tiled=True
    )


def swap(block, r):
    owners = lax.axis_size("owner")
    return lax.ppermute(block, "owner", [(s, s ^ (2 * r)) for s in range(owners)])


def swap_together(blocks):
    chips = len(blocks)
    order = jnp.arange(chips, dtype=i32) ^ (lax.axis_index("owner").astype(i32) >> 1)
    arrived = exchange_chips(jnp.stack(blocks)[order])[order]
    return [arrived[r] for r in range(chips)]


def swap_cores(x):
    owners = lax.axis_size("owner")
    return lax.ppermute(x, "owner", [(s, s ^ 1) for s in range(owners)])


def local(embeddings, cluster_ids):
    rows = embeddings.shape[0]
    owners = lax.axis_size("owner")
    chips = owners // 2
    clusters = CL_DEV * owners
    row_limit = 2 * rows // clusters
    most = round_up(2 * CL_DEV * row_limit, STEP)
    usual = min(most, round_up(17 * rows // (8 * owners), STEP))
    few = chips <= MAX_PERMUTES
    me = lax.axis_index("owner").astype(i32).reshape(1)
    ids0 = cluster_ids.reshape(1, rows)
    ids1 = swap_cores(ids0)
    own, own_total = rank_own(ids0, clusters)
    mine, ids1, own = lax.optimization_barrier((embeddings, ids1, own))
    other = swap_cores(mine)
    counts, rank0, rank1 = count_rows(me, ids1, own, own_total, chips, clusters)
    counts = exchange_chips(counts)
    both = (embeddings, other)
    *places, bound, total, load = assign(me, counts, rank0, rank1)
    owner_row, slot_row = places[0], places[2]

    half = chips // 2
    far = list(range(chips - 1, half - 1, -1))
    far = far[: half // 2 : 2] + far[half // 2 :: 2] + far[1 : half // 2 : 2] + far[half // 2 + 1 :: 2]
    near = list(range(half - 1, 0, -1))
    sent = far[:2] + near + far[2:] + [0]
    share = max(half // 4, 1)
    groups = [[0] + near, far[: 2 * share], far[2 * share : 3 * share], far[3 * share :]]

    def compare(slots, apart):
        blocks = [None] * chips
        here = list(places)
        for r in sent:
            blocks[r] = pack(me, here, both, r, slots)
            here[0], blocks[r] = lax.optimization_barrier((here[0], blocks[r]))
        if apart:
            arrived = blocks[:1] + [None] * (chips - 1)
            for r in sent[:-1]:
                if r in far[2:]:
                    before = far[far.index(r) - 2]
                    blocks[r], arrived[before] = lax.optimization_barrier(
                        (blocks[r], arrived[before])
                    )
                arrived[r] = swap(blocks[r], r)
        else:
            arrived = swap_together(blocks)
        state = ([], [], [], None)
        for group in groups[:-1]:
            state = score(bound, [arrived[r] for r in group], group, state)
        last = groups[-1]
        answers = finish(
            me, bound, total, [arrived[r] for r in last], last, groups[:-1], state
        )
        return restore(owner_row, slot_row, exchange(answers), slots)

    best, gap = compare(usual, few)
    if usual < most:
        best, gap = lax.cond(
            load[0, 0] <= usual, lambda: (best, gap), lambda: compare(most, False)
        )
    return best.reshape(rows), gap.reshape(rows)


def solution(mesh):
    return jax.shard_map(
        local,
        mesh=mesh,
        in_specs=(P(("groups", "owner"), None), P(("groups", "owner"))),
        out_specs=(P(("groups", "owner")), P(("groups", "owner"))),
        check_vma=False,
    )
```

```python
import functools

import jax
import jax.numpy as jnp
from jax import lax
from jax.experimental import pallas as pl
from jax.experimental.pallas import tpu as pltpu
from jax.sharding import PartitionSpec as P

CL_DEV = 4
VARIANTS = 32
STEP = 16
TILE = 256
LANES = 128
MAX_PERMUTES = 8
RANKS = 4096
MIB = 1 << 20

epsilon = 1e-06
f32 = jnp.float32
bf16 = jnp.bfloat16
i32 = jnp.int32
VMEM = pl.BlockSpec(memory_space=pltpu.VMEM)
SMEM = pl.BlockSpec(memory_space=pltpu.SMEM)


def iota(shape, axis):
    return lax.broadcasted_iota(i32, shape, axis)


def round_up(value, unit):
    return -(-value // unit) * unit


def nt_dot(a, b):
    return lax.dot_general(a, b, (((1,), (1,)), ((), ())), preferred_element_type=f32)


def mm(a, b):
    return jnp.dot(a, b, preferred_element_type=f32)


def to_bf16(mask):
    return mask.astype(f32).astype(bf16)


def rank_rows(ids_ref, rank_ref, clusters):
    label = iota((clusters, TILE), 0)
    upto = to_bf16(iota((TILE, TILE), 0) <= iota((TILE, TILE), 1))
    total = jnp.zeros((clusters, 1), f32)
    for first in range(0, ids_ref.shape[1], TILE):
        at = slice(first, first + TILE)
        hot = ids_ref[:, at] == label
        prefix = mm(to_bf16(hot), upto)
        rank = jnp.sum(jnp.where(hot, prefix + total - 1.0, 0.0), axis=0, keepdims=True)
        rank_ref[:, at] = ids_ref[:, at] * RANKS + rank.astype(i32)
        total = total + prefix[:, TILE - 1 :]
    return total


def own_kernel(ids_ref, rank_ref, total_ref):
    total = rank_rows(ids_ref, rank_ref, total_ref.shape[0])
    total_ref[...] = jnp.broadcast_to(total, total_ref.shape)


def rank_own(ids, clusters):
    return pl.pallas_call(
        own_kernel,
        out_shape=(
            jax.ShapeDtypeStruct(ids.shape, i32),
            jax.ShapeDtypeStruct((clusters, LANES), f32),
        ),
        in_specs=[VMEM],
        out_specs=(VMEM, VMEM),
        compiler_params=pltpu.CompilerParams(vmem_limit_bytes=16 * MIB),
        cost_estimate=pl.CostEstimate(flops=1_000_000_000, bytes_accessed=1 << 20, transcendentals=0),
        name="rank_own",
    )(ids)


def count_kernel(
    me_ref, ids1_ref, own_ref, total_ref, counts_ref, rank0_ref, rank1_ref
):
    rows = ids1_ref.shape[1]
    clusters = counts_ref.shape[2]
    core = me_ref[0] & 1
    label = iota((clusters, TILE), 0)
    total0 = total_ref[:, 0:1]
    total1 = rank_rows(ids1_ref, rank1_ref, clusters)
    square = (clusters, clusters)
    eye = iota(square, 0) == iota(square, 1)
    total_row = jnp.sum(jnp.where(eye, total0 + total1, 0.0), axis=0, keepdims=True).astype(i32)
    counts_ref[0] = total_row
    for from_ref, rank_ref, ahead in (
        (own_ref, rank0_ref, jnp.where(core == 1, total1, 0.0)),
        (rank1_ref, rank1_ref, jnp.where(core == 0, total0, 0.0)),
    ):
        for first in range(0, rows, TILE):
            at = slice(first, first + TILE)
            rank = from_ref[:, at]
            more = jnp.where((rank // RANKS) == label, ahead, 0.0)
            rank_ref[:, at] = rank + jnp.sum(more, axis=0, keepdims=True).astype(i32)


def count_rows(me, ids1, own, total, clusters):
    return pl.pallas_call(
        count_kernel,
        out_shape=(
            jax.ShapeDtypeStruct((1, 1, clusters), i32),
            jax.ShapeDtypeStruct(ids1.shape, i32),
            jax.ShapeDtypeStruct(ids1.shape, i32),
        ),
        in_specs=[SMEM, VMEM, VMEM, VMEM],
        out_specs=(VMEM,) * 3,
        compiler_params=pltpu.CompilerParams(vmem_limit_bytes=16 * MIB),
        cost_estimate=pl.CostEstimate(flops=8_000_000_000, bytes_accessed=1 << 20, transcendentals=0),
        name="count_rows",
    )(me, ids1, own, total)


def assign_kernel(
    me_ref,
    counts_ref,
    rank0_ref,
    rank1_ref,
    owner0_ref,
    owner1_ref,
    slot0_ref,
    slot1_ref,
    bound_ref,
    total_ref,
    load_ref,
):
    chips, _, clusters = counts_ref.shape
    owners = 2 * chips
    rows = rank0_ref.shape[1]
    shift = owners.bit_length() - 1
    me = me_ref[0]
    chip = me >> 1
    count = jnp.concatenate([counts_ref[s].astype(f32) for s in range(chips)], axis=0)
    count16 = count.astype(bf16)
    square = (clusters, clusters)
    sub, lane = iota(square, 0), iota(square, 1)
    total_row = jnp.sum(count, axis=0, keepdims=True)
    total_col = jnp.sum(jnp.where(sub == lane, total_row, 0.0), axis=1, keepdims=True)
    tie = total_row == total_col
    outranks_col = (total_row > total_col) | (tie & (lane < sub))
    outranks_row = (total_col > total_row) | (tie & (sub < lane))
    rank_col = jnp.sum(outranks_col.astype(f32), axis=1, keepdims=True).astype(i32)
    rank_row = jnp.sum(outranks_row.astype(f32), axis=0, keepdims=True).astype(i32)

    layer_col, layer_row = rank_col >> shift, rank_row >> shift

    def plain(rank, layer):
        return (rank & (owners - 1)) ^ jnp.where((layer & 1) == 1, owners - 1, 0)

    def flip(p, variant):
        bits = (variant >> (p - 1)) & 1
        if p < CL_DEV - 1:
            bits = bits + 2 * ((variant >> (p + CL_DEV - 2)) & 1)
        return bits

    lanes = iota((1, VARIANTS * owners), 1)
    target = lanes & (owners - 1)
    for p in range(1, CL_DEV):
        swapped = (lanes & (owners - 1)) ^ flip(p, lanes >> shift)
        target = jnp.where(layer_col == p, swapped, target)
    tried = plain(rank_col, layer_col) == target
    load = jnp.max(mm(count16, to_bf16(tried)), axis=0, keepdims=True)
    by_variant = (VARIANTS, VARIANTS * owners)
    worst = jnp.max(
        jnp.where((iota(by_variant, 1) >> shift) == iota(by_variant, 0), load, 0.0),
        axis=1,
        keepdims=True,
    )
    best = jnp.min(worst, axis=0, keepdims=True)
    chosen = jnp.min(
        jnp.where(worst == best, iota((VARIANTS, 1), 0), VARIANTS), axis=0, keepdims=True
    )

    def owner_of(rank, layer):
        swaps = jnp.zeros_like(rank)
        for p in range(1, CL_DEV):
            swaps = jnp.where(layer == p, flip(p, chosen), swaps)
        return plain(rank, layer) ^ swaps

    owner_col = owner_of(rank_col, layer_col)
    owner_row = owner_of(rank_row, layer_row)
    load_ref[...] = jnp.broadcast_to(best, load_ref.shape).astype(i32)

    mine = jnp.sum(jnp.where(iota(count.shape, 0) == chip, count, 0.0), axis=0, keepdims=True)
    earlier = (owner_row == owner_col) & (layer_row < layer_col)
    offset_col = jnp.sum(jnp.where(earlier, mine, 0.0), axis=1, keepdims=True)
    for rank_ref, owner_ref, slot_ref in (
        (rank0_ref, owner0_ref, slot0_ref),
        (rank1_ref, owner1_ref, slot1_ref),
    ):
        hot = (rank_ref[...] // RANKS) == iota((clusters, rows), 0)
        owner_ref[...] = jnp.sum(
            jnp.where(hot, owner_col.astype(f32), 0.0), axis=0, keepdims=True
        ).astype(i32)
        slot_ref[...] = jnp.sum(jnp.where(hot, offset_col, 0.0), axis=0, keepdims=True).astype(
            i32
        ) + (rank_ref[...] & (RANKS - 1))

    select = (owner_col == me) & (layer_col <= iota((clusters, LANES), 1))
    turn = iota((chips, chips), 1) == (iota((chips, chips), 0) ^ chip)
    turned = mm(to_bf16(turn), count16).astype(bf16)
    bound_ref[...] = mm(turned, to_bf16(select))
    own = (owner_row == me) & (layer_row == iota((8, clusters), 0))
    total_ref[...] = jnp.broadcast_to(
        jnp.sum(jnp.where(own, total_row, 0.0), axis=1, keepdims=True), total_ref.shape
    )


def assign(me, counts, rank0, rank1):
    chips, _, clusters = counts.shape
    line = jax.ShapeDtypeStruct(rank0.shape, i32)
    return pl.pallas_call(
        assign_kernel,
        out_shape=(
            line,
            line,
            line,
            line,
            jax.ShapeDtypeStruct((chips, LANES), f32),
            jax.ShapeDtypeStruct((8, LANES), f32),
            jax.ShapeDtypeStruct((1, LANES), i32),
        ),
        in_specs=[SMEM, VMEM, VMEM, VMEM],
        out_specs=(VMEM,) * 7,
        compiler_params=pltpu.CompilerParams(vmem_limit_bytes=16 * MIB),
        name="assign",
    )(me, counts, rank0, rank1)


def pack_kernel(
    partner, me_ref, owner0_ref, owner1_ref, slot0_ref, slot1_ref, rows0_ref, rows1_ref, out_ref
):
    slots = out_ref.shape[0]
    rows = rows0_ref.shape[0]
    target = me_ref[0] ^ (2 * partner)
    slot = iota((slots, rows), 0)
    total = None
    for owner_ref, slot_ref, rows_ref in (
        (owner0_ref, slot0_ref, rows0_ref),
        (owner1_ref, slot1_ref, rows1_ref),
    ):
        key = jnp.where(owner_ref[...] == target, slot_ref[...], -1)
        part = mm(to_bf16(slot == key), rows_ref[...])
        total = part if total is None else total + part
    out_ref[...] = total.astype(bf16)


def pack(me, places, both, partner, slots):
    width = both[0].shape[1]
    return pl.pallas_call(
        functools.partial(pack_kernel, partner),
        out_shape=jax.ShapeDtypeStruct((slots, width), bf16),
        in_specs=[SMEM] + [VMEM] * 6,
        out_specs=VMEM,
        compiler_params=pltpu.CompilerParams(vmem_limit_bytes=24 * MIB),
        cost_estimate=pl.CostEstimate(flops=slots, bytes_accessed=slots, transcendentals=0),
        name="pack_rows",
    )(me, *places, *both)


def unit_rows(ref):
    x = ref[...].astype(f32)
    scale = lax.rsqrt(jnp.sum(x * x, axis=1, keepdims=True) + epsilon)
    return (x * scale).astype(bf16)


def cluster_lanes(bound_ref, partners, slots, width):
    lane = iota((1, width), 1).astype(f32)
    result = jnp.where(lane < len(partners) * slots, 0.0, -1.0)
    for i, r in enumerate(partners):
        for k in range(CL_DEV):
            first = bound_ref[r : r + 1, k : k + 1] + float(i * slots)
            result = result + ((lane >= first) & (lane < float((i + 1) * slots))).astype(f32)
    return result


def cluster_rows(bound_ref, r, slots):
    slot = iota((slots, LANES), 0).astype(f32)
    result = jnp.zeros((slots, LANES), f32)
    for k in range(CL_DEV):
        result = result + (slot >= bound_ref[r : r + 1, k : k + 1]).astype(f32)
    return result


def score_group(new_ref, new_cids, olds, cid_row, slots_new):
    padded = new_ref.shape[0]
    groups = padded // LANES
    new = new_ref[...]

    def folded(scores, cids, skip_same):
        rows = scores.shape[0]
        row = iota((rows, LANES), 0)
        lane = iota((rows, LANES), 1)
        best, cols = None, []
        for g in range(groups):
            at = slice(g * LANES, (g + 1) * LANES)
            allowed = cids == cid_row[:, at]
            if skip_same:
                allowed = allowed & (row != lane + g * LANES)
            part = jnp.where(allowed, scores[:, at], -1.0)
            best = part if best is None else jnp.maximum(best, part)
            cols.append(jnp.max(part, axis=0, keepdims=True))
        return best, cols

    columns = None
    results = []
    for unit_ref, acc_ref, cid_ref in olds:
        scores = nt_dot(unit_ref[0 : acc_ref.shape[0], :], new)
        best, cols = folded(scores, cid_ref[...], False)
        columns = cols if columns is None else [jnp.maximum(a, b) for a, b in zip(columns, cols)]
        results.append(jnp.maximum(acc_ref[...], best))
    scores = nt_dot(new[0:slots_new], new)
    best, _ = folded(scores, new_cids, True)
    if columns is not None:
        row = iota((slots_new, LANES), 0)
        lane = iota((slots_new, LANES), 1)
        for g, col in enumerate(columns):
            best = jnp.maximum(best, jnp.where(row == lane + g * LANES, col, -1.0))
    results.append(best)
    return results


def member_sums(cid_row, new):
    hot = to_bf16(cid_row == iota((8, cid_row.shape[1]), 0).astype(f32))
    return mm(hot, new)


def score_kernel(slots, partners, olds, bound_ref, *refs):
    fresh = len(partners)
    raw_refs, refs = refs[:fresh], refs[fresh:]
    old_refs = [refs[3 * i : 3 * i + 3] for i in range(olds)]
    refs = refs[3 * olds :]
    if olds:
        sums_ref, refs = refs[0], refs[1:]
    unit_ref, acc_ref, cid_ref, sums_out = refs[:4]
    old_accs = refs[4 : 4 + olds]
    new_ref = refs[4 + olds]
    rows = fresh * slots
    for i, r in enumerate(partners):
        at = slice(i * slots, (i + 1) * slots)
        new_ref[at, :] = unit_rows(raw_refs[i])
        cid_ref[at, :] = cluster_rows(bound_ref, r, slots)
    padded = new_ref.shape[0]
    if padded > rows:
        new_ref[rows:, :] = jnp.zeros((padded - rows, new_ref.shape[1]), bf16)
    unit_ref[...] = new_ref[...]
    cid_row = cluster_lanes(bound_ref, partners, slots, padded)
    results = score_group(new_ref, cid_ref[...], old_refs, cid_row, rows)
    for best, ref in zip(results, list(old_accs) + [acc_ref]):
        ref[...] = best
    sums = member_sums(cid_row, new_ref[...])
    sums_out[...] = sums + sums_ref[...] if olds else sums


def score(bound, blocks, partners, state):
    slots, width = blocks[0].shape
    units, accs, cids, sums = state
    rows = len(blocks) * slots
    padded = round_up(rows, LANES)
    old = [x for group in zip(units, accs, cids) for x in group]
    old_rows = sum(a.shape[0] for a in accs)
    acc_shapes = [jax.ShapeDtypeStruct(a.shape, f32) for a in accs]
    out_shape = (
        jax.ShapeDtypeStruct((padded, width), bf16),
        jax.ShapeDtypeStruct((rows, LANES), f32),
        jax.ShapeDtypeStruct((rows, LANES), f32),
        jax.ShapeDtypeStruct((8, width), f32),
        *acc_shapes,
    )
    args = [bound, *blocks, *old] + ([sums] if units else [])
    out = pl.pallas_call(
        functools.partial(score_kernel, slots, partners, len(units)),
        out_shape=out_shape,
        in_specs=[VMEM] * len(args),
        out_specs=(VMEM,) * len(out_shape),
        scratch_shapes=[pltpu.VMEM((padded, width), bf16)],
        compiler_params=pltpu.CompilerParams(vmem_limit_bytes=(36 if slots < 400 else 58) * MIB),
        cost_estimate=pl.CostEstimate(
            flops=2 * (old_rows + rows) * padded,
            bytes_accessed=2 * (old_rows + rows),
            transcendentals=rows,
        ),
        name="score_rows",
    )(*args)
    return units + [out[0]], list(out[4:]) + [out[1]], cids + [out[2]], out[3]


def diagonal():
    return iota((LANES, LANES), 0) == iota((LANES, LANES), 1)


def to_line(col, first):
    piece = col[first : first + LANES]
    return jnp.sum(jnp.where(diagonal()[: piece.shape[0]], piece, 0.0), axis=0, keepdims=True)


def line_kernel(slots, names, bound_ref, *refs):
    count = len(names)
    for i, partners in enumerate(names):
        acc_ref, best_ref, cid_ref = refs[i], refs[count + 2 * i], refs[count + 2 * i + 1]
        best = jnp.max(acc_ref[...], axis=1, keepdims=True)
        for first in range(0, best_ref.shape[1], LANES):
            best_ref[:, first : first + LANES] = to_line(best, first)
        cid_ref[...] = cluster_lanes(bound_ref, partners, slots, cid_ref.shape[1])


def lines(bound, names, slots, accs):
    widths = [round_up(acc.shape[0], LANES) for acc in accs]
    out = pl.pallas_call(
        functools.partial(line_kernel, slots, names),
        out_shape=tuple(jax.ShapeDtypeStruct((1, w), f32) for w in widths for _ in range(2)),
        in_specs=[VMEM] * (1 + len(accs)),
        out_specs=(VMEM,) * (2 * len(accs)),
        compiler_params=pltpu.CompilerParams(vmem_limit_bytes=16 * MIB),
        name="line_rows",
    )(bound, *accs)
    return out[0::2], out[1::2]


def finish_kernel(slots, partners, earlier, me_ref, bound_ref, total_ref, *refs):
    fresh = len(partners)
    olds = len(earlier)
    raw_refs, refs = refs[:fresh], refs[fresh:]
    old_refs = [refs[3 * i : 3 * i + 3] for i in range(olds)]
    sums_ref, out_ref, new_ref = refs[3 * olds :]
    chip = me_ref[0] >> 1
    rows = fresh * slots
    padded, width = new_ref.shape
    half = out_ref.shape[2] // 2
    new_ref[rows:, :] = jnp.zeros((padded - rows, width), bf16)
    pieces = []
    for i, r in enumerate(partners):
        new_ref[i * slots : (i + 1) * slots, :] = unit_rows(raw_refs[i])
        pieces.append(cluster_rows(bound_ref, r, slots))
    new_cids = jnp.concatenate(pieces, axis=0)
    cid_row = cluster_lanes(bound_ref, partners, slots, padded)
    sums = sums_ref[...] + member_sums(cid_row, new_ref[...])
    centroid = (sums / jnp.maximum(total_ref[:, 0:1], 1.0)).astype(bf16)
    centroid = jnp.concatenate([centroid, jnp.zeros_like(centroid)], axis=0)
    new_ref[rows : rows + STEP, :] = centroid
    left = new_ref[0 : rows + STEP, :]
    label = iota((8, LANES), 0).astype(f32)
    row = iota((rows, LANES), 0)
    lane = iota((rows, LANES), 1)

    def write(names, best_line, gap_line):
        for i, r in enumerate(names):
            at = slice(i * slots, (i + 1) * slots)
            for j, line in enumerate((best_line, gap_line)):
                piece = line[:, at]
                for core in range(2):
                    out_ref[2 * (r ^ chip) + core, :, j * half : j * half + slots] = piece

    best_new = jnp.full((rows, LANES), -1.0, f32)
    for names, (unit_ref, best_ref, cid_ref) in zip(earlier, old_refs):
        scores = nt_dot(left, unit_ref[...])
        bests, gaps = [], []
        for first in range(0, unit_ref.shape[0], LANES):
            at = slice(first, first + LANES)
            cids = cid_ref[:, at]
            part = jnp.where(new_cids == cids, scores[0:rows, at], -1.0)
            best_new = jnp.maximum(best_new, part)
            bests.append(jnp.maximum(best_ref[:, at], jnp.max(part, axis=0, keepdims=True)))
            dots = jnp.where(label == cids, scores[rows : rows + 8, at], 0.0)
            gaps.append(1.0 - jnp.sum(dots, axis=0, keepdims=True))
        write(names, jnp.concatenate(bests, axis=1), jnp.concatenate(gaps, axis=1))
    scores = nt_dot(left, new_ref[...])
    gaps = []
    for first in range(0, padded, LANES):
        at = slice(first, first + LANES)
        cids = cid_row[:, at]
        allowed = (new_cids == cids) & (row != lane + first)
        best_new = jnp.maximum(best_new, jnp.where(allowed, scores[0:rows, at], -1.0))
        dots = jnp.where(label == cids, scores[rows : rows + 8, at], 0.0)
        gaps.append(1.0 - jnp.sum(dots, axis=0, keepdims=True))
    best = jnp.max(best_new, axis=1, keepdims=True)
    bests = [to_line(best, first) for first in range(0, rows, LANES)]
    write(partners, jnp.concatenate(bests, axis=1), jnp.concatenate(gaps, axis=1))


def finish(me, bound, total, blocks, partners, earlier, state):
    slots, width = blocks[0].shape
    owners = 2 * bound.shape[0]
    units, accs, _, sums = state
    rows = len(blocks) * slots
    padded = round_up(rows + STEP, LANES)
    best_lines, cid_lines = lines(bound, earlier, slots, accs)
    old = [x for group in zip(units, best_lines, cid_lines) for x in group]
    args = [me, bound, total, *blocks, *old, sums]
    return pl.pallas_call(
        functools.partial(finish_kernel, slots, partners, earlier),
        out_shape=jax.ShapeDtypeStruct((owners, 1, 2 * round_up(slots, LANES)), f32),
        in_specs=[SMEM] + [VMEM] * (len(args) - 1),
        out_specs=VMEM,
        scratch_shapes=[pltpu.VMEM((padded, width), bf16)],
        compiler_params=pltpu.CompilerParams(vmem_limit_bytes=(36 if slots < 400 else 58) * MIB),
        cost_estimate=pl.CostEstimate(
            flops=2 * owners * slots * padded * width,
            bytes_accessed=2 * owners * slots * width,
            transcendentals=rows,
        ),
        name="finish_rows",
    )(*args)


def restore_kernel(slots, owner_ref, slot_ref, back_ref, best_ref, gap_ref):
    rows = owner_ref.shape[1]
    owners, _, width = back_ref.shape
    half = width // 2
    from_owner = to_bf16(owner_ref[...] == iota((owners, rows), 0))
    from_owner = jnp.concatenate([from_owner] * 3, axis=0)
    at_slot = slot_ref[...] == iota((slots, rows), 0)
    back = jnp.concatenate([back_ref[s] for s in range(owners)], axis=0)
    part0 = back.astype(bf16)
    rest = back - part0.astype(f32)
    part1 = rest.astype(bf16)
    part2 = (rest - part1.astype(f32)).astype(bf16)
    parts = jnp.concatenate([part0, part1, part2], axis=0)
    for i, ref in enumerate((best_ref, gap_ref)):
        table = lax.dot_general(
            parts[:, i * half : i * half + slots],
            from_owner,
            (((0,), (0,)), ((), ())),
            preferred_element_type=f32,
        )
        ref[...] = jnp.sum(jnp.where(at_slot, table, 0.0), axis=0, keepdims=True)


def restore(owner_row, slot_row, back, slots):
    return pl.pallas_call(
        functools.partial(restore_kernel, slots),
        out_shape=(jax.ShapeDtypeStruct(owner_row.shape, f32),) * 2,
        in_specs=[VMEM] * 3,
        out_specs=(VMEM, VMEM),
        compiler_params=pltpu.CompilerParams(vmem_limit_bytes=28 * MIB),
        name="restore_rows",
    )(owner_row, slot_row, back)


def exchange(x):
    return lax.all_to_all(x, "owner", split_axis=0, concat_axis=0, tiled=True)


def exchange_chips(x):
    chips = lax.axis_size("owner") // 2
    cores = [[2 * chip + core for chip in range(chips)] for core in range(2)]
    return lax.all_to_all(
        x, "owner", split_axis=0, concat_axis=0, axis_index_groups=cores, tiled=True
    )


def gather_chips(x):
    chips = lax.axis_size("owner") // 2
    cores = [[2 * chip + core for chip in range(chips)] for core in range(2)]
    return lax.all_gather(x, "owner", axis_index_groups=cores, tiled=True)


def swap(block, r):
    owners = lax.axis_size("owner")
    return lax.ppermute(block, "owner", [(s, s ^ (2 * r)) for s in range(owners)])


def swap_together(blocks):
    chips = len(blocks)
    order = jnp.arange(chips, dtype=i32) ^ (lax.axis_index("owner").astype(i32) >> 1)
    arrived = exchange_chips(jnp.stack(blocks)[order])[order]
    return [arrived[r] for r in range(chips)]


def swap_cores(x):
    owners = lax.axis_size("owner")
    return lax.ppermute(x, "owner", [(s, s ^ 1) for s in range(owners)])


def local(embeddings, cluster_ids):
    rows = embeddings.shape[0]
    owners = lax.axis_size("owner")
    chips = owners // 2
    clusters = CL_DEV * owners
    row_limit = 2 * rows // clusters
    most = round_up(2 * CL_DEV * row_limit, STEP)
    usual = min(most, round_up(17 * rows // (8 * owners), STEP))
    few = chips <= MAX_PERMUTES
    me = lax.axis_index("owner").astype(i32).reshape(1)
    ids0 = cluster_ids.reshape(1, rows)
    ids1 = swap_cores(ids0)
    own, own_total = rank_own(ids0, clusters)
    mine, ids1, own = lax.optimization_barrier((embeddings, ids1, own))
    other = swap_cores(mine)
    counts, rank0, rank1 = count_rows(me, ids1, own, own_total, clusters)
    counts = gather_chips(counts)
    both = (embeddings, other)
    *places, bound, total, load = assign(me, counts, rank0, rank1)
    owner_row, slot_row = places[0], places[2]

    half = chips // 2
    far = list(range(chips - 1, half - 1, -1))
    near = list(range(half - 1, 0, -1))
    sent = far[:2] + near + far[2:] + [0]
    share = max(half // 4, 1)
    groups = [[0] + near, far[: 2 * share], far[2 * share : 3 * share], far[3 * share :]]

    def compare(slots, apart):
        blocks = [None] * chips
        here = list(places)
        for r in sent:
            blocks[r] = pack(me, here, both, r, slots)
            here[0], blocks[r] = lax.optimization_barrier((here[0], blocks[r]))
        if apart:
            arrived = blocks[:1] + [None] * (chips - 1)
            for r in sent[:-1]:
                if r in far[2:]:
                    before = far[far.index(r) - 2]
                    blocks[r], arrived[before] = lax.optimization_barrier(
                        (blocks[r], arrived[before])
                    )
                arrived[r] = swap(blocks[r], r)
        else:
            arrived = swap_together(blocks)
        state = ([], [], [], None)
        for group in groups[:-1]:
            state = score(bound, [arrived[r] for r in group], group, state)
        last = groups[-1]
        answers = finish(
            me, bound, total, [arrived[r] for r in last], last, groups[:-1], state
        )
        return restore(owner_row, slot_row, exchange(answers), slots)

    best, gap = compare(usual, few)
    if usual < most:
        best, gap = lax.cond(
            load[0, 0] <= usual, lambda: (best, gap), lambda: compare(most, False)
        )
    return best.reshape(rows), gap.reshape(rows)


def solution(mesh):
    return jax.shard_map(
        local,
        mesh=mesh,
        in_specs=(P(("groups", "owner"), None), P(("groups", "owner"))),
        out_specs=(P(("groups", "owner")), P(("groups", "owner"))),
        check_vma=False,
    )
```
